32 devices in a mesh: dp: 8 (over z, y), opt: 4 (over x, core).
Axes of the slice: x: 2, y: 2, z: 4, core: 2. Of those that a mesh axis runs over, the one named last changes fastest.
Arguments:
- tokens: bfloat16 [32768, 768], P(('dp', 'opt')), may hold values from -6 to 6
- cotangent: bfloat16 [32768, 768], P(('dp', 'opt')), may hold values from -6 to 6
- w_in: float32 [768, 3352], P(None, 'opt'), may hold values from -0.21875 to 0.21875
- w_out: float32 [1536, 768], P('opt'), may hold values from -0.15625 to 0.15625
- small: float32 [11336], P('opt'), may hold values from -6 to 2.75, as said below
- mom_in: float32 [768, 3352], P(None, 'opt'), may hold values from -512 to 512
- mom_out: float32 [1536, 768], P('opt'), may hold values from -1024 to 1024
- adam_m: float32 [11336], P('opt'), as said below
- adam_v: float32 [11336], P('opt'), as said below
Outputs:
- block: bfloat16 [32768, 768], P(('dp', 'opt'))
- grad_tokens: float32 [32768, 768], P(('dp', 'opt'))
- grad_w_in: float32 [768, 3352], P(None, 'opt')
- grad_w_out: float32 [1536, 768], P('opt')
- grad_small: float32 [11336], P('opt')
- mom_in_new: float32 [768, 3352], P(None, 'opt')
- mom_out_new: float32 [1536, 768], P('opt')
- w_in_new: float32 [768, 3352], P(None, 'opt')
- w_out_new: float32 [1536, 768], P('opt')
- small_new: float32 [11336], P('opt')
- adam_m_new: float32 [11336], P('opt')
- adam_v_new: float32 [11336], P('opt')
The draws below stay inside these ranges and needn't reach their ends.
Inputs may be any that keep to these rules, and one draw needn't show every extreme that they name: Laid out as stated for small; gains lie in 0.6 to 1.4, taps and convolution biases in -0.5 to 0.5, step biases in -6 to -2, decay logarithms in 0 to 2.75, skip factors in 0.5 to 1.5. `adam_m`: both signs. `adam_v`: Positive.
All inputs are finite; a program needn't handle non-finite values.
Results may differ from the reference program's by a relative error of at most 0.017.
Values may be sent and summed in bfloat16 or wider, within the bound.
No kernel may reach another device: no remote copies, remote signals or barrier semaphores. Data moves between devices by JAX's collectives and lax.ppermute only.
A program may use at most 256 MiB of HBM per device.

```python
import math
import jax
import jax.numpy as jnp
from jax import lax

D = 768
HEADS = 24
HEAD_CHANNELS = 64
STATE = 128
CONV = 4
SCAN_BLOCK_SPAN = 256
SEQ_LEN = 1024
SEQS_DEV = 1
STEP = 10
D_INNER = 1536
CONV_CH = 1792
PROJ = 3352
SMALL = 11336
SEQS = 32
TOKENS = 32768


def segment_scale():
    return jnp.concatenate([jnp.full((D,), 1.0, jnp.float32), jnp.full((D_INNER,), 0.7, jnp.float32), jnp.full((CONV * CONV_CH,), 0.3, jnp.float32), jnp.full((CONV_CH,), 0.3, jnp.float32), jnp.full((HEADS,), 1.0, jnp.float32), jnp.full((HEADS,), 1.0, jnp.float32), jnp.full((HEADS,), 3.0, jnp.float32)])


def draw_small(key, part):
    key = jax.random.fold_in(key, 11)
    subkeys = jax.random.split(key, 7)
    pieces = [jax.random.uniform(subkeys[0], (D,), jnp.float32, 0.6, 1.4), jax.random.uniform(subkeys[1], (D_INNER,), jnp.float32, 0.6, 1.4), jax.random.uniform(subkeys[2], (CONV * CONV_CH,), jnp.float32, -0.5, 0.5), jax.random.uniform(subkeys[3], (CONV_CH,), jnp.float32, -0.5, 0.5), jax.random.uniform(subkeys[4], (HEADS,), jnp.float32, -6.0, -2.0), jax.random.uniform(subkeys[5], (HEADS,), jnp.float32, 0.0, 2.75), jax.random.uniform(subkeys[6], (HEADS,), jnp.float32, 0.5, 1.5)]
    return jnp.concatenate(pieces)


def draw_adam_m(key, part):
    key = jax.random.fold_in(key, 12)
    scale_vec = segment_scale() * (0.111 * math.sqrt(TOKENS))
    return scale_vec * jax.random.uniform(key, (SMALL,), jnp.float32, -2.0, 2.0)


def draw_adam_v(key, part):
    key = jax.random.fold_in(key, 13)
    base = segment_scale()
    scale_vec = base * base * (0.0526 * 2.0 * TOKENS)
    factor = jnp.exp(jax.random.uniform(key, (SMALL,), jnp.float32, math.log(0.5), math.log(2.0)))
    return scale_vec * factor


def levels(key, extent, cuts, smallest, high):
    level, own = 1.0, jax.random.fold_in(key, 6)
    for position, shards_of in cuts:
        draws = jnp.exp(jax.random.uniform(jax.random.fold_in(own, position), (shards_of,), jnp.float32, smallest / len(cuts), high / len(cuts)))
        level = level * jnp.repeat(draws, extent[position] // shards_of).reshape([-1 if axis == position else 1 for axis in range(len(extent))])
    return level


def noise(rng, dims, width, bound, cuts=(), kind=jnp.bfloat16):
    factor_of = levels(rng, dims, cuts, -0.22, 0.18) if cuts else 1.0
    drawn = jax.random.normal(rng, dims, jnp.float32) * width * factor_of
    return jnp.minimum(jnp.maximum(drawn, -bound), bound).astype(kind)


def setup_inputs(seed: int = 0) -> dict:
    arg_keys = jax.random.split(jax.random.key(seed), 10)
    return {
        "tokens": noise(arg_keys[0], (TOKENS, D), 1.0, 6.0, ((0, 32),)),
        "cotangent": noise(arg_keys[1], (TOKENS, D), 1.0, 6.0, ((0, 32),)),
        "w_in": noise(arg_keys[2], (D, PROJ), D ** -0.5, 0.21875, ((1, 4),), jnp.float32),
        "w_out": noise(arg_keys[3], (D_INNER, D), D_INNER ** -0.5, 0.15625, ((0, 4),), jnp.float32),
        "small": draw_small(jax.random.fold_in(arg_keys[9], 71), 0),
        "mom_in": noise(arg_keys[5], (D, PROJ), (0.5 * TOKENS ** 0.5), 512.0, ((1, 4),), jnp.float32),
        "mom_out": noise(arg_keys[6], (D_INNER, D), (TOKENS ** 0.5), 1024.0, ((0, 4),), jnp.float32),
        "adam_m": draw_adam_m(jax.random.fold_in(arg_keys[9], 71), 0),
        "adam_v": draw_adam_v(jax.random.fold_in(arg_keys[9], 71), 0),
    }


EPSILON = 1e-05
TOP_PRECISION = lax.Precision.HIGHEST
COEF_A = 3.4445
COEF_B = -4.775
COEF_C = 2.0315
MOMENTUM = 0.95
MUON_RATE = 0.5
DECAY = 0.01
ADAM_RATE = 0.2
BETA_ONE = 0.9
BETA_TWO = 0.95
ADAM_EPS = 1e-08

@jax.custom_vjp
def low(v):
    return lax.optimization_barrier(v.astype(jnp.bfloat16)).astype(jnp.float32)

@jax.custom_vjp
def low_back(v):
    return v

def low_keep(v):
    return (low(v), None)

def low_pass(kept, grad):
    return (grad,)

def back_keep(v):
    return (v, None)

def back_low(kept, grad):
    return (low(grad),)
low.defvjp(low_keep, low_pass)
low_back.defvjp(back_keep, back_low)

def pre_norm(inflow, gain_vec):
    scale_row = lax.rsqrt(lax.optimization_barrier(jnp.mean(inflow * inflow, axis=-1, keepdims=True)) + EPSILON)
    return inflow * scale_row * gain_vec

def ssd_blocks(values, input_b, output_c, step_size, decay_rate):
    length = values.shape[0]
    blocks = length // SCAN_BLOCK_SPAN
    block_vals = values.reshape(blocks, SCAN_BLOCK_SPAN, HEADS, HEAD_CHANNELS)
    block_input_rows = input_b.reshape(blocks, SCAN_BLOCK_SPAN, STATE)
    block_output_rows = output_c.reshape(blocks, SCAN_BLOCK_SPAN, STATE)
    block_dt = step_size.reshape(blocks, SCAN_BLOCK_SPAN, HEADS)
    log_decay = jnp.cumsum(block_dt * decay_rate, axis=1)
    places = jnp.arange(SCAN_BLOCK_SPAN)
    causal = (places[:, None] >= places[None, :])[None, :, :, None]
    differ = log_decay[:, :, None, :] - log_decay[:, None, :, :]
    decay_mat = jnp.where(causal, jnp.exp(jnp.where(causal, differ, 0.0)), 0.0)
    output_input_scores = jnp.einsum('jes,jvs->jev', block_output_rows, block_input_rows, precision=TOP_PRECISION)
    mixing = output_input_scores[:, :, :, None] * decay_mat * block_dt[:, None, :, :]
    inside = jnp.einsum('bqkh,bkhp->bqhp', mixing, block_vals, precision=TOP_PRECISION)
    to_end = jnp.exp(log_decay[:, -1:, :] - log_decay) * block_dt
    weighted = block_vals * to_end[:, :, :, None]
    states = jnp.einsum('bkn,bkhp->bhpn', block_input_rows, weighted, precision=TOP_PRECISION)
    block_decay = jnp.exp(log_decay[:, -1, :])

    def carry_state(entering, pieces):
        state_add, decay_all = pieces
        return (entering * decay_all[:, None, None] + state_add, entering)
    initial = jnp.zeros((HEADS, HEAD_CHANNELS, STATE), jnp.float32)
    unused, entering = lax.scan(carry_state, initial, (states, block_decay))
    crossing = jnp.einsum('bqn,bhpn->bqhp', block_output_rows, entering, precision=TOP_PRECISION) * jnp.exp(log_decay)[:, :, :, None]
    return (inside + crossing).reshape(length, HEADS, HEAD_CHANNELS)

def mixer(projected, rest_vec):
    length = projected.shape[0]
    offset = D_INNER
    gate_gain = rest_vec[:offset]
    conv_taps = rest_vec[offset:offset + CONV * CONV_CH].reshape(CONV, CONV_CH)
    offset = offset + CONV * CONV_CH
    conv_bias = rest_vec[offset:offset + CONV_CH]
    offset = offset + CONV_CH
    dt_bias = rest_vec[offset:offset + HEADS]
    a_log = rest_vec[offset + HEADS:offset + 2 * HEADS]
    skip_gain = rest_vec[offset + 2 * HEADS:offset + 3 * HEADS]
    gate_in = projected[:, :D_INNER]
    conv_in = projected[:, D_INNER:D_INNER + CONV_CH]
    dt_raw = projected[:, D_INNER + CONV_CH:]
    padded = jnp.pad(conv_in, ((CONV - 1, 0), (0, 0)))
    conv_out = conv_bias + conv_taps[0] * padded[0:length]
    for tap_index in range(1, CONV):
        conv_out = conv_out + conv_taps[tap_index] * padded[tap_index:tap_index + length]
    active = jax.nn.silu(conv_out)
    values = active[:, :D_INNER].reshape(length, HEADS, HEAD_CHANNELS)
    input_b = active[:, D_INNER:D_INNER + STATE]
    output_c = active[:, D_INNER + STATE:]
    step_size = jax.nn.softplus(dt_raw + dt_bias)
    decay_rate = -jnp.exp(a_log)
    scanned = ssd_blocks(values, input_b, output_c, step_size, decay_rate) + skip_gain[None, :, None] * values
    gated_out = scanned.reshape(length, D_INNER) * jax.nn.silu(gate_in)
    return pre_norm(gated_out, gate_gain)

def forward(inflow, w_in_c, w_out_c, small_c):
    gain_vec = small_c[:D]
    rest_vec = small_c[D:]
    hidden = low(pre_norm(inflow, gain_vec))
    projected = low_back(low(jnp.einsum('gld,dp->glp', hidden, w_in_c, precision=TOP_PRECISION)))
    mixed = low(lax.map(jax.checkpoint(lambda single: mixer(single, rest_vec)), projected))
    return inflow + jnp.einsum('gli,id->gld', mixed, w_out_c, precision=TOP_PRECISION)

def newton_ref(matrix, wide):
    total = jnp.sqrt(jnp.sum(matrix * matrix))
    iterate = low(matrix / (total + 1e-07))
    for sweep in range(5):
        if wide:
            gram = low(jnp.dot(iterate, iterate.T, precision=TOP_PRECISION))
        else:
            gram = low(jnp.dot(iterate.T, iterate, precision=TOP_PRECISION))
        poly = low(COEF_B * gram + COEF_C * jnp.dot(gram, gram, precision=TOP_PRECISION))
        if wide:
            iterate = low(COEF_A * iterate + jnp.dot(poly, iterate, precision=TOP_PRECISION))
        else:
            iterate = low(COEF_A * iterate + jnp.dot(iterate, poly, precision=TOP_PRECISION))
    return iterate

def reference(tokens, cotangent, w_in, w_out, small, mom_in, mom_out, adam_m, adam_v):
    w_in_c = low(w_in)
    w_out_c = low(w_out)
    small_c = low(small)
    group = 4 * SEQS_DEV
    count = SEQS // group
    inflow = tokens.astype(jnp.float32).reshape(count, group, SEQ_LEN, D)
    cot_all = cotangent.astype(jnp.float32).reshape(count, group, SEQ_LEN, D)

    def per_group(totals, pieces):
        inflow_g, cot_g = pieces
        result, backward = jax.vjp(forward, inflow_g, w_in_c, w_out_c, small_c)
        grad_inflow, grad_in_g, grad_out_g, grad_small_grouped = backward(cot_g)
        totals = (totals[0] + grad_in_g, totals[1] + grad_out_g, totals[2] + grad_small_grouped)
        return (totals, (result.astype(jnp.bfloat16), grad_inflow))
    initial = (jnp.zeros((D, PROJ), jnp.float32), jnp.zeros((D_INNER, D), jnp.float32), jnp.zeros((SMALL,), jnp.float32))
    totals, outputs = lax.scan(per_group, initial, (inflow, cot_all))
    grad_w_in, grad_w_out, grad_small = totals
    block = outputs[0].reshape(TOKENS, D)
    grad_tokens = outputs[1].reshape(TOKENS, D)
    adam_m_new = BETA_ONE * adam_m + (1.0 - BETA_ONE) * grad_small
    adam_v_new = BETA_TWO * adam_v + (1.0 - BETA_TWO) * grad_small * grad_small
    small_new = small * (1.0 - ADAM_RATE * DECAY) - ADAM_RATE * (adam_m_new / (1.0 - BETA_ONE ** STEP)) / (jnp.sqrt(adam_v_new / (1.0 - BETA_TWO ** STEP)) + ADAM_EPS)
    mom_in_new = MOMENTUM * mom_in + grad_w_in
    push_in = grad_w_in + MOMENTUM * mom_in_new
    mom_out_new = MOMENTUM * mom_out + grad_w_out
    push_out = grad_w_out + MOMENTUM * mom_out_new
    ortho_in = newton_ref(push_in, True)
    ortho_out = newton_ref(push_out, False)
    w_in_new = w_in * (1.0 - MUON_RATE * DECAY) - MUON_RATE * math.sqrt(max(1.0, PROJ / D)) * ortho_in
    w_out_new = w_out * (1.0 - MUON_RATE * DECAY) - MUON_RATE * math.sqrt(max(1.0, D / D_INNER)) * ortho_out
    return (block, grad_tokens, grad_w_in, grad_w_out, grad_small, mom_in_new, mom_out_new, w_in_new, w_out_new, small_new, adam_m_new, adam_v_new)
```

```python
import functools
import math

import jax
import jax.numpy as jnp
from jax import lax
from jax.experimental import pallas as pl
from jax.experimental.pallas import tpu as pltpu
from jax.sharding import PartitionSpec as P

D = 768
HEADS = 24
HEAD_CHANNELS = 64
STATE = 128
CONV = 4
SCAN_BLOCK_SPAN = 256
SEQ_LEN = 1024
STEP = 10
D_INNER = 1536
CONV_CH = 1792
PROJ = 3352


EPSILON = 1e-05
COEF_A = 3.4445
COEF_B = -4.775
COEF_C = 2.0315
MOMENTUM = 0.95
MUON_RATE = 0.5
DECAY = 0.01
ADAM_RATE = 0.2
BETA_ONE = 0.9
BETA_TWO = 0.95
ADAM_EPS = 1e-08


def pre_norm(inflow, gain_vec):
    scale_row = lax.rsqrt(jnp.mean(inflow * inflow, axis=-1, keepdims=True) + EPSILON)
    return inflow * scale_row * gain_vec


def ssd_blocks(values, input_b, output_c, step_size, decay_rate):
    length = values.shape[0]
    blocks = length // SCAN_BLOCK_SPAN
    block_vals = values.reshape(blocks, SCAN_BLOCK_SPAN, HEADS, HEAD_CHANNELS)
    block_input_rows = input_b.reshape(blocks, SCAN_BLOCK_SPAN, STATE)
    block_output_rows = output_c.reshape(blocks, SCAN_BLOCK_SPAN, STATE)
    block_dt = step_size.reshape(blocks, SCAN_BLOCK_SPAN, HEADS)
    log_decay = jnp.cumsum(block_dt * decay_rate, axis=1)
    places = jnp.arange(SCAN_BLOCK_SPAN)
    causal = (places[:, None] >= places[None, :])[None, :, :, None]
    differ = log_decay[:, :, None, :] - log_decay[:, None, :, :]
    decay_mat = jnp.where(causal, jnp.exp(jnp.where(causal, differ, 0.0)), 0.0)
    output_input_scores = jnp.einsum(
        "jes,jvs->jev", block_output_rows, block_input_rows, preferred_element_type=jnp.float32
    )
    mixing = output_input_scores[:, :, :, None] * decay_mat * block_dt[:, None, :, :]
    inside = jnp.einsum("bqkh,bkhp->bqhp", mixing, block_vals, preferred_element_type=jnp.float32)
    to_end = jnp.exp(log_decay[:, -1:, :] - log_decay) * block_dt
    weighted = block_vals * to_end[:, :, :, None]
    states = jnp.einsum(
        "bkn,bkhp->bhpn", block_input_rows, weighted, preferred_element_type=jnp.float32
    )
    block_decay = jnp.exp(log_decay[:, -1, :])

    def carry_state(entering, pieces):
        state_add, decay_all = pieces
        return (entering * decay_all[:, None, None] + state_add, entering)

    initial = jnp.zeros((HEADS, HEAD_CHANNELS, STATE), jnp.float32)
    unused, entering = lax.scan(carry_state, initial, (states, block_decay))
    crossing = (
        jnp.einsum(
            "bqn,bhpn->bqhp", block_output_rows, entering, preferred_element_type=jnp.float32
        )
        * jnp.exp(log_decay)[:, :, :, None]
    )
    return (inside + crossing).reshape(length, HEADS, HEAD_CHANNELS)


def mixer(projected, rest_vec):
    length = projected.shape[0]
    offset = D_INNER
    gate_gain = rest_vec[:offset]
    conv_taps = rest_vec[offset : offset + CONV * CONV_CH].reshape(CONV, CONV_CH)
    offset = offset + CONV * CONV_CH
    conv_bias = rest_vec[offset : offset + CONV_CH]
    offset = offset + CONV_CH
    dt_bias = rest_vec[offset : offset + HEADS]
    a_log = rest_vec[offset + HEADS : offset + 2 * HEADS]
    skip_gain = rest_vec[offset + 2 * HEADS : offset + 3 * HEADS]
    gate_in = projected[:, :D_INNER]
    conv_in = projected[:, D_INNER : D_INNER + CONV_CH]
    dt_raw = projected[:, D_INNER + CONV_CH :]
    padded = jnp.pad(conv_in, ((CONV - 1, 0), (0, 0)))
    conv_out = conv_bias + conv_taps[0] * padded[0:length]
    for tap_index in range(1, CONV):
        conv_out = conv_out + conv_taps[tap_index] * padded[tap_index : tap_index + length]
    active = jax.nn.silu(conv_out)
    values = active[:, :D_INNER].reshape(length, HEADS, HEAD_CHANNELS)
    input_b = active[:, D_INNER : D_INNER + STATE]
    output_c = active[:, D_INNER + STATE :]
    step_size = jax.nn.softplus(dt_raw + dt_bias)
    decay_rate = -jnp.exp(a_log)
    scanned = (
        ssd_blocks(values, input_b, output_c, step_size, decay_rate)
        + skip_gain[None, :, None] * values
    )
    gated_out = scanned.reshape(length, D_INNER) * jax.nn.silu(gate_in)
    return pre_norm(gated_out, gate_gain)


def mix_all(projected, rest_vec):
    return lax.map(jax.checkpoint(lambda single: mixer(single, rest_vec)), projected)


def diagonal(size):
    rows = lax.broadcasted_iota(jnp.int32, (size, size), 0)
    cols = lax.broadcasted_iota(jnp.int32, (size, size), 1)
    return rows == cols


def dot32(left, right):
    return jnp.dot(left, right, preferred_element_type=jnp.float32)


ROW_BLOCK = 256


def newton_kernel(wide, rate, gram_ref, push_ref, weight_ref, new_ref, a_ref, p_ref, t_ref, r_ref, e_ref, k_ref, f_ref):
    blocks = [slice(i, i + ROW_BLOCK) for i in range(0, D, ROW_BLOCK)]
    size = 1.0 / D

    def eye_of(block):
        rows = lax.broadcasted_iota(jnp.int32, (ROW_BLOCK, D), 0) + block.start
        cols = lax.broadcasted_iota(jnp.int32, (ROW_BLOCK, D), 1)
        return rows == cols

    def trace_part(value, block):
        kept = jnp.where(eye_of(block), value, 0.0)
        return jnp.sum(jnp.sum(kept, axis=0, keepdims=True), axis=1, keepdims=True)

    def shifted(value, block, amount):
        return value - jnp.where(eye_of(block), amount, 0.0)

    total = sum(trace_part(gram_ref[block, :], block) for block in blocks)
    norm = 1.0 / (jnp.sqrt(total) + 1e-07)
    scale = norm * norm
    for block in blocks:
        a_ref[block, :] = gram_ref[block, :] * scale
    mean = total * scale * size
    for sweep in range(5):
        for block in blocks:
            e_ref[block, :] = shifted(a_ref[block, :], block, mean).astype(jnp.bfloat16)
        trace = 0.0
        for block in blocks:
            rest = shifted(a_ref[block, :], block, mean)
            square = 2.0 * mean * rest + dot32(e_ref[block, :], e_ref[...])
            poly = COEF_B * a_ref[block, :] + COEF_C * shifted(square, block, -mean * mean)
            trace += trace_part(poly, block)
            p_ref[block, :] = poly
        shift = trace * size
        lead = COEF_A + shift
        for block in blocks:
            k_ref[block, :] = shifted(p_ref[block, :], block, shift).astype(jnp.bfloat16)
        if sweep == 0:
            for block in blocks:
                r_ref[block, :] = shifted(p_ref[block, :], block, -COEF_A)
            r_mean = lead
        else:
            for block in blocks:
                f_ref[block, :] = shifted(r_ref[block, :], block, r_mean).astype(jnp.bfloat16)
            trace = 0.0
            for block in blocks:
                value = (
                    lead * r_ref[block, :]
                    + r_mean * k_ref[block, :].astype(jnp.float32)
                    + dot32(k_ref[block, :], f_ref[...])
                )
                trace += trace_part(value, block)
                r_ref[block, :] = value
            r_mean = trace * size
        if sweep < 4:
            trace = 0.0
            for block in blocks:
                value = (
                    lead * a_ref[block, :]
                    + mean * k_ref[block, :].astype(jnp.float32)
                    + dot32(k_ref[block, :], e_ref[...])
                )
                trace += trace_part(value, block)
                t_ref[block, :] = value
            t_mean = trace * size
            for block in blocks:
                f_ref[block, :] = shifted(t_ref[block, :], block, t_mean).astype(jnp.bfloat16)
            trace = 0.0
            for block in blocks:
                value = (
                    lead * t_ref[block, :]
                    + t_mean * k_ref[block, :].astype(jnp.float32)
                    + dot32(f_ref[block, :], k_ref[...])
                )
                trace += trace_part(value, block)
                a_ref[block, :] = value
            mean = trace * size
    for block in blocks:
        f_ref[block, :] = shifted(r_ref[block, :], block, r_mean).astype(jnp.bfloat16)
    step = norm * (MUON_RATE * rate)
    if wide:
        moved = push_ref[...].astype(jnp.bfloat16)
        for block in blocks:
            ortho = r_mean * push_ref[block, :] + dot32(f_ref[block, :], moved)
            new_ref[block, :] = weight_ref[block, :] * (1.0 - MUON_RATE * DECAY) - step * ortho
    else:
        ortho = r_mean * push_ref[...] + dot32(push_ref[...].astype(jnp.bfloat16), f_ref[...])
        new_ref[...] = weight_ref[...] * (1.0 - MUON_RATE * DECAY) - step * ortho


def newton_update(gram, push, weight, wide):
    rate = math.sqrt(max(1.0, PROJ / D)) if wide else math.sqrt(max(1.0, D / D_INNER))
    whole = pltpu.VMEM((D, D), jnp.float32)
    half = pltpu.VMEM((D, D), jnp.bfloat16)
    return pl.pallas_call(
        functools.partial(newton_kernel, wide, rate),
        out_shape=jax.ShapeDtypeStruct(weight.shape, jnp.float32),
        scratch_shapes=[whole, whole, whole, whole, half, half, half],
        compiler_params=pltpu.CompilerParams(vmem_limit_bytes=56 * 1024 * 1024),
        cost_estimate=pl.CostEstimate(
            flops=17 * 2 * D**3 + 2 * D * push.size, bytes_accessed=12 * push.size, transcendentals=0
        ),
        name="newton_in" if wide else "newton_out",
    )(gram, push, weight)


def reduce_owned(parts):
    shard = lax.psum_scatter(parts, "opt", scatter_dimension=0, tiled=False)
    piece = lax.psum_scatter(shard, "dp", scatter_dimension=0, tiled=True)
    return lax.all_gather(piece, "dp", axis=0, tiled=True).astype(jnp.float32)


def on_device(tokens, cotangent, w_in, w_out, small, mom_in, mom_out, adam_m, adam_v):
    w_in_b, w_out_b, small_b = (
        lax.all_gather(w_in.astype(jnp.bfloat16), "opt", axis=1, tiled=True),
        lax.all_gather(w_out.astype(jnp.bfloat16), "opt", axis=0, tiled=True),
        lax.all_gather(small.astype(jnp.bfloat16), "opt", axis=0, tiled=True),
    )
    params = small_b.astype(jnp.float32)
    gain_vec = params[:D]
    rest_vec = params[D:]
    inflow = tokens.astype(jnp.float32)
    normed, norm_back = jax.vjp(pre_norm, inflow, gain_vec)
    hidden = normed.astype(jnp.bfloat16)
    projected = jnp.dot(hidden, w_in_b, preferred_element_type=jnp.float32).astype(jnp.bfloat16)
    seq_count = tokens.shape[0] // SEQ_LEN
    proj_seqs = projected.astype(jnp.float32).reshape(seq_count, SEQ_LEN, projected.shape[1])
    mixed_float, mix_back = jax.vjp(mix_all, proj_seqs, rest_vec)
    mixed = mixed_float.reshape(tokens.shape[0], mixed_float.shape[2]).astype(jnp.bfloat16)
    outflow = jnp.dot(mixed, w_out_b, preferred_element_type=jnp.float32)
    block = (inflow + outflow).astype(jnp.bfloat16)
    grad_w_out = jnp.einsum("ti,td->id", mixed, cotangent, preferred_element_type=jnp.float32)
    grad_mixed = jnp.einsum("td,id->ti", cotangent, w_out_b, preferred_element_type=jnp.float32)
    grad_proj_f, grad_rest = mix_back(grad_mixed.reshape(mixed_float.shape))
    grad_proj = grad_proj_f.reshape(projected.shape).astype(jnp.bfloat16)
    grad_w_in = jnp.einsum(
        "td,tsp->sdp",
        hidden,
        grad_proj.reshape(grad_proj.shape[0], lax.axis_size("opt"), -1),
        preferred_element_type=jnp.float32,
    )
    grad_hidden = jnp.einsum("tp,dp->td", grad_proj, w_in_b, preferred_element_type=jnp.float32)
    grad_inflow, grad_gain = norm_back(grad_hidden)
    grad_tokens = cotangent.astype(jnp.float32) + grad_inflow
    grad_small = jnp.concatenate([grad_gain, grad_rest])
    owned_in = reduce_owned(grad_w_in.astype(jnp.bfloat16))
    owned_out = reduce_owned(grad_w_out.reshape(lax.axis_size("opt"), -1, D).astype(jnp.bfloat16))
    owned_small = lax.psum(
        lax.psum_scatter(grad_small.astype(jnp.bfloat16), "opt", scatter_dimension=0, tiled=True), "dp"
    ).astype(jnp.float32)
    adam_m_new = BETA_ONE * adam_m + (1.0 - BETA_ONE) * owned_small
    adam_v_new = BETA_TWO * adam_v + (1.0 - BETA_TWO) * owned_small * owned_small
    small_new = small * (1.0 - ADAM_RATE * DECAY) - ADAM_RATE * (
        adam_m_new / (1.0 - BETA_ONE**STEP)
    ) / (jnp.sqrt(adam_v_new / (1.0 - BETA_TWO**STEP)) + ADAM_EPS)
    mom_in_new = MOMENTUM * mom_in + owned_in
    push_in = owned_in + MOMENTUM * mom_in_new
    mom_out_new = MOMENTUM * mom_out + owned_out
    push_out = owned_out + MOMENTUM * mom_out_new
    pushed_in = push_in.astype(jnp.bfloat16)
    pushed_out = push_out.astype(jnp.bfloat16)
    gram_in = lax.psum(
        jnp.einsum("ik,jk->ij", pushed_in, pushed_in, preferred_element_type=jnp.float32), "opt"
    )
    gram_out = lax.psum(
        jnp.einsum("ki,kj->ij", pushed_out, pushed_out, preferred_element_type=jnp.float32), "opt"
    )
    w_in_new = newton_update(gram_in, push_in, w_in, True)
    w_out_new = newton_update(gram_out, push_out, w_out, False)
    return (
        block,
        grad_tokens,
        owned_in,
        owned_out,
        owned_small,
        mom_in_new,
        mom_out_new,
        w_in_new,
        w_out_new,
        small_new,
        adam_m_new,
        adam_v_new,
    )


def solution(mesh):
    in_specs = (
        P(("dp", "opt"), None),
        P(("dp", "opt"), None),
        P(None, "opt"),
        P("opt", None),
        P("opt"),
        P(None, "opt"),
        P("opt", None),
        P("opt"),
        P("opt"),
    )
    out_specs = (
        P(("dp", "opt"), None),
        P(("dp", "opt"), None),
        P(None, "opt"),
        P("opt", None),
        P("opt"),
        P(None, "opt"),
        P("opt", None),
        P(None, "opt"),
        P("opt", None),
        P("opt"),
        P("opt"),
        P("opt"),
    )
    return jax.shard_map(
        on_device, mesh=mesh, in_specs=in_specs, out_specs=out_specs, check_vma=False
    )
```

```python
import functools
import math

import jax
import jax.numpy as jnp
from jax import lax
from jax.experimental import pallas as pl
from jax.experimental.pallas import tpu as pltpu
from jax.sharding import PartitionSpec as P

D = 768
HEADS = 24
HEAD_CHANNELS = 64
STATE = 128
CONV = 4
SEQ_LEN = 1024
STEP = 10
D_INNER = 1536
CONV_CH = 1792
PROJ = 3352


EPSILON = 1e-05
COEF_A = 3.4445
COEF_B = -4.775
COEF_C = 2.0315
MOMENTUM = 0.95
MUON_RATE = 0.5
DECAY = 0.01
ADAM_RATE = 0.2
BETA_ONE = 0.9
BETA_TWO = 0.95
ADAM_EPS = 1e-08


SPAN = 128
CHUNKS = SEQ_LEN // SPAN
PAIRS = HEADS // 2
WIDTH = 2 * HEAD_CHANNELS
CONV_END = D_INNER + CONV_CH
PADDED = CONV_END + 128
TAIL = 8
VMEM_LIMIT = 56 * 1024 * 1024


def dot32(left, right):
    return jnp.dot(left, right, preferred_element_type=jnp.float32)


def dot_nt(left, right):
    return lax.dot_general(left, right, (((1,), (1,)), ((), ())), preferred_element_type=jnp.float32)


def dot_tn(left, right):
    return lax.dot_general(left, right, (((0,), (0,)), ((), ())), preferred_element_type=jnp.float32)


def halves(value):
    high = value.astype(jnp.bfloat16)
    return high, (value - high.astype(jnp.float32)).astype(jnp.bfloat16)


def sigmoid(value):
    return 0.5 * jnp.tanh(0.5 * value) + 0.5


def softplus(value):
    return jnp.maximum(value, 0.0) + jnp.log1p(jnp.exp(-jnp.abs(value)))


def fold_rows(value):
    return jnp.sum(value.reshape(value.shape[0] // 8, 8, value.shape[1]), axis=0)


def triangle(lower):
    rows = lax.broadcasted_iota(jnp.int32, (SPAN, SPAN), 0)
    cols = lax.broadcasted_iota(jnp.int32, (SPAN, SPAN), 1)
    return rows >= cols if lower else rows <= cols


def running_sum(mask, value):
    ones = jnp.where(mask, 1.0, 0.0).astype(jnp.bfloat16)
    high, rest = halves(value)
    low = (value - high.astype(jnp.float32) - rest.astype(jnp.float32)).astype(jnp.bfloat16)
    return dot32(ones, high) + (dot32(ones, rest) + dot32(ones, low))


def head_sums(value, reduce_mat):
    high, low = halves(value)
    return dot32(high, reduce_mat) + dot32(low, reduce_mat)


def step_factors(raw, dt_bias, rate, spread):
    step_size = softplus(raw + dt_bias)
    log_decay = running_sum(triangle(True), step_size * rate)
    last = log_decay[SPAN - 1 : SPAN, :]
    stacked = jnp.concatenate([step_size, jnp.exp(log_decay), jnp.exp(last - log_decay)], axis=0)
    high, low = halves(stacked)
    wide = dot32(jnp.concatenate([high, low], axis=1), spread)
    return step_size, log_decay, wide[:SPAN], wide[SPAN : 2 * SPAN], wide[2 * SPAN :]


def split_pair(value, first):
    return jnp.concatenate(
        [jnp.where(first, value, 0.0), jnp.where(first, 0.0, value)], axis=0
    ).astype(jnp.bfloat16)


def forward_kernel(
    proj_ref, back_ref, taps_ref, conv_bias_ref, gate_gain_ref, skip_ref, dt_bias_ref, rate_ref, spread_ref, reduce_ref,
    mixed_ref, active_ref, slope_ref, grad_scan_ref, grad_gate_ref, states_ref, inner_ref, gain_acc_ref, skip_acc_ref,
    window_ref, state_ref,
):
    f32, bf16 = jnp.float32, jnp.bfloat16

    @pl.when(pl.program_id(0) == 0)
    def start():
        window_ref[0:TAIL, :] = jnp.zeros((TAIL, CONV_CH), f32)
        state_ref[...] = jnp.zeros((STATE, D_INNER), f32)
        gain_acc_ref[...] = jnp.zeros((8, D_INNER), f32)
        skip_acc_ref[...] = jnp.zeros((8, D_INNER), f32)

    window_ref[TAIL:, :] = proj_ref[:, D_INNER:CONV_END].astype(f32)
    conv_out = conv_bias_ref[...]
    for tap in range(CONV):
        start_row = TAIL - (CONV - 1) + tap
        conv_out = conv_out + taps_ref[tap : tap + 1, :] * window_ref[start_row : start_row + SPAN, :]
    window_ref[0:TAIL, :] = window_ref[SPAN:, :]
    part = sigmoid(conv_out)
    silu = conv_out * part
    active_ref[...] = silu.astype(bf16)
    slope_ref[...] = (part + silu * (1.0 - part)).astype(bf16)

    values = active_ref[:, :D_INNER].astype(f32)
    input_b = active_ref[:, D_INNER : D_INNER + STATE]
    output_c = active_ref[:, D_INNER + STATE :]
    step_size, log_decay, step_wide, decay_wide, end_wide = step_factors(
        proj_ref[:, CONV_END:].astype(f32), dt_bias_ref[...], rate_ref[...], spread_ref[...]
    )
    decay_rows = log_decay.T
    moved = step_wide * values
    state = state_ref[...]
    state_low = state.astype(bf16)
    states_ref[0] = state_low
    state_ref[...] = state * decay_wide[SPAN - 1 : SPAN, :] + dot_tn(input_b, (moved * end_wide).astype(bf16))
    scores = dot_nt(output_c, input_b)
    causal = triangle(True)
    first = lax.broadcasted_iota(jnp.int32, (SPAN, WIDTH), 1) < HEAD_CHANNELS
    pieces = []
    for pair in range(PAIRS):
        lanes = slice(pair * WIDTH, (pair + 1) * WIDTH)
        mixing = []
        for head in (2 * pair, 2 * pair + 1):
            differ = log_decay[:, head : head + 1] - decay_rows[head : head + 1, :]
            mixing.append((scores * jnp.exp(jnp.where(causal, differ, -1e30))).astype(bf16))
        pieces.append(dot32(jnp.concatenate(mixing, axis=1), split_pair(moved[:, lanes], first)))
    inner = jnp.concatenate(pieces, axis=1) + dot32(output_c, state_low) * decay_wide
    scanned = inner + skip_ref[...] * values

    gate_in = proj_ref[:, :D_INNER].astype(f32)
    part = sigmoid(gate_in)
    gate = gate_in * part
    gated = scanned * gate
    scale = lax.rsqrt(jnp.mean(gated * gated, axis=1, keepdims=True) + EPSILON)
    normal = gated * scale
    mixed_ref[...] = (normal * gate_gain_ref[...]).astype(bf16)
    back = back_ref[...].astype(f32)
    gain_acc_ref[...] += fold_rows(back * normal)
    back = back * gate_gain_ref[...]
    grad_gated = scale * (back - normal * jnp.mean(back * normal, axis=1, keepdims=True))
    grad_gate_ref[...] = (grad_gated * scanned * (part + gate * (1.0 - part))).astype(bf16)
    grad_scan_low = (grad_gated * gate).astype(bf16)
    grad_scan_ref[...] = grad_scan_low
    grad_scan = grad_scan_low.astype(f32)
    skip_acc_ref[...] += fold_rows(grad_scan * values)
    inner_ref[...] = head_sums(grad_scan * inner, reduce_ref[...])


def backward_kernel(
    proj_ref, active_ref, slope_ref, grad_scan_ref, states_ref, inner_ref, taps_ref, skip_ref, dt_bias_ref, rate_ref,
    spread_ref, reduce_ref,
    grad_ref, taps_acc_ref, bias_acc_ref, dt_acc_ref, rate_acc_ref,
    window_ref, costate_ref,
):
    f32, bf16 = jnp.float32, jnp.bfloat16

    @pl.when(pl.program_id(0) == 0)
    def start():
        window_ref[SPAN:, :] = jnp.zeros((TAIL, CONV_CH), f32)
        costate_ref[...] = jnp.zeros((STATE, D_INNER), f32)
        taps_acc_ref[...] = jnp.zeros((CONV, 8, CONV_CH), f32)
        bias_acc_ref[...] = jnp.zeros((8, CONV_CH), f32)
        dt_acc_ref[...] = jnp.zeros((8, 128), f32)
        rate_acc_ref[...] = jnp.zeros((8, 128), f32)

    values = active_ref[:, :D_INNER].astype(f32)
    input_b = active_ref[:, D_INNER : D_INNER + STATE]
    output_c = active_ref[:, D_INNER + STATE :]
    raw = proj_ref[:, CONV_END:].astype(f32)
    rate = rate_ref[...]
    step_size, log_decay, step_wide, decay_wide, end_wide = step_factors(raw, dt_bias_ref[...], rate, spread_ref[...])
    decay_rows = log_decay.T
    moved = step_wide * values
    grad_scan_low = grad_scan_ref[...]
    grad_scan = grad_scan_low.astype(f32)
    scores = dot_nt(input_b, output_c)
    causal = triangle(False)
    first = lax.broadcasted_iota(jnp.int32, (SPAN, WIDTH), 1) < HEAD_CHANNELS
    grad_scores = jnp.zeros((SPAN, SPAN), f32)
    pieces = []
    for pair in range(PAIRS):
        lanes = slice(pair * WIDTH, (pair + 1) * WIDTH)
        moved_low = moved[:, lanes].astype(bf16)
        grad_pair = split_pair(grad_scan[:, lanes], first)
        grad_mixing = dot_nt(moved_low, grad_pair)
        mixing = []
        for place, head in enumerate((2 * pair, 2 * pair + 1)):
            differ = decay_rows[head : head + 1, :] - log_decay[:, head : head + 1]
            decay = jnp.exp(jnp.where(causal, differ, -1e30))
            mixing.append((scores * decay).astype(bf16))
            grad_scores = grad_scores + decay * grad_mixing[:, place * SPAN : (place + 1) * SPAN]
        pieces.append(dot32(jnp.concatenate(mixing, axis=1), grad_pair))
    grad_inner = jnp.concatenate(pieces, axis=1)

    costate = costate_ref[...]
    costate_low = costate.astype(bf16)
    states_low = states_ref[0]
    last_wide = decay_wide[SPAN - 1 : SPAN, :]
    kept = fold_rows(costate * states_low.astype(f32)) * last_wide
    grad_cross = dot32(input_b, costate_low) * end_wide
    grad_decayed = (grad_scan * decay_wide).astype(bf16)
    grad_scores_low = grad_scores.astype(bf16)
    grad_b = dot32(grad_scores_low, output_c) + dot_nt((moved * end_wide).astype(bf16), costate_low)
    grad_c = dot_tn(grad_scores_low, input_b) + dot_nt(grad_decayed, states_low)
    costate_ref[...] = costate * last_wide + dot_tn(output_c, grad_decayed)

    moved_round = moved.astype(bf16).astype(f32)
    grad_moved = grad_inner + grad_cross
    reduce_mat = reduce_ref[...]
    own = head_sums(moved_round * grad_inner, reduce_mat)
    crossing = dot32((moved * grad_cross).astype(bf16), reduce_mat)
    grad_step = dot32((values * grad_moved).astype(bf16), reduce_mat)
    keeping = jnp.sum(head_sums(kept, reduce_mat), axis=0, keepdims=True)
    grad_log = (
        running_sum(triangle(False), inner_ref[...] - own)
        + running_sum(triangle(True), crossing) - crossing
        + keeping
    )
    grad_raw = (grad_step + rate * grad_log) * sigmoid(raw + dt_bias_ref[...])
    rate_acc_ref[...] += fold_rows(step_size * grad_log)
    dt_acc_ref[...] += fold_rows(grad_raw)
    grad_ref[:, CONV_CH:] = grad_raw.astype(bf16)

    grad_values = step_wide * grad_moved + skip_ref[...] * grad_scan
    grad_active = jnp.concatenate([grad_values, grad_b, grad_c], axis=1)
    grad_conv = grad_active * slope_ref[...].astype(f32)
    bias_acc_ref[...] += fold_rows(grad_conv)
    window_ref[0:SPAN, :] = grad_conv
    conv_in = proj_ref[:, D_INNER:CONV_END].astype(f32)
    grad_in = jnp.zeros((SPAN, CONV_CH), f32)
    for tap in range(CONV):
        start_row = CONV - 1 - tap
        shifted = window_ref[start_row : start_row + SPAN, :]
        grad_in = grad_in + taps_ref[tap : tap + 1, :] * shifted
        taps_acc_ref[tap] += fold_rows(conv_in * shifted)
    grad_ref[:, :CONV_CH] = grad_in.astype(bf16)
    window_ref[SPAN:, :] = window_ref[0:TAIL, :]


def head_matrices():
    spread = jnp.pad(jnp.repeat(jnp.eye(HEADS, dtype=jnp.bfloat16), HEAD_CHANNELS, axis=1), ((0, 128 - HEADS), (0, 0)))
    return jnp.concatenate([spread, spread], axis=0), spread.T


def row_block(width, order):
    return pl.BlockSpec((SPAN, width), lambda i: (order(i), 0))


def fixed_block(*shape):
    return pl.BlockSpec(shape, lambda i: (0,) * len(shape))


def state_block(order):
    return pl.BlockSpec((1, STATE, D_INNER), lambda i: (order(i), 0, 0))


def pad_heads(vector):
    return jnp.pad(vector, (0, 128 - HEADS))[None, :]


def mixer_forward(projected, back, taps, conv_bias, gate_gain, skip_wide, dt_bias, rate, spread, reduce_mat):
    f32, bf16 = jnp.float32, jnp.bfloat16
    order = lambda i: i
    rows = lambda width, kind: jax.ShapeDtypeStruct((SEQ_LEN, width), kind)
    return pl.pallas_call(
        forward_kernel,
        grid=(CHUNKS,),
        in_specs=[
            row_block(PADDED, order), row_block(D_INNER, order), fixed_block(CONV, CONV_CH), fixed_block(1, CONV_CH),
            fixed_block(1, D_INNER), fixed_block(1, D_INNER), fixed_block(1, 128), fixed_block(1, 128),
            fixed_block(256, D_INNER), fixed_block(D_INNER, 128),
        ],
        out_specs=[
            row_block(D_INNER, order), row_block(CONV_CH, order), row_block(CONV_CH, order), row_block(D_INNER, order),
            row_block(D_INNER, order), state_block(order), row_block(128, order), fixed_block(8, D_INNER),
            fixed_block(8, D_INNER),
        ],
        out_shape=[
            rows(D_INNER, bf16), rows(CONV_CH, bf16), rows(CONV_CH, bf16), rows(D_INNER, bf16), rows(D_INNER, bf16),
            jax.ShapeDtypeStruct((CHUNKS, STATE, D_INNER), bf16), rows(128, f32),
            jax.ShapeDtypeStruct((8, D_INNER), f32), jax.ShapeDtypeStruct((8, D_INNER), f32),
        ],
        scratch_shapes=[pltpu.VMEM((SPAN + TAIL, CONV_CH), f32), pltpu.VMEM((STATE, D_INNER), f32)],
        compiler_params=pltpu.CompilerParams(
            dimension_semantics=("arbitrary",), vmem_limit_bytes=VMEM_LIMIT
        ),
        cost_estimate=pl.CostEstimate(flops=8 * 10**9, bytes_accessed=32 * 10**6, transcendentals=10**7),
        name="mixer_forward",
    )(projected, back, taps, conv_bias, gate_gain, skip_wide, dt_bias, rate, spread, reduce_mat)


def mixer_backward(projected, active, slope, grad_scan, states, inner, taps, skip_wide, dt_bias, rate, spread, reduce_mat):
    f32, bf16 = jnp.float32, jnp.bfloat16
    order = lambda i: CHUNKS - 1 - i
    return pl.pallas_call(
        backward_kernel,
        grid=(CHUNKS,),
        in_specs=[
            row_block(PADDED, order), row_block(CONV_CH, order), row_block(CONV_CH, order), row_block(D_INNER, order),
            state_block(order), row_block(128, order), fixed_block(CONV, CONV_CH), fixed_block(1, D_INNER),
            fixed_block(1, 128), fixed_block(1, 128), fixed_block(256, D_INNER), fixed_block(D_INNER, 128),
        ],
        out_specs=[
            row_block(CONV_CH + 128, order), fixed_block(CONV, 8, CONV_CH), fixed_block(8, CONV_CH),
            fixed_block(8, 128), fixed_block(8, 128),
        ],
        out_shape=[
            jax.ShapeDtypeStruct((SEQ_LEN, CONV_CH + 128), bf16), jax.ShapeDtypeStruct((CONV, 8, CONV_CH), f32),
            jax.ShapeDtypeStruct((8, CONV_CH), f32), jax.ShapeDtypeStruct((8, 128), f32),
            jax.ShapeDtypeStruct((8, 128), f32),
        ],
        scratch_shapes=[pltpu.VMEM((SPAN + TAIL, CONV_CH), f32), pltpu.VMEM((STATE, D_INNER), f32)],
        compiler_params=pltpu.CompilerParams(
            dimension_semantics=("arbitrary",), vmem_limit_bytes=VMEM_LIMIT
        ),
        cost_estimate=pl.CostEstimate(flops=12 * 10**9, bytes_accessed=32 * 10**6, transcendentals=10**7),
        name="mixer_backward",
    )(projected, active, slope, grad_scan, states, inner, taps, skip_wide, dt_bias, rate, spread, reduce_mat)


ROW_BLOCK = 256
UPPER = [(0, 0), (0, 1), (0, 2), (1, 1), (1, 2), (2, 2)]


def gram_kernel(wide, push_ref, gram_ref):
    for place, (row, col) in enumerate(UPPER):
        rows = slice(row * ROW_BLOCK, (row + 1) * ROW_BLOCK)
        cols = slice(col * ROW_BLOCK, (col + 1) * ROW_BLOCK)
        if wide:
            gram_ref[place] = dot_nt(push_ref[rows, :], push_ref[cols, :])
        else:
            gram_ref[place] = dot_tn(push_ref[:, rows], push_ref[:, cols])


def gram_sum(push, wide):
    tiles = pl.pallas_call(
        functools.partial(gram_kernel, wide),
        out_shape=jax.ShapeDtypeStruct((len(UPPER), ROW_BLOCK, ROW_BLOCK), jnp.float32),
        compiler_params=pltpu.CompilerParams(vmem_limit_bytes=VMEM_LIMIT),
        cost_estimate=pl.CostEstimate(
            flops=2 * D * push.size, bytes_accessed=2 * push.size, transcendentals=0
        ),
        name="gram_in" if wide else "gram_out",
    )(push)
    part = fold(tiles, "opt", 0, 0)
    part = part + exchange(part, "opt", 1)
    return unfold(part, "opt", 0, 0)


def newton_kernel(wide, rate, gram_ref, push_ref, weight_ref, new_ref, a_ref, p_ref, t_ref, r_ref, e_ref, k_ref, f_ref):
    blocks = [slice(i, i + ROW_BLOCK) for i in range(0, D, ROW_BLOCK)]
    size = 1.0 / D

    def eye_of(block):
        rows = lax.broadcasted_iota(jnp.int32, (ROW_BLOCK, D), 0) + block.start
        cols = lax.broadcasted_iota(jnp.int32, (ROW_BLOCK, D), 1)
        return rows == cols

    def trace_part(value, block):
        kept = jnp.where(eye_of(block), value, 0.0)
        return jnp.sum(jnp.sum(kept, axis=0, keepdims=True), axis=1, keepdims=True)

    def shifted(value, block, amount):
        return value - jnp.where(eye_of(block), amount, 0.0)

    total = 0.0
    for place, (row, col) in enumerate(UPPER):
        tile = gram_ref[place]
        a_ref[blocks[row], blocks[col]] = tile
        if row == col:
            kept = jnp.where(eye_of(blocks[0])[:, :ROW_BLOCK], tile, 0.0)
            total += jnp.sum(jnp.sum(kept, axis=0, keepdims=True), axis=1, keepdims=True)
        else:
            a_ref[blocks[col], blocks[row]] = tile.T
    norm = 1.0 / (jnp.sqrt(total) + 1e-07)
    scale = norm * norm
    for block in blocks:
        a_ref[block, :] = a_ref[block, :] * scale
    mean = total * scale * size
    for sweep in range(5):
        for block in blocks:
            e_ref[block, :] = shifted(a_ref[block, :], block, mean).astype(jnp.bfloat16)
        trace = 0.0
        for block in blocks:
            rest = shifted(a_ref[block, :], block, mean)
            square = 2.0 * mean * rest + dot32(e_ref[block, :], e_ref[...])
            poly = COEF_B * a_ref[block, :] + COEF_C * shifted(square, block, -mean * mean)
            trace += trace_part(poly, block)
            p_ref[block, :] = poly
        shift = trace * size
        lead = COEF_A + shift
        for block in blocks:
            k_ref[block, :] = shifted(p_ref[block, :], block, shift).astype(jnp.bfloat16)
        if sweep == 0:
            for block in blocks:
                r_ref[block, :] = shifted(p_ref[block, :], block, -COEF_A)
            r_mean = lead
        else:
            for block in blocks:
                f_ref[block, :] = shifted(r_ref[block, :], block, r_mean).astype(jnp.bfloat16)
            trace = 0.0
            for block in blocks:
                value = (
                    lead * r_ref[block, :]
                    + r_mean * k_ref[block, :].astype(jnp.float32)
                    + dot32(k_ref[block, :], f_ref[...])
                )
                trace += trace_part(value, block)
                r_ref[block, :] = value
            r_mean = trace * size
        if sweep < 4:
            trace = 0.0
            for block in blocks:
                value = (
                    lead * a_ref[block, :]
                    + mean * k_ref[block, :].astype(jnp.float32)
                    + dot32(k_ref[block, :], e_ref[...])
                )
                trace += trace_part(value, block)
                t_ref[block, :] = value
            t_mean = trace * size
            for block in blocks:
                f_ref[block, :] = shifted(t_ref[block, :], block, t_mean).astype(jnp.bfloat16)
            trace = 0.0
            for block in blocks:
                value = (
                    lead * t_ref[block, :]
                    + t_mean * k_ref[block, :].astype(jnp.float32)
                    + dot32(f_ref[block, :], k_ref[...])
                )
                trace += trace_part(value, block)
                a_ref[block, :] = value
            mean = trace * size
    for block in blocks:
        f_ref[block, :] = shifted(r_ref[block, :], block, r_mean).astype(jnp.bfloat16)
    step = norm * (MUON_RATE * rate)
    if wide:
        moved = push_ref[...].astype(jnp.bfloat16)
        for block in blocks:
            ortho = r_mean * push_ref[block, :] + dot32(f_ref[block, :], moved)
            new_ref[block, :] = weight_ref[block, :] * (1.0 - MUON_RATE * DECAY) - step * ortho
    else:
        ortho = r_mean * push_ref[...] + dot32(push_ref[...].astype(jnp.bfloat16), f_ref[...])
        new_ref[...] = weight_ref[...] * (1.0 - MUON_RATE * DECAY) - step * ortho


def newton_update(gram, push, weight, wide):
    rate = math.sqrt(max(1.0, PROJ / D)) if wide else math.sqrt(max(1.0, D / D_INNER))
    whole = pltpu.VMEM((D, D), jnp.float32)
    half = pltpu.VMEM((D, D), jnp.bfloat16)
    return pl.pallas_call(
        functools.partial(newton_kernel, wide, rate),
        out_shape=jax.ShapeDtypeStruct(weight.shape, jnp.float32),
        scratch_shapes=[whole, whole, whole, whole, half, half, half],
        compiler_params=pltpu.CompilerParams(vmem_limit_bytes=56 * 1024 * 1024),
        cost_estimate=pl.CostEstimate(
            flops=17 * 2 * D**3 + 2 * D * push.size, bytes_accessed=12 * push.size, transcendentals=0
        ),
        name="newton_in" if wide else "newton_out",
    )(gram, push, weight)


def own_slice(whole, width, along):
    return lax.dynamic_slice_in_dim(whole, lax.axis_index("opt") * width, width, along)


def exchange(value, axis, bit):
    count = lax.axis_size(axis)
    return lax.ppermute(value, axis, [(i, i ^ (1 << bit)) for i in range(count)])


def side_of(axis, bit):
    return (lax.axis_index(axis) >> bit) & 1


def fold(value, axis, bit, dim):
    half = value.shape[dim] // 2
    side = side_of(axis, bit)
    sent = lax.dynamic_slice_in_dim(value, (1 - side) * half, half, dim)
    kept = lax.dynamic_slice_in_dim(value, side * half, half, dim)
    return kept + exchange(sent, axis, bit)


def unfold(value, axis, bit, dim):
    other = exchange(value, axis, bit)
    first = jnp.where(side_of(axis, bit) == 0, value, other)
    second = jnp.where(side_of(axis, bit) == 0, other, value)
    return jnp.concatenate([first, second], axis=dim)


def group_bits():
    return range(1, (lax.axis_size("dp") - 1).bit_length())


def gather_rows(piece):
    for bit in reversed(group_bits()):
        piece = unfold(piece, "dp", bit, 1)
    piece = unfold(piece, "dp", 0, 1)
    return piece.reshape(-1, piece.shape[-1])


def reduce_owned(pair):
    rows = pair.shape[1] // 2
    one = fold(pair[:, :rows], "opt", 1, 0)[0]
    two = fold(pair[:, rows:], "dp", 0, 1)
    one = fold(one, "dp", 0, 0)
    two = fold(two, "opt", 1, 0)[0]
    piece = jnp.stack([one, two])
    for bit in group_bits():
        piece = fold(piece, "dp", bit, 1)
    return gather_rows(piece).astype(jnp.float32)


def sum_everywhere(value):
    for axis in ("opt", "dp"):
        for bit in range((lax.axis_size(axis) - 1).bit_length()):
            value = value + exchange(value, axis, bit)
    return value


def fetch_shards(shard):
    across = exchange(shard, "opt", 1)
    return [shard, exchange(shard, "opt", 0), across, exchange(across, "opt", 0)]


def in_order(pieces):
    core, far = side_of("opt", 0) == 0, side_of("opt", 1) == 0
    near = [jnp.where(core, pieces[0], pieces[1]), jnp.where(core, pieces[1], pieces[0])]
    other = [jnp.where(core, pieces[2], pieces[3]), jnp.where(core, pieces[3], pieces[2])]
    low = [jnp.where(far, n, o) for n, o in zip(near, other)]
    high = [jnp.where(far, o, n) for n, o in zip(near, other)]
    return jnp.concatenate(low + high, axis=0)


COLUMN_BLOCK = 384
SHARD = PROJ // 4


def project_kernel(
    place_ref, tokens_ref, gain_ref, own_ref, core_ref, across_ref, last_ref,
    proj_ref, hidden_ref, weight_out_ref, scale_ref,
    shards_ref, weight_ref, normed_ref, sems,
):
    step = pl.program_id(0)

    @pl.when(step == 0)
    def start():
        copies = [
            pltpu.make_async_copy(ref, shards_ref.at[place_ref[0] ^ place], sems.at[place])
            for place, ref in enumerate((own_ref, core_ref, across_ref, last_ref))
        ]
        for copy in copies:
            copy.start()
        inflow = tokens_ref[...].astype(jnp.float32)
        scale = lax.rsqrt(jnp.mean(inflow * inflow, axis=1, keepdims=True) + EPSILON)
        normed_ref[...] = (inflow * scale * gain_ref[...]).astype(jnp.bfloat16)
        hidden_ref[...] = normed_ref[...]
        scale_ref[...] = jnp.broadcast_to(scale, scale_ref.shape)
        for copy in copies:
            copy.wait()
        weight_ref[:, PROJ - PROJ % 128 :] = jnp.zeros((D, PADDED - PROJ + PROJ % 128), jnp.bfloat16)
        for place in range(4):
            weight_ref[:, place * SHARD : (place + 1) * SHARD] = shards_ref[place]

    block = weight_ref[:, pl.ds(pl.multiple_of(step * COLUMN_BLOCK, 128), COLUMN_BLOCK)]
    weight_out_ref[...] = block
    proj_ref[...] = dot32(normed_ref[...], block).astype(jnp.bfloat16)


def project(tokens, gain_vec, pieces):
    length = tokens.shape[0]
    bf16 = jnp.bfloat16
    hold = pl.BlockSpec(memory_space=pl.ANY)
    return pl.pallas_call(
        project_kernel,
        grid=(PADDED // COLUMN_BLOCK,),
        in_specs=[pl.BlockSpec(memory_space=pltpu.SMEM), fixed_block(length, D), fixed_block(1, D)] + [hold] * 4,
        out_specs=[
            pl.BlockSpec((length, COLUMN_BLOCK), lambda i: (0, i)),
            fixed_block(length, D),
            pl.BlockSpec((D, COLUMN_BLOCK), lambda i: (0, i)),
            fixed_block(length, 128),
        ],
        out_shape=[
            jax.ShapeDtypeStruct((length, PADDED), bf16), jax.ShapeDtypeStruct((length, D), bf16),
            jax.ShapeDtypeStruct((D, PADDED), bf16), jax.ShapeDtypeStruct((length, 128), jnp.float32),
        ],
        scratch_shapes=[
            pltpu.VMEM((4, D, SHARD), bf16), pltpu.VMEM((D, PADDED), bf16), pltpu.VMEM((length, D), bf16),
            pltpu.SemaphoreType.DMA((4,)),
        ],
        compiler_params=pltpu.CompilerParams(
            dimension_semantics=("arbitrary",), vmem_limit_bytes=VMEM_LIMIT
        ),
        cost_estimate=pl.CostEstimate(
            flops=2 * length * D * PADDED, bytes_accessed=22 * 10**6, transcendentals=0
        ),
        name="project",
    )(lax.axis_index("opt").astype(jnp.int32)[None], tokens, gain_vec[None, :], *pieces)


GATE_BLOCKS = D_INNER // COLUMN_BLOCK
CONV_BLOCKS = (PADDED - D_INNER) // COLUMN_BLOCK


def weight_grad_kernel(place_ref, hidden_ref, gate_ref, conv_ref, kept_ref, sent_ref, turned_ref, whole_ref):
    step = pl.program_id(0)

    @pl.when(step == 0)
    def start():
        turned_ref[...] = hidden_ref[...].astype(jnp.float32).T.astype(jnp.bfloat16)

    def work(ref):
        columns = pl.ds(pl.multiple_of(step * COLUMN_BLOCK, 128), COLUMN_BLOCK)
        whole_ref[:, columns] = dot32(turned_ref[...], ref[...]).astype(jnp.bfloat16)

    pl.when(step < GATE_BLOCKS)(lambda: work(gate_ref))
    pl.when(step >= GATE_BLOCKS)(lambda: work(conv_ref))

    @pl.when(step == GATE_BLOCKS + CONV_BLOCKS - 1)
    def finish():
        for core in range(2):
            @pl.when(place_ref[0] == core)
            def store():
                for shard in range(4):
                    target = kept_ref if shard % 2 == core else sent_ref
                    target[shard // 2] = whole_ref[:, shard * SHARD : (shard + 1) * SHARD]


def weight_grad(hidden, gate, conv):
    length = hidden.shape[0]
    bf16 = jnp.bfloat16
    shards = jax.ShapeDtypeStruct((2, D, SHARD), bf16)
    return pl.pallas_call(
        weight_grad_kernel,
        grid=(GATE_BLOCKS + CONV_BLOCKS,),
        in_specs=[
            pl.BlockSpec(memory_space=pltpu.SMEM),
            fixed_block(length, D),
            pl.BlockSpec((length, COLUMN_BLOCK), lambda i: (0, jnp.minimum(i, GATE_BLOCKS - 1))),
            pl.BlockSpec((length, COLUMN_BLOCK), lambda i: (0, jnp.maximum(i - GATE_BLOCKS, 0))),
        ],
        out_specs=[fixed_block(2, D, SHARD), fixed_block(2, D, SHARD)],
        out_shape=[shards, shards],
        scratch_shapes=[pltpu.VMEM((D, length), bf16), pltpu.VMEM((D, PADDED), bf16)],
        compiler_params=pltpu.CompilerParams(
            dimension_semantics=("arbitrary",), vmem_limit_bytes=VMEM_LIMIT
        ),
        cost_estimate=pl.CostEstimate(
            flops=2 * length * D * PADDED, bytes_accessed=14 * 10**6, transcendentals=0
        ),
        name="weight_grad",
    )(side_of("opt", 0).astype(jnp.int32)[None], hidden, gate, conv)


def on_device(tokens, cotangent, w_in, w_out, small, mom_in, mom_out, adam_m, adam_v):
    bf16 = jnp.bfloat16
    small_b = in_order(fetch_shards(small.astype(bf16)))
    pieces = fetch_shards(w_in.astype(bf16))
    own_out, pieces[2] = lax.optimization_barrier((w_out.astype(bf16), pieces[2]))
    w_out_b = in_order(fetch_shards(own_out))
    params = small_b.astype(jnp.float32)
    gain_vec = params[:D]
    sections = [D, D + D_INNER, D + D_INNER + CONV * CONV_CH]
    sections += [sections[-1] + CONV_CH + place * HEADS for place in range(3)]
    gain_vec, gate_gain, taps, conv_bias, dt_bias, a_log, skip_gain = jnp.split(params, sections)
    taps = taps.reshape(CONV, CONV_CH)
    rate = -jnp.exp(a_log)
    skip_wide = jnp.repeat(skip_gain, HEAD_CHANNELS)[None, :]
    spread, reduce_mat = head_matrices()
    fixed = (skip_wide, pad_heads(dt_bias), pad_heads(rate), spread, reduce_mat)
    inflow = tokens.astype(jnp.float32)
    projected, hidden, w_pad, scale = project(tokens, gain_vec, pieces)
    grad_mixed = dot_nt(cotangent, w_out_b).astype(jnp.bfloat16)
    mixed, active, slope, grad_scan, grad_gate, states, inner, gain_acc, skip_acc = mixer_forward(
        projected, grad_mixed, taps, conv_bias[None, :], gate_gain[None, :], *fixed
    )
    block = (inflow + dot32(mixed, w_out_b)).astype(jnp.bfloat16)
    grad_w_out = dot_tn(mixed, cotangent).astype(bf16).reshape(2, 2, -1, D)
    owned_out = reduce_owned(fold(grad_w_out, "opt", 0, 1)[:, 0])
    grad_conv, taps_acc, bias_acc, dt_acc, rate_acc = mixer_backward(
        projected, active, slope, grad_scan, states, inner, taps, *fixed
    )
    kept, sent = weight_grad(hidden, grad_gate, grad_conv)
    grad_hidden = dot_nt(grad_gate, w_pad[:, :D_INNER]) + dot_nt(grad_conv, w_pad[:, D_INNER:])
    normal = inflow * scale[:, :1]
    grad_gain = jnp.sum(normal * grad_hidden, axis=0)
    grad_normal = grad_hidden * gain_vec
    grad_tokens = cotangent.astype(jnp.float32) + scale[:, :1] * (
        grad_normal - normal * jnp.mean(grad_normal * normal, axis=1, keepdims=True)
    )
    grad_small = jnp.concatenate([
        grad_gain,
        gain_acc.sum(0),
        taps_acc.sum(1).reshape(-1),
        bias_acc.sum(0),
        dt_acc.sum(0)[:HEADS],
        rate_acc.sum(0)[:HEADS] * rate,
        skip_acc.sum(0).reshape(HEADS, HEAD_CHANNELS).sum(1),
    ])
    pair_in = kept + exchange(sent, "opt", 0)
    owned_in = reduce_owned(pair_in)
    owned_small = own_slice(sum_everywhere(grad_small), small.shape[0], 0)
    adam_m_new = BETA_ONE * adam_m + (1.0 - BETA_ONE) * owned_small
    adam_v_new = BETA_TWO * adam_v + (1.0 - BETA_TWO) * owned_small * owned_small
    small_new = small * (1.0 - ADAM_RATE * DECAY) - ADAM_RATE * (
        adam_m_new / (1.0 - BETA_ONE**STEP)
    ) / (jnp.sqrt(adam_v_new / (1.0 - BETA_TWO**STEP)) + ADAM_EPS)
    mom_in_new = MOMENTUM * mom_in + owned_in
    push_in = owned_in + MOMENTUM * mom_in_new
    mom_out_new = MOMENTUM * mom_out + owned_out
    push_out = owned_out + MOMENTUM * mom_out_new
    pushed_in = push_in.astype(jnp.bfloat16)
    pushed_out = push_out.astype(jnp.bfloat16)
    gram_in = gram_sum(pushed_in, True)
    gram_out = gram_sum(pushed_out, False)
    w_in_new = newton_update(gram_in, push_in, w_in, True)
    w_out_new = newton_update(gram_out, push_out, w_out, False)
    return (
        block,
        grad_tokens,
        owned_in,
        owned_out,
        owned_small,
        mom_in_new,
        mom_out_new,
        w_in_new,
        w_out_new,
        small_new,
        adam_m_new,
        adam_v_new,
    )


def solution(mesh):
    in_specs = (
        P(("dp", "opt"), None),
        P(("dp", "opt"), None),
        P(None, "opt"),
        P("opt", None),
        P("opt"),
        P(None, "opt"),
        P("opt", None),
        P("opt"),
        P("opt"),
    )
    out_specs = (
        P(("dp", "opt"), None),
        P(("dp", "opt"), None),
        P(None, "opt"),
        P("opt", None),
        P("opt"),
        P(None, "opt"),
        P("opt", None),
        P(None, "opt"),
        P("opt", None),
        P("opt"),
        P("opt"),
        P("opt"),
    )
    return jax.shard_map(
        on_device, mesh=mesh, in_specs=in_specs, out_specs=out_specs, check_vma=False
    )
```

```python
import functools
import math

import jax
import jax.numpy as jnp
from jax import lax
from jax.experimental import pallas as pl
from jax.experimental.pallas import tpu as pltpu
from jax.sharding import PartitionSpec as P

D = 768
HEADS = 24
HEAD_CHANNELS = 64
STATE = 128
CONV = 4
SEQ_LEN = 1024
STEP = 10
D_INNER = 1536
CONV_CH = 1792
PROJ = 3352


EPSILON = 1e-05
COEF_A = 3.4445
COEF_B = -4.775
COEF_C = 2.0315
MOMENTUM = 0.95
MUON_RATE = 0.5
DECAY = 0.01
ADAM_RATE = 0.2
BETA_ONE = 0.9
BETA_TWO = 0.95
ADAM_EPS = 1e-08


SPAN = 128
CHUNKS = SEQ_LEN // SPAN
PAIRS = HEADS // 2
WIDTH = 2 * HEAD_CHANNELS
CONV_END = D_INNER + CONV_CH
PADDED = CONV_END + 128
TAIL = 8
VMEM_LIMIT = 56 * 1024 * 1024


def dot32(left, right):
    return jnp.dot(left, right, preferred_element_type=jnp.float32)


def dot_nt(left, right):
    return lax.dot_general(left, right, (((1,), (1,)), ((), ())), preferred_element_type=jnp.float32)


def dot_tn(left, right):
    return lax.dot_general(left, right, (((0,), (0,)), ((), ())), preferred_element_type=jnp.float32)


def halves(value):
    high = value.astype(jnp.bfloat16)
    return high, (value - high.astype(jnp.float32)).astype(jnp.bfloat16)


def sigmoid(value):
    return 0.5 * jnp.tanh(0.5 * value) + 0.5


def softplus(value):
    return jnp.maximum(value, 0.0) + jnp.log1p(jnp.exp(-jnp.abs(value)))


def fold_rows(value):
    return jnp.sum(value.reshape(value.shape[0] // 8, 8, value.shape[1]), axis=0)


def triangle(lower):
    rows = lax.broadcasted_iota(jnp.int32, (SPAN, SPAN), 0)
    cols = lax.broadcasted_iota(jnp.int32, (SPAN, SPAN), 1)
    return rows >= cols if lower else rows <= cols


def running_sum(mask, value):
    ones = jnp.where(mask, 1.0, 0.0).astype(jnp.bfloat16)
    high, rest = halves(value)
    low = (value - high.astype(jnp.float32) - rest.astype(jnp.float32)).astype(jnp.bfloat16)
    return dot32(ones, high) + (dot32(ones, rest) + dot32(ones, low))


def head_sums(value, reduce_mat):
    high, low = halves(value)
    return dot32(high, reduce_mat) + dot32(low, reduce_mat)


def step_factors(raw, dt_bias, rate, spread):
    step_size = softplus(raw + dt_bias)
    log_decay = running_sum(triangle(True), step_size * rate)
    last = log_decay[SPAN - 1 : SPAN, :]
    stacked = jnp.concatenate([step_size, jnp.exp(log_decay), jnp.exp(last - log_decay)], axis=0)
    high, low = halves(stacked)
    wide = dot32(jnp.concatenate([high, low], axis=1), spread)
    return step_size, log_decay, wide[:SPAN], wide[SPAN : 2 * SPAN], wide[2 * SPAN :]


def split_pair(value, first):
    return jnp.concatenate(
        [jnp.where(first, value, 0.0), jnp.where(first, 0.0, value)], axis=0
    ).astype(jnp.bfloat16)


def forward_kernel(
    proj_ref, back_ref, taps_ref, conv_bias_ref, gate_gain_ref, skip_ref, dt_bias_ref, rate_ref, spread_ref, reduce_ref,
    mixed_ref, active_ref, slope_ref, grad_scan_ref, grad_gate_ref, states_ref, inner_ref, gain_acc_ref, skip_acc_ref,
    window_ref, state_ref,
):
    f32, bf16 = jnp.float32, jnp.bfloat16

    @pl.when(pl.program_id(0) == 0)
    def start():
        window_ref[0:TAIL, :] = jnp.zeros((TAIL, CONV_CH), f32)
        state_ref[...] = jnp.zeros((STATE, D_INNER), f32)
        gain_acc_ref[...] = jnp.zeros((8, D_INNER), f32)
        skip_acc_ref[...] = jnp.zeros((8, D_INNER), f32)

    window_ref[TAIL:, :] = proj_ref[:, D_INNER:CONV_END].astype(f32)
    conv_out = conv_bias_ref[...]
    for tap in range(CONV):
        start_row = TAIL - (CONV - 1) + tap
        conv_out = conv_out + taps_ref[tap : tap + 1, :] * window_ref[start_row : start_row + SPAN, :]
    window_ref[0:TAIL, :] = window_ref[SPAN:, :]
    part = sigmoid(conv_out)
    silu = conv_out * part
    active_ref[...] = silu.astype(bf16)
    slope_ref[...] = (part + silu * (1.0 - part)).astype(bf16)

    values = active_ref[:, :D_INNER].astype(f32)
    input_b = active_ref[:, D_INNER : D_INNER + STATE]
    output_c = active_ref[:, D_INNER + STATE :]
    step_size, log_decay, step_wide, decay_wide, end_wide = step_factors(
        proj_ref[:, CONV_END:].astype(f32), dt_bias_ref[...], rate_ref[...], spread_ref[...]
    )
    decay_rows = log_decay.T
    moved = step_wide * values
    state = state_ref[...]
    state_low = state.astype(bf16)
    states_ref[0] = state_low
    state_ref[...] = state * decay_wide[SPAN - 1 : SPAN, :] + dot_tn(input_b, (moved * end_wide).astype(bf16))
    scores = dot_nt(output_c, input_b)
    causal = triangle(True)
    first = lax.broadcasted_iota(jnp.int32, (SPAN, WIDTH), 1) < HEAD_CHANNELS
    pieces = []
    for pair in range(PAIRS):
        lanes = slice(pair * WIDTH, (pair + 1) * WIDTH)
        mixing = []
        for head in (2 * pair, 2 * pair + 1):
            differ = log_decay[:, head : head + 1] - decay_rows[head : head + 1, :]
            mixing.append((scores * jnp.exp(jnp.where(causal, differ, -1e30))).astype(bf16))
        pieces.append(dot32(jnp.concatenate(mixing, axis=1), split_pair(moved[:, lanes], first)))
    inner = jnp.concatenate(pieces, axis=1) + dot32(output_c, state_low) * decay_wide
    scanned = inner + skip_ref[...] * values

    gate_in = proj_ref[:, :D_INNER].astype(f32)
    part = sigmoid(gate_in)
    gate = gate_in * part
    gated = scanned * gate
    scale = lax.rsqrt(jnp.mean(gated * gated, axis=1, keepdims=True) + EPSILON)
    normal = gated * scale
    mixed_ref[...] = (normal * gate_gain_ref[...]).astype(bf16)
    back = back_ref[...].astype(f32)
    gain_acc_ref[...] += fold_rows(back * normal)
    back = back * gate_gain_ref[...]
    grad_gated = scale * (back - normal * jnp.mean(back * normal, axis=1, keepdims=True))
    grad_gate_ref[...] = (grad_gated * scanned * (part + gate * (1.0 - part))).astype(bf16)
    grad_scan_low = (grad_gated * gate).astype(bf16)
    grad_scan_ref[...] = grad_scan_low
    grad_scan = grad_scan_low.astype(f32)
    skip_acc_ref[...] += fold_rows(grad_scan * values)
    inner_ref[...] = head_sums(grad_scan * inner, reduce_ref[...])


def backward_kernel(
    proj_ref, active_ref, slope_ref, grad_scan_ref, states_ref, inner_ref, taps_ref, skip_ref, dt_bias_ref, rate_ref,
    spread_ref, reduce_ref,
    grad_ref, taps_acc_ref, bias_acc_ref, dt_acc_ref, rate_acc_ref,
    window_ref, costate_ref,
):
    f32, bf16 = jnp.float32, jnp.bfloat16

    @pl.when(pl.program_id(0) == 0)
    def start():
        window_ref[SPAN:, :] = jnp.zeros((TAIL, CONV_CH), f32)
        costate_ref[...] = jnp.zeros((STATE, D_INNER), f32)
        taps_acc_ref[...] = jnp.zeros((CONV, 8, CONV_CH), f32)
        bias_acc_ref[...] = jnp.zeros((8, CONV_CH), f32)
        dt_acc_ref[...] = jnp.zeros((8, 128), f32)
        rate_acc_ref[...] = jnp.zeros((8, 128), f32)

    values = active_ref[:, :D_INNER].astype(f32)
    input_b = active_ref[:, D_INNER : D_INNER + STATE]
    output_c = active_ref[:, D_INNER + STATE :]
    raw = proj_ref[:, CONV_END:].astype(f32)
    rate = rate_ref[...]
    step_size, log_decay, step_wide, decay_wide, end_wide = step_factors(raw, dt_bias_ref[...], rate, spread_ref[...])
    decay_rows = log_decay.T
    moved = step_wide * values
    grad_scan_low = grad_scan_ref[...]
    grad_scan = grad_scan_low.astype(f32)
    scores = dot_nt(input_b, output_c)
    causal = triangle(False)
    first = lax.broadcasted_iota(jnp.int32, (SPAN, WIDTH), 1) < HEAD_CHANNELS
    grad_scores = jnp.zeros((SPAN, SPAN), f32)
    pieces = []
    for pair in range(PAIRS):
        lanes = slice(pair * WIDTH, (pair + 1) * WIDTH)
        moved_low = moved[:, lanes].astype(bf16)
        grad_pair = split_pair(grad_scan[:, lanes], first)
        grad_mixing = dot_nt(moved_low, grad_pair)
        mixing = []
        for place, head in enumerate((2 * pair, 2 * pair + 1)):
            differ = decay_rows[head : head + 1, :] - log_decay[:, head : head + 1]
            decay = jnp.exp(jnp.where(causal, differ, -1e30))
            mixing.append((scores * decay).astype(bf16))
            grad_scores = grad_scores + decay * grad_mixing[:, place * SPAN : (place + 1) * SPAN]
        pieces.append(dot32(jnp.concatenate(mixing, axis=1), grad_pair))
    grad_inner = jnp.concatenate(pieces, axis=1)

    costate = costate_ref[...]
    costate_low = costate.astype(bf16)
    states_low = states_ref[0]
    last_wide = decay_wide[SPAN - 1 : SPAN, :]
    kept = fold_rows(costate * states_low.astype(f32)) * last_wide
    grad_cross = dot32(input_b, costate_low) * end_wide
    grad_decayed = (grad_scan * decay_wide).astype(bf16)
    grad_scores_low = grad_scores.astype(bf16)
    grad_b = dot32(grad_scores_low, output_c) + dot_nt((moved * end_wide).astype(bf16), costate_low)
    grad_c = dot_tn(grad_scores_low, input_b) + dot_nt(grad_decayed, states_low)
    costate_ref[...] = costate * last_wide + dot_tn(output_c, grad_decayed)

    moved_round = moved.astype(bf16).astype(f32)
    grad_moved = grad_inner + grad_cross
    reduce_mat = reduce_ref[...]
    own = head_sums(moved_round * grad_inner, reduce_mat)
    crossing = dot32((moved * grad_cross).astype(bf16), reduce_mat)
    grad_step = dot32((values * grad_moved).astype(bf16), reduce_mat)
    keeping = jnp.sum(head_sums(kept, reduce_mat), axis=0, keepdims=True)
    grad_log = (
        running_sum(triangle(False), inner_ref[...] - own)
        + running_sum(triangle(True), crossing) - crossing
        + keeping
    )
    grad_raw = (grad_step + rate * grad_log) * sigmoid(raw + dt_bias_ref[...])
    rate_acc_ref[...] += fold_rows(step_size * grad_log)
    dt_acc_ref[...] += fold_rows(grad_raw)
    grad_ref[:, CONV_CH:] = grad_raw.astype(bf16)

    grad_values = step_wide * grad_moved + skip_ref[...] * grad_scan
    grad_active = jnp.concatenate([grad_values, grad_b, grad_c], axis=1)
    grad_conv = grad_active * slope_ref[...].astype(f32)
    bias_acc_ref[...] += fold_rows(grad_conv)
    window_ref[0:SPAN, :] = grad_conv
    conv_in = proj_ref[:, D_INNER:CONV_END].astype(f32)
    grad_in = jnp.zeros((SPAN, CONV_CH), f32)
    for tap in range(CONV):
        start_row = CONV - 1 - tap
        shifted = window_ref[start_row : start_row + SPAN, :]
        grad_in = grad_in + taps_ref[tap : tap + 1, :] * shifted
        taps_acc_ref[tap] += fold_rows(conv_in * shifted)
    grad_ref[:, :CONV_CH] = grad_in.astype(bf16)
    window_ref[SPAN:, :] = window_ref[0:TAIL, :]


def head_matrices():
    spread = jnp.pad(jnp.repeat(jnp.eye(HEADS, dtype=jnp.bfloat16), HEAD_CHANNELS, axis=1), ((0, 128 - HEADS), (0, 0)))
    return jnp.concatenate([spread, spread], axis=0), spread.T


def row_block(width, order):
    return pl.BlockSpec((SPAN, width), lambda i: (order(i), 0))


def fixed_block(*shape):
    return pl.BlockSpec(shape, lambda i: (0,) * len(shape))


def state_block(order):
    return pl.BlockSpec((1, STATE, D_INNER), lambda i: (order(i), 0, 0))


def pad_heads(vector):
    return jnp.pad(vector, (0, 128 - HEADS))[None, :]


def mixer_forward(projected, back, taps, conv_bias, gate_gain, skip_wide, dt_bias, rate, spread, reduce_mat):
    f32, bf16 = jnp.float32, jnp.bfloat16
    order = lambda i: i
    rows = lambda width, kind: jax.ShapeDtypeStruct((SEQ_LEN, width), kind)
    return pl.pallas_call(
        forward_kernel,
        grid=(CHUNKS,),
        in_specs=[
            row_block(PADDED, order), row_block(D_INNER, order), fixed_block(CONV, CONV_CH), fixed_block(1, CONV_CH),
            fixed_block(1, D_INNER), fixed_block(1, D_INNER), fixed_block(1, 128), fixed_block(1, 128),
            fixed_block(256, D_INNER), fixed_block(D_INNER, 128),
        ],
        out_specs=[
            row_block(D_INNER, order), row_block(CONV_CH, order), row_block(CONV_CH, order), row_block(D_INNER, order),
            row_block(D_INNER, order), state_block(order), row_block(128, order), fixed_block(8, D_INNER),
            fixed_block(8, D_INNER),
        ],
        out_shape=[
            rows(D_INNER, bf16), rows(CONV_CH, bf16), rows(CONV_CH, bf16), rows(D_INNER, bf16), rows(D_INNER, bf16),
            jax.ShapeDtypeStruct((CHUNKS, STATE, D_INNER), bf16), rows(128, f32),
            jax.ShapeDtypeStruct((8, D_INNER), f32), jax.ShapeDtypeStruct((8, D_INNER), f32),
        ],
        scratch_shapes=[pltpu.VMEM((SPAN + TAIL, CONV_CH), f32), pltpu.VMEM((STATE, D_INNER), f32)],
        compiler_params=pltpu.CompilerParams(
            dimension_semantics=("arbitrary",), vmem_limit_bytes=VMEM_LIMIT
        ),
        cost_estimate=pl.CostEstimate(flops=8 * 10**9, bytes_accessed=32 * 10**6, transcendentals=10**7),
        name="mixer_forward",
    )(projected, back, taps, conv_bias, gate_gain, skip_wide, dt_bias, rate, spread, reduce_mat)


def mixer_backward(projected, active, slope, grad_scan, states, inner, taps, skip_wide, dt_bias, rate, spread, reduce_mat):
    f32, bf16 = jnp.float32, jnp.bfloat16
    order = lambda i: CHUNKS - 1 - i
    return pl.pallas_call(
        backward_kernel,
        grid=(CHUNKS,),
        in_specs=[
            row_block(PADDED, order), row_block(CONV_CH, order), row_block(CONV_CH, order), row_block(D_INNER, order),
            state_block(order), row_block(128, order), fixed_block(CONV, CONV_CH), fixed_block(1, D_INNER),
            fixed_block(1, 128), fixed_block(1, 128), fixed_block(256, D_INNER), fixed_block(D_INNER, 128),
        ],
        out_specs=[
            row_block(CONV_CH + 128, order), fixed_block(CONV, 8, CONV_CH), fixed_block(8, CONV_CH),
            fixed_block(8, 128), fixed_block(8, 128),
        ],
        out_shape=[
            jax.ShapeDtypeStruct((SEQ_LEN, CONV_CH + 128), bf16), jax.ShapeDtypeStruct((CONV, 8, CONV_CH), f32),
            jax.ShapeDtypeStruct((8, CONV_CH), f32), jax.ShapeDtypeStruct((8, 128), f32),
            jax.ShapeDtypeStruct((8, 128), f32),
        ],
        scratch_shapes=[pltpu.VMEM((SPAN + TAIL, CONV_CH), f32), pltpu.VMEM((STATE, D_INNER), f32)],
        compiler_params=pltpu.CompilerParams(
            dimension_semantics=("arbitrary",), vmem_limit_bytes=VMEM_LIMIT
        ),
        cost_estimate=pl.CostEstimate(flops=12 * 10**9, bytes_accessed=32 * 10**6, transcendentals=10**7),
        name="mixer_backward",
    )(projected, active, slope, grad_scan, states, inner, taps, skip_wide, dt_bias, rate, spread, reduce_mat)


ROW_BLOCK = 256
UPPER = [(0, 0), (0, 1), (0, 2), (1, 1), (1, 2), (2, 2)]


def gram_kernel(wide, push_ref, gram_ref):
    for place, (row, col) in enumerate(UPPER):
        rows = slice(row * ROW_BLOCK, (row + 1) * ROW_BLOCK)
        cols = slice(col * ROW_BLOCK, (col + 1) * ROW_BLOCK)
        if wide:
            gram_ref[place] = dot_nt(push_ref[rows, :], push_ref[cols, :])
        else:
            gram_ref[place] = dot_tn(push_ref[:, rows], push_ref[:, cols])


def gram_sum(push, wide):
    tiles = pl.pallas_call(
        functools.partial(gram_kernel, wide),
        out_shape=jax.ShapeDtypeStruct((len(UPPER), ROW_BLOCK, ROW_BLOCK), jnp.float32),
        compiler_params=pltpu.CompilerParams(vmem_limit_bytes=VMEM_LIMIT),
        cost_estimate=pl.CostEstimate(
            flops=2 * D * push.size, bytes_accessed=2 * push.size, transcendentals=0
        ),
        name="gram_in" if wide else "gram_out",
    )(push)
    part = fold(tiles, "opt", 0, 0)
    part = part + exchange(part, "opt", 1)
    return unfold(part, "opt", 0, 0)


def newton_kernel(wide, rate, begin, end, *refs):
    if begin == 0:
        gram_ref, refs = refs[0], refs[1:]
    else:
        (a_in_ref, r_in_ref, norm_ref), refs = refs[:3], refs[3:]
    if end == 5:
        (push_ref, weight_ref, new_ref), refs = refs[:3], refs[3:]
    else:
        (a_out_ref, r_out_ref, norm_out_ref), refs = refs[:3], refs[3:]
    a_ref, p_ref, t_ref, r_ref, e_ref, k_ref, f_ref = refs
    blocks = [slice(i, i + ROW_BLOCK) for i in range(0, D, ROW_BLOCK)]
    size = 1.0 / D

    def eye_of(block):
        rows = lax.broadcasted_iota(jnp.int32, (ROW_BLOCK, D), 0) + block.start
        cols = lax.broadcasted_iota(jnp.int32, (ROW_BLOCK, D), 1)
        return rows == cols

    def trace_part(value, block):
        kept = jnp.where(eye_of(block), value, 0.0)
        return jnp.sum(jnp.sum(kept, axis=0, keepdims=True), axis=1, keepdims=True)

    def shifted(value, block, amount):
        return value - jnp.where(eye_of(block), amount, 0.0)

    if begin == 0:
        total = 0.0
        for place, (row, col) in enumerate(UPPER):
            tile = gram_ref[place]
            a_ref[blocks[row], blocks[col]] = tile
            if row == col:
                kept = jnp.where(eye_of(blocks[0])[:, :ROW_BLOCK], tile, 0.0)
                total += jnp.sum(jnp.sum(kept, axis=0, keepdims=True), axis=1, keepdims=True)
            else:
                a_ref[blocks[col], blocks[row]] = tile.T
        norm = 1.0 / (jnp.sqrt(total) + 1e-07)
        scale = norm * norm
        for block in blocks:
            a_ref[block, :] = a_ref[block, :] * scale
        mean = total * scale * size
    else:
        norm = norm_ref[...]
        a_ref[...] = a_in_ref[...]
        r_ref[...] = r_in_ref[...]
        mean = sum(trace_part(a_ref[block, :], block) for block in blocks) * size
        r_mean = sum(trace_part(r_ref[block, :], block) for block in blocks) * size
    for sweep in range(begin, end):
        for block in blocks:
            e_ref[block, :] = shifted(a_ref[block, :], block, mean).astype(jnp.bfloat16)
        trace = 0.0
        for block in blocks:
            rest = shifted(a_ref[block, :], block, mean)
            square = 2.0 * mean * rest + dot32(e_ref[block, :], e_ref[...])
            poly = COEF_B * a_ref[block, :] + COEF_C * shifted(square, block, -mean * mean)
            trace += trace_part(poly, block)
            p_ref[block, :] = poly
        shift = trace * size
        lead = COEF_A + shift
        for block in blocks:
            k_ref[block, :] = shifted(p_ref[block, :], block, shift).astype(jnp.bfloat16)
        if sweep == 0:
            for block in blocks:
                r_ref[block, :] = shifted(p_ref[block, :], block, -COEF_A)
            r_mean = lead
        else:
            for block in blocks:
                f_ref[block, :] = shifted(r_ref[block, :], block, r_mean).astype(jnp.bfloat16)
            trace = 0.0
            for block in blocks:
                value = (
                    lead * r_ref[block, :]
                    + r_mean * k_ref[block, :].astype(jnp.float32)
                    + dot32(k_ref[block, :], f_ref[...])
                )
                trace += trace_part(value, block)
                r_ref[block, :] = value
            r_mean = trace * size
        if sweep < 4:
            trace = 0.0
            for block in blocks:
                value = (
                    lead * a_ref[block, :]
                    + mean * k_ref[block, :].astype(jnp.float32)
                    + dot32(k_ref[block, :], e_ref[...])
                )
                trace += trace_part(value, block)
                t_ref[block, :] = value
            t_mean = trace * size
            for block in blocks:
                f_ref[block, :] = shifted(t_ref[block, :], block, t_mean).astype(jnp.bfloat16)
            trace = 0.0
            for block in blocks:
                value = (
                    lead * t_ref[block, :]
                    + t_mean * k_ref[block, :].astype(jnp.float32)
                    + dot32(f_ref[block, :], k_ref[...])
                )
                trace += trace_part(value, block)
                a_ref[block, :] = value
            mean = trace * size
    if end < 5:
        a_out_ref[...] = a_ref[...]
        r_out_ref[...] = r_ref[...]
        norm_out_ref[...] = norm
        return
    for block in blocks:
        f_ref[block, :] = shifted(r_ref[block, :], block, r_mean).astype(jnp.bfloat16)
    step = norm * (MUON_RATE * rate)
    if wide:
        moved = push_ref[...].astype(jnp.bfloat16)
        for block in blocks:
            ortho = r_mean * push_ref[block, :] + dot32(f_ref[block, :], moved)
            new_ref[block, :] = weight_ref[block, :] * (1.0 - MUON_RATE * DECAY) - step * ortho
    else:
        ortho = r_mean * push_ref[...] + dot32(push_ref[...].astype(jnp.bfloat16), f_ref[...])
        new_ref[...] = weight_ref[...] * (1.0 - MUON_RATE * DECAY) - step * ortho


def newton_call(inputs, outs, wide, begin, end):
    rate = math.sqrt(max(1.0, PROJ / D)) if wide else math.sqrt(max(1.0, D / D_INNER))
    whole = pltpu.VMEM((D, D), jnp.float32)
    half = pltpu.VMEM((D, D), jnp.bfloat16)
    return pl.pallas_call(
        functools.partial(newton_kernel, wide, rate, begin, end),
        out_shape=[jax.ShapeDtypeStruct(shape, jnp.float32) for shape in outs],
        scratch_shapes=[whole, whole, whole, whole, half, half, half],
        compiler_params=pltpu.CompilerParams(vmem_limit_bytes=VMEM_LIMIT),
        cost_estimate=pl.CostEstimate(
            flops=2 * 5 * (end - begin) * 2 * D**3, bytes_accessed=10**7, transcendentals=0
        ),
        name=("newton_in" if wide else "newton_out") + str(begin),
    )(*inputs)


def own_slice(whole, width, along):
    return lax.dynamic_slice_in_dim(whole, lax.axis_index("opt") * width, width, along)


def exchange(value, axis, bit):
    count = lax.axis_size(axis)
    return lax.ppermute(value, axis, [(i, i ^ (1 << bit)) for i in range(count)])


def side_of(axis, bit):
    return (lax.axis_index(axis) >> bit) & 1


def fold(value, axis, bit, dim):
    half = value.shape[dim] // 2
    side = side_of(axis, bit)
    sent = lax.dynamic_slice_in_dim(value, (1 - side) * half, half, dim)
    kept = lax.dynamic_slice_in_dim(value, side * half, half, dim)
    return kept + exchange(sent, axis, bit)


def unfold(value, axis, bit, dim):
    other = exchange(value, axis, bit)
    first = jnp.where(side_of(axis, bit) == 0, value, other)
    second = jnp.where(side_of(axis, bit) == 0, other, value)
    return jnp.concatenate([first, second], axis=dim)


AXES = ("dp", "opt")


def partner_index(bits, offset):
    across = lax.axis_size("opt")
    flip = 0
    for place, (axis, bit) in enumerate(reversed(bits)):
        if (offset >> place) & 1:
            flip ^= (1 << bit) * (across if axis == "dp" else 1)
    return [(i, i ^ flip) for i in range(lax.axis_size("dp") * across)]


def own_index(bits):
    index = 0
    for axis, bit in bits:
        index = 2 * index + side_of(axis, bit)
    return index


def send_parts(parts, bits):
    own = own_index(bits)
    take = lambda offset: lax.dynamic_index_in_dim(parts, own ^ offset, 0, keepdims=False)
    return take(0), [take(offset) for offset in range(1, 1 << len(bits))]


def add_parts(kept, sent, bits):
    total = kept.astype(jnp.float32)
    for offset, part in enumerate(sent, 1):
        total = total + lax.ppermute(part, AXES, partner_index(bits, offset)).astype(jnp.float32)
    return total.astype(kept.dtype)


def gather_parts(piece, bits):
    pieces = [piece] + [
        lax.ppermute(piece, AXES, partner_index(bits, offset)) for offset in range(1, 1 << len(bits))
    ]
    own = own_index(bits)
    places = []
    for place in range(1 << len(bits)):
        value = pieces[0]
        for offset in range(1, 1 << len(bits)):
            value = jnp.where(own ^ offset == place, pieces[offset], value)
        places.append(value)
    return jnp.stack(places)


def dp_groups():
    bits = [("dp", bit) for bit in range(1, (lax.axis_size("dp") - 1).bit_length())]
    return [bits[i : i + 2] for i in range(0, len(bits), 2)]


def scatter_dp(piece, bits):
    parts = piece.reshape(piece.shape[0], 1 << len(bits), -1, piece.shape[-1]).swapaxes(0, 1)
    return add_parts(*send_parts(parts, bits), bits)


def gather_dp(piece, bits):
    parts = gather_parts(piece, bits).swapaxes(0, 1)
    return parts.reshape(piece.shape[0], -1, piece.shape[-1])


def tie(value, others):
    return lax.optimization_barrier((value, others))


def sum_everywhere(value):
    for axis in ("opt", "dp"):
        for bit in range((lax.axis_size(axis) - 1).bit_length()):
            value = value + exchange(value, axis, bit)
    return value


def fetch_shards(shard):
    across = exchange(shard, "opt", 1)
    return [shard, exchange(shard, "opt", 0), across, exchange(across, "opt", 0)]


def in_order(pieces):
    core, far = side_of("opt", 0) == 0, side_of("opt", 1) == 0
    near = [jnp.where(core, pieces[0], pieces[1]), jnp.where(core, pieces[1], pieces[0])]
    other = [jnp.where(core, pieces[2], pieces[3]), jnp.where(core, pieces[3], pieces[2])]
    low = [jnp.where(far, n, o) for n, o in zip(near, other)]
    high = [jnp.where(far, o, n) for n, o in zip(near, other)]
    return jnp.concatenate(low + high, axis=0)


COLUMN_BLOCK = 384
SHARD = PROJ // 4
SHARD_LANES = 896


def project_kernel(
    place_ref, tokens_ref, gain_ref, own_ref, core_ref, across_ref, last_ref,
    proj_ref, hidden_ref, weight_out_ref, scale_ref,
    shards_ref, weight_ref, normed_ref, sems,
):
    step = pl.program_id(0)

    @pl.when(step == 0)
    def start():
        copies = [
            pltpu.make_async_copy(ref, shards_ref.at[place_ref[0] ^ place], sems.at[place])
            for place, ref in enumerate((own_ref, core_ref, across_ref, last_ref))
        ]
        for copy in copies:
            copy.start()
        inflow = tokens_ref[...].astype(jnp.float32)
        scale = lax.rsqrt(jnp.mean(inflow * inflow, axis=1, keepdims=True) + EPSILON)
        normed_ref[...] = (inflow * scale * gain_ref[...]).astype(jnp.bfloat16)
        hidden_ref[...] = normed_ref[...]
        scale_ref[...] = jnp.broadcast_to(scale, scale_ref.shape)
        for copy in copies:
            copy.wait()
        weight_ref[:, PROJ - PROJ % 128 :] = jnp.zeros((D, PADDED - PROJ + PROJ % 128), jnp.bfloat16)
        for place in range(4):
            weight_ref[:, place * SHARD : (place + 1) * SHARD] = shards_ref[place, :, :SHARD]

    block = weight_ref[:, pl.ds(pl.multiple_of(step * COLUMN_BLOCK, 128), COLUMN_BLOCK)]
    weight_out_ref[...] = block
    proj_ref[...] = dot32(normed_ref[...], block).astype(jnp.bfloat16)


def project(tokens, gain_vec, pieces):
    length = tokens.shape[0]
    bf16 = jnp.bfloat16
    hold = pl.BlockSpec(memory_space=pl.ANY)
    return pl.pallas_call(
        project_kernel,
        grid=(PADDED // COLUMN_BLOCK,),
        in_specs=[pl.BlockSpec(memory_space=pltpu.SMEM), fixed_block(length, D), fixed_block(1, D)] + [hold] * 4,
        out_specs=[
            pl.BlockSpec((length, COLUMN_BLOCK), lambda i: (0, i)),
            fixed_block(length, D),
            pl.BlockSpec((D, COLUMN_BLOCK), lambda i: (0, i)),
            fixed_block(length, 128),
        ],
        out_shape=[
            jax.ShapeDtypeStruct((length, PADDED), bf16), jax.ShapeDtypeStruct((length, D), bf16),
            jax.ShapeDtypeStruct((D, PADDED), bf16), jax.ShapeDtypeStruct((length, 128), jnp.float32),
        ],
        scratch_shapes=[
            pltpu.VMEM((4, D, SHARD_LANES), bf16), pltpu.VMEM((D, PADDED), bf16), pltpu.VMEM((length, D), bf16),
            pltpu.SemaphoreType.DMA((4,)),
        ],
        compiler_params=pltpu.CompilerParams(
            dimension_semantics=("arbitrary",), vmem_limit_bytes=VMEM_LIMIT
        ),
        cost_estimate=pl.CostEstimate(
            flops=2 * length * D * PADDED, bytes_accessed=22 * 10**6, transcendentals=0
        ),
        name="project",
    )(lax.axis_index("opt").astype(jnp.int32)[None], tokens, gain_vec[None, :], *pieces)


def weight_grad_kernel(place_ref, hidden_ref, gate_ref, conv_ref, kept_ref, sent_ref, turned_ref, whole_ref):
    step = pl.program_id(0)

    @pl.when(step == 0)
    def start():
        turned_ref[...] = hidden_ref[...].astype(jnp.float32).T.astype(jnp.bfloat16)

    for shard in range(4):
        first = (shard * SHARD) // 128 * 128
        last = min(-(-((shard + 1) * SHARD) // 128) * 128, PADDED)

        @pl.when(step == shard)
        def work():
            done = -(-(shard * SHARD) // 128) * 128
            for ref, begin, end in ((gate_ref, 0, D_INNER), (conv_ref, D_INNER, PADDED)):
                low, high = max(begin, done), min(end, last)
                if low < high:
                    whole_ref[:, low:high] = dot32(turned_ref[...], ref[:, low - begin : high - begin]).astype(jnp.bfloat16)
            block = whole_ref[:, shard * SHARD : (shard + 1) * SHARD]
            block = jnp.concatenate([block, jnp.zeros((D, SHARD_LANES - SHARD), jnp.bfloat16)], axis=1)

            @pl.when(place_ref[0] == shard % 2)
            def keep():
                kept_ref[0] = block

            @pl.when(place_ref[0] != shard % 2)
            def send():
                sent_ref[0] = block


def weight_grad(hidden, gate, conv):
    length = hidden.shape[0]
    bf16 = jnp.bfloat16
    shards = jax.ShapeDtypeStruct((2, D, SHARD_LANES), bf16)
    return pl.pallas_call(
        weight_grad_kernel,
        grid=(4,),
        in_specs=[
            pl.BlockSpec(memory_space=pltpu.SMEM), fixed_block(length, D), fixed_block(length, D_INNER),
            fixed_block(length, PADDED - D_INNER),
        ],
        out_specs=[pl.BlockSpec((1, D, SHARD_LANES), lambda i: (i // 2, 0, 0))] * 2,
        out_shape=[shards, shards],
        scratch_shapes=[pltpu.VMEM((D, length), bf16), pltpu.VMEM((D, PADDED), bf16)],
        compiler_params=pltpu.CompilerParams(
            dimension_semantics=("arbitrary",), vmem_limit_bytes=VMEM_LIMIT
        ),
        cost_estimate=pl.CostEstimate(
            flops=2 * length * D * PADDED, bytes_accessed=14 * 10**6, transcendentals=0
        ),
        name="weight_grad",
    )(side_of("opt", 0).astype(jnp.int32)[None], hidden, gate, conv)


def on_device(tokens, cotangent, w_in, w_out, small, mom_in, mom_out, adam_m, adam_v):
    bf16 = jnp.bfloat16
    small_b = in_order(fetch_shards(small.astype(bf16)))
    pieces = fetch_shards(jnp.pad(w_in.astype(bf16), ((0, 0), (0, SHARD_LANES - SHARD))))
    own_out, pieces[2] = lax.optimization_barrier((w_out.astype(bf16), pieces[2]))
    w_out_b = in_order(fetch_shards(own_out))
    params = small_b.astype(jnp.float32)
    gain_vec = params[:D]
    sections = [D, D + D_INNER, D + D_INNER + CONV * CONV_CH]
    sections += [sections[-1] + CONV_CH + place * HEADS for place in range(3)]
    gain_vec, gate_gain, taps, conv_bias, dt_bias, a_log, skip_gain = jnp.split(params, sections)
    taps = taps.reshape(CONV, CONV_CH)
    rate = -jnp.exp(a_log)
    skip_wide = jnp.repeat(skip_gain, HEAD_CHANNELS)[None, :]
    spread, reduce_mat = head_matrices()
    fixed = (skip_wide, pad_heads(dt_bias), pad_heads(rate), spread, reduce_mat)
    inflow = tokens.astype(jnp.float32)
    projected, hidden, w_pad, scale = project(tokens, gain_vec, pieces)
    grad_mixed = dot_nt(cotangent, w_out_b).astype(jnp.bfloat16)
    mixed, active, slope, grad_scan, grad_gate, states, inner, gain_acc, skip_acc = mixer_forward(
        projected, grad_mixed, taps, conv_bias[None, :], gate_gain[None, :], *fixed
    )
    square = [("opt", 1), ("dp", 0)]
    grad_w_out = dot_tn(mixed, cotangent).astype(bf16).reshape(2, 2, -1, D)
    out_pair = fold(grad_w_out, "opt", 0, 1)
    block = (inflow + dot32(mixed, w_out_b)).astype(bf16)
    out_kept, out_sent = send_parts(out_pair.reshape(4, -1, D), square)
    grad_scan, (out_sent, block) = tie(grad_scan, (out_sent, block))
    grad_conv, taps_acc, bias_acc, dt_acc, rate_acc = mixer_backward(
        projected, active, slope, grad_scan, states, inner, taps, *fixed
    )
    out_piece = add_parts(out_kept, out_sent, square)[None]
    groups = dp_groups()
    parts = out_piece.reshape(1 << len(groups[0]), -1, D)
    out_kept, out_sent = send_parts(parts, groups[0])
    grad_conv, out_sent = tie(grad_conv, out_sent)
    kept, sent = weight_grad(hidden, grad_gate, grad_conv)
    out_piece = add_parts(out_kept, out_sent, groups[0])[None]
    for bits in groups[1:]:
        out_piece = scatter_dp(out_piece, bits)
    for bits in reversed(groups):
        out_piece = gather_dp(out_piece, bits)
    owned_out = unfold(out_piece[0], "dp", 0, 0).astype(jnp.float32)

    pair_in = kept + exchange(sent, "opt", 0)
    rows = D // 2
    one = fold(pair_in[:, :rows], "opt", 1, 0)[0]
    two = fold(pair_in[:, rows:], "dp", 0, 1)
    grad_gate, (one, two) = tie(grad_gate, (one, two))
    grad_hidden = dot_nt(grad_gate, w_pad[:, :D_INNER])
    one = fold(one, "dp", 0, 0)
    two = fold(two, "opt", 1, 0)[0]
    in_piece = jnp.stack([one, two])
    for bits in groups:
        in_piece = scatter_dp(in_piece, bits)
    for bits in reversed(groups):
        in_piece = gather_dp(in_piece, bits)
    in_piece = unfold(in_piece, "dp", 0, 1)
    owned_in = in_piece.reshape(D, SHARD_LANES)[:, :SHARD].astype(jnp.float32)
    grad_hidden = grad_hidden + dot_nt(grad_conv, w_pad[:, D_INNER:])
    normal = inflow * scale[:, :1]
    grad_gain = jnp.sum(normal * grad_hidden, axis=0)
    grad_normal = grad_hidden * gain_vec
    grad_tokens = cotangent.astype(jnp.float32) + scale[:, :1] * (
        grad_normal - normal * jnp.mean(grad_normal * normal, axis=1, keepdims=True)
    )
    grad_small = jnp.concatenate([
        grad_gain,
        gain_acc.sum(0),
        taps_acc.sum(1).reshape(-1),
        bias_acc.sum(0),
        dt_acc.sum(0)[:HEADS],
        rate_acc.sum(0)[:HEADS] * rate,
        skip_acc.sum(0).reshape(HEADS, HEAD_CHANNELS).sum(1),
    ])
    owned_small = own_slice(sum_everywhere(grad_small), small.shape[0], 0)
    adam_m_new = BETA_ONE * adam_m + (1.0 - BETA_ONE) * owned_small
    adam_v_new = BETA_TWO * adam_v + (1.0 - BETA_TWO) * owned_small * owned_small
    small_new = small * (1.0 - ADAM_RATE * DECAY) - ADAM_RATE * (
        adam_m_new / (1.0 - BETA_ONE**STEP)
    ) / (jnp.sqrt(adam_v_new / (1.0 - BETA_TWO**STEP)) + ADAM_EPS)
    mom_in_new = MOMENTUM * mom_in + owned_in
    push_in = owned_in + MOMENTUM * mom_in_new
    mom_out_new = MOMENTUM * mom_out + owned_out
    push_out = owned_out + MOMENTUM * mom_out_new
    pushed_in = push_in.astype(jnp.bfloat16)
    pushed_out = push_out.astype(jnp.bfloat16)
    gram_out = gram_sum(pushed_out, False)
    halfway = newton_call((gram_out,), ((D, D), (D, D), (1, 1)), False, 0, 2)
    (w_out_new,) = newton_call((*halfway, push_out, w_out), (w_out.shape,), False, 2, 5)
    pushed_in, w_out_new = tie(pushed_in, w_out_new)
    gram_in = gram_sum(pushed_in, True)
    (w_in_new,) = newton_call((gram_in, push_in, w_in), (w_in.shape,), True, 0, 5)
    return (
        block,
        grad_tokens,
        owned_in,
        owned_out,
        owned_small,
        mom_in_new,
        mom_out_new,
        w_in_new,
        w_out_new,
        small_new,
        adam_m_new,
        adam_v_new,
    )


def solution(mesh):
    in_specs = (
        P(("dp", "opt"), None),
        P(("dp", "opt"), None),
        P(None, "opt"),
        P("opt", None),
        P("opt"),
        P(None, "opt"),
        P("opt", None),
        P("opt"),
        P("opt"),
    )
    out_specs = (
        P(("dp", "opt"), None),
        P(("dp", "opt"), None),
        P(None, "opt"),
        P("opt", None),
        P("opt"),
        P(None, "opt"),
        P("opt", None),
        P(None, "opt"),
        P("opt", None),
        P("opt"),
        P("opt"),
        P("opt"),
    )
    return jax.shard_map(
        on_device, mesh=mesh, in_specs=in_specs, out_specs=out_specs, check_vma=False
    )
```

```python
import functools
import math

import jax
import jax.numpy as jnp
from jax import lax
from jax.experimental import pallas as pl
from jax.experimental.pallas import tpu as pltpu
from jax.sharding import PartitionSpec as P

D = 768
HEADS = 24
HEAD_CHANNELS = 64
STATE = 128
CONV = 4
SEQ_LEN = 1024
STEP = 10
D_INNER = 1536
CONV_CH = 1792
PROJ = 3352


EPSILON = 1e-05
COEF_A = 3.4445
COEF_B = -4.775
COEF_C = 2.0315
MOMENTUM = 0.95
MUON_RATE = 0.5
DECAY = 0.01
ADAM_RATE = 0.2
BETA_ONE = 0.9
BETA_TWO = 0.95
ADAM_EPS = 1e-08


SPAN = 128
CHUNKS = SEQ_LEN // SPAN
PAIRS = HEADS // 2
WIDTH = 2 * HEAD_CHANNELS
CONV_END = D_INNER + CONV_CH
PADDED = CONV_END + 128
TAIL = 8
VMEM_LIMIT = 56 * 1024 * 1024


def dot32(left, right):
    return jnp.dot(left, right, preferred_element_type=jnp.float32)


def dot_nt(left, right):
    return lax.dot_general(left, right, (((1,), (1,)), ((), ())), preferred_element_type=jnp.float32)


def dot_tn(left, right):
    return lax.dot_general(left, right, (((0,), (0,)), ((), ())), preferred_element_type=jnp.float32)


def halves(value):
    high = value.astype(jnp.bfloat16)
    return high, (value - high.astype(jnp.float32)).astype(jnp.bfloat16)


def sigmoid(value):
    return 0.5 * jnp.tanh(0.5 * value) + 0.5


def softplus(value):
    return jnp.maximum(value, 0.0) + jnp.log1p(jnp.exp(-jnp.abs(value)))


def fold_rows(value):
    return jnp.sum(value.reshape(value.shape[0] // 8, 8, value.shape[1]), axis=0)


def triangle(lower):
    rows = lax.broadcasted_iota(jnp.int32, (SPAN, SPAN), 0)
    cols = lax.broadcasted_iota(jnp.int32, (SPAN, SPAN), 1)
    return rows >= cols if lower else rows <= cols


def running_sum(mask, value):
    ones = jnp.where(mask, 1.0, 0.0).astype(jnp.bfloat16)
    high, rest = halves(value)
    low = (value - high.astype(jnp.float32) - rest.astype(jnp.float32)).astype(jnp.bfloat16)
    return dot32(ones, high) + (dot32(ones, rest) + dot32(ones, low))


def head_sums(value, reduce_mat):
    high, low = halves(value)
    return dot32(high, reduce_mat) + dot32(low, reduce_mat)


def step_factors(raw, dt_bias, rate, spread):
    step_size = softplus(raw + dt_bias)
    log_decay = running_sum(triangle(True), step_size * rate)
    last = log_decay[SPAN - 1 : SPAN, :]
    stacked = jnp.concatenate([step_size, jnp.exp(log_decay), jnp.exp(last - log_decay)], axis=0)
    high, low = halves(stacked)
    wide = dot32(jnp.concatenate([high, low], axis=1), spread)
    return step_size, log_decay, wide[:SPAN], wide[SPAN : 2 * SPAN], wide[2 * SPAN :]


def split_pair(value, first):
    return jnp.concatenate(
        [jnp.where(first, value, 0.0), jnp.where(first, 0.0, value)], axis=0
    ).astype(jnp.bfloat16)


def forward_kernel(
    proj_ref, back_ref, taps_ref, conv_bias_ref, gate_gain_ref, skip_ref, dt_bias_ref, rate_ref, spread_ref, reduce_ref,
    mixed_ref, active_ref, slope_ref, grad_scan_ref, grad_gate_ref, states_ref, inner_ref, gain_acc_ref, skip_acc_ref,
    window_ref, state_ref,
):
    f32, bf16 = jnp.float32, jnp.bfloat16

    @pl.when(pl.program_id(0) == 0)
    def start():
        window_ref[0:TAIL, :] = jnp.zeros((TAIL, CONV_CH), f32)
        state_ref[...] = jnp.zeros((STATE, D_INNER), f32)
        gain_acc_ref[...] = jnp.zeros((8, D_INNER), f32)
        skip_acc_ref[...] = jnp.zeros((8, D_INNER), f32)

    window_ref[TAIL:, :] = proj_ref[:, D_INNER:CONV_END].astype(f32)
    conv_out = conv_bias_ref[...]
    for tap in range(CONV):
        start_row = TAIL - (CONV - 1) + tap
        conv_out = conv_out + taps_ref[tap : tap + 1, :] * window_ref[start_row : start_row + SPAN, :]
    window_ref[0:TAIL, :] = window_ref[SPAN:, :]
    part = sigmoid(conv_out)
    silu = conv_out * part
    active_ref[...] = silu.astype(bf16)
    slope_ref[...] = (part + silu * (1.0 - part)).astype(bf16)

    values = active_ref[:, :D_INNER].astype(f32)
    input_b = active_ref[:, D_INNER : D_INNER + STATE]
    output_c = active_ref[:, D_INNER + STATE :]
    step_size, log_decay, step_wide, decay_wide, end_wide = step_factors(
        proj_ref[:, CONV_END:].astype(f32), dt_bias_ref[...], rate_ref[...], spread_ref[...]
    )
    decay_rows = log_decay.T
    moved = step_wide * values
    state = state_ref[...]
    state_low = state.astype(bf16)
    states_ref[0] = state_low
    state_ref[...] = state * decay_wide[SPAN - 1 : SPAN, :] + dot_tn(input_b, (moved * end_wide).astype(bf16))
    scores = dot_nt(output_c, input_b)
    causal = triangle(True)
    first = lax.broadcasted_iota(jnp.int32, (SPAN, WIDTH), 1) < HEAD_CHANNELS
    pieces = []
    for pair in range(PAIRS):
        lanes = slice(pair * WIDTH, (pair + 1) * WIDTH)
        mixing = []
        for head in (2 * pair, 2 * pair + 1):
            differ = log_decay[:, head : head + 1] - decay_rows[head : head + 1, :]
            mixing.append((scores * jnp.exp(jnp.where(causal, differ, -1e30))).astype(bf16))
        pieces.append(dot32(jnp.concatenate(mixing, axis=1), split_pair(moved[:, lanes], first)))
    inner = jnp.concatenate(pieces, axis=1) + dot32(output_c, state_low) * decay_wide
    scanned = inner + skip_ref[...] * values

    gate_in = proj_ref[:, :D_INNER].astype(f32)
    part = sigmoid(gate_in)
    gate = gate_in * part
    gated = scanned * gate
    scale = lax.rsqrt(jnp.mean(gated * gated, axis=1, keepdims=True) + EPSILON)
    normal = gated * scale
    mixed_ref[...] = (normal * gate_gain_ref[...]).astype(bf16)
    back = back_ref[...].astype(f32)
    gain_acc_ref[...] += fold_rows(back * normal)
    back = back * gate_gain_ref[...]
    grad_gated = scale * (back - normal * jnp.mean(back * normal, axis=1, keepdims=True))
    grad_gate_ref[...] = (grad_gated * scanned * (part + gate * (1.0 - part))).astype(bf16)
    grad_scan_low = (grad_gated * gate).astype(bf16)
    grad_scan_ref[...] = grad_scan_low
    grad_scan = grad_scan_low.astype(f32)
    skip_acc_ref[...] += fold_rows(grad_scan * values)
    inner_ref[...] = head_sums(grad_scan * inner, reduce_ref[...])


def backward_kernel(
    proj_ref, active_ref, slope_ref, grad_scan_ref, states_ref, inner_ref, taps_ref, skip_ref, dt_bias_ref, rate_ref,
    spread_ref, reduce_ref,
    grad_ref, taps_acc_ref, bias_acc_ref, dt_acc_ref, rate_acc_ref,
    window_ref, costate_ref,
):
    f32, bf16 = jnp.float32, jnp.bfloat16

    @pl.when(pl.program_id(0) == 0)
    def start():
        window_ref[SPAN:, :] = jnp.zeros((TAIL, CONV_CH), f32)
        costate_ref[...] = jnp.zeros((STATE, D_INNER), f32)
        taps_acc_ref[...] = jnp.zeros((CONV, 8, CONV_CH), f32)
        bias_acc_ref[...] = jnp.zeros((8, CONV_CH), f32)
        dt_acc_ref[...] = jnp.zeros((8, 128), f32)
        rate_acc_ref[...] = jnp.zeros((8, 128), f32)

    values = active_ref[:, :D_INNER].astype(f32)
    input_b = active_ref[:, D_INNER : D_INNER + STATE]
    output_c = active_ref[:, D_INNER + STATE :]
    raw = proj_ref[:, CONV_END:].astype(f32)
    rate = rate_ref[...]
    step_size, log_decay, step_wide, decay_wide, end_wide = step_factors(raw, dt_bias_ref[...], rate, spread_ref[...])
    decay_rows = log_decay.T
    moved = step_wide * values
    grad_scan_low = grad_scan_ref[...]
    grad_scan = grad_scan_low.astype(f32)
    scores = dot_nt(input_b, output_c)
    causal = triangle(False)
    first = lax.broadcasted_iota(jnp.int32, (SPAN, WIDTH), 1) < HEAD_CHANNELS
    grad_scores = jnp.zeros((SPAN, SPAN), f32)
    pieces = []
    for pair in range(PAIRS):
        lanes = slice(pair * WIDTH, (pair + 1) * WIDTH)
        moved_low = moved[:, lanes].astype(bf16)
        grad_pair = split_pair(grad_scan[:, lanes], first)
        grad_mixing = dot_nt(moved_low, grad_pair)
        mixing = []
        for place, head in enumerate((2 * pair, 2 * pair + 1)):
            differ = decay_rows[head : head + 1, :] - log_decay[:, head : head + 1]
            decay = jnp.exp(jnp.where(causal, differ, -1e30))
            mixing.append((scores * decay).astype(bf16))
            grad_scores = grad_scores + decay * grad_mixing[:, place * SPAN : (place + 1) * SPAN]
        pieces.append(dot32(jnp.concatenate(mixing, axis=1), grad_pair))
    grad_inner = jnp.concatenate(pieces, axis=1)

    costate = costate_ref[...]
    costate_low = costate.astype(bf16)
    states_low = states_ref[0]
    last_wide = decay_wide[SPAN - 1 : SPAN, :]
    kept = fold_rows(costate * states_low.astype(f32)) * last_wide
    grad_cross = dot32(input_b, costate_low) * end_wide
    grad_decayed = (grad_scan * decay_wide).astype(bf16)
    grad_scores_low = grad_scores.astype(bf16)
    grad_b = dot32(grad_scores_low, output_c) + dot_nt((moved * end_wide).astype(bf16), costate_low)
    grad_c = dot_tn(grad_scores_low, input_b) + dot_nt(grad_decayed, states_low)
    costate_ref[...] = costate * last_wide + dot_tn(output_c, grad_decayed)

    moved_round = moved.astype(bf16).astype(f32)
    grad_moved = grad_inner + grad_cross
    reduce_mat = reduce_ref[...]
    own = head_sums(moved_round * grad_inner, reduce_mat)
    crossing = dot32((moved * grad_cross).astype(bf16), reduce_mat)
    grad_step = dot32((values * grad_moved).astype(bf16), reduce_mat)
    keeping = jnp.sum(head_sums(kept, reduce_mat), axis=0, keepdims=True)
    grad_log = (
        running_sum(triangle(False), inner_ref[...] - own)
        + running_sum(triangle(True), crossing) - crossing
        + keeping
    )
    grad_raw = (grad_step + rate * grad_log) * sigmoid(raw + dt_bias_ref[...])
    rate_acc_ref[...] += fold_rows(step_size * grad_log)
    dt_acc_ref[...] += fold_rows(grad_raw)
    grad_ref[:, CONV_CH:] = grad_raw.astype(bf16)

    grad_values = step_wide * grad_moved + skip_ref[...] * grad_scan
    grad_active = jnp.concatenate([grad_values, grad_b, grad_c], axis=1)
    grad_conv = grad_active * slope_ref[...].astype(f32)
    bias_acc_ref[...] += fold_rows(grad_conv)
    window_ref[0:SPAN, :] = grad_conv
    conv_in = proj_ref[:, D_INNER:CONV_END].astype(f32)
    grad_in = jnp.zeros((SPAN, CONV_CH), f32)
    for tap in range(CONV):
        start_row = CONV - 1 - tap
        shifted = window_ref[start_row : start_row + SPAN, :]
        grad_in = grad_in + taps_ref[tap : tap + 1, :] * shifted
        taps_acc_ref[tap] += fold_rows(conv_in * shifted)
    grad_ref[:, :CONV_CH] = grad_in.astype(bf16)
    window_ref[SPAN:, :] = window_ref[0:TAIL, :]


def head_matrices():
    spread = jnp.pad(jnp.repeat(jnp.eye(HEADS, dtype=jnp.bfloat16), HEAD_CHANNELS, axis=1), ((0, 128 - HEADS), (0, 0)))
    return jnp.concatenate([spread, spread], axis=0), spread.T


def row_block(width, order):
    return pl.BlockSpec((SPAN, width), lambda i: (order(i), 0))


def fixed_block(*shape):
    return pl.BlockSpec(shape, lambda i: (0,) * len(shape))


def state_block(order):
    return pl.BlockSpec((1, STATE, D_INNER), lambda i: (order(i), 0, 0))


def pad_heads(vector):
    return jnp.pad(vector, (0, 128 - HEADS))[None, :]


def mixer_forward(projected, back, taps, conv_bias, gate_gain, skip_wide, dt_bias, rate, spread, reduce_mat):
    f32, bf16 = jnp.float32, jnp.bfloat16
    order = lambda i: i
    rows = lambda width, kind: jax.ShapeDtypeStruct((SEQ_LEN, width), kind)
    return pl.pallas_call(
        forward_kernel,
        grid=(CHUNKS,),
        in_specs=[
            row_block(PADDED, order), row_block(D_INNER, order), fixed_block(CONV, CONV_CH), fixed_block(1, CONV_CH),
            fixed_block(1, D_INNER), fixed_block(1, D_INNER), fixed_block(1, 128), fixed_block(1, 128),
            fixed_block(256, D_INNER), fixed_block(D_INNER, 128),
        ],
        out_specs=[
            row_block(D_INNER, order), row_block(CONV_CH, order), row_block(CONV_CH, order), row_block(D_INNER, order),
            row_block(D_INNER, order), state_block(order), row_block(128, order), fixed_block(8, D_INNER),
            fixed_block(8, D_INNER),
        ],
        out_shape=[
            rows(D_INNER, bf16), rows(CONV_CH, bf16), rows(CONV_CH, bf16), rows(D_INNER, bf16), rows(D_INNER, bf16),
            jax.ShapeDtypeStruct((CHUNKS, STATE, D_INNER), bf16), rows(128, f32),
            jax.ShapeDtypeStruct((8, D_INNER), f32), jax.ShapeDtypeStruct((8, D_INNER), f32),
        ],
        scratch_shapes=[pltpu.VMEM((SPAN + TAIL, CONV_CH), f32), pltpu.VMEM((STATE, D_INNER), f32)],
        compiler_params=pltpu.CompilerParams(
            dimension_semantics=("arbitrary",), vmem_limit_bytes=VMEM_LIMIT
        ),
        cost_estimate=pl.CostEstimate(flops=8 * 10**9, bytes_accessed=32 * 10**6, transcendentals=10**7),
        name="mixer_forward",
    )(projected, back, taps, conv_bias, gate_gain, skip_wide, dt_bias, rate, spread, reduce_mat)


def mixer_backward(projected, active, slope, grad_scan, states, inner, taps, skip_wide, dt_bias, rate, spread, reduce_mat):
    f32, bf16 = jnp.float32, jnp.bfloat16
    order = lambda i: CHUNKS - 1 - i
    return pl.pallas_call(
        backward_kernel,
        grid=(CHUNKS,),
        in_specs=[
            row_block(PADDED, order), row_block(CONV_CH, order), row_block(CONV_CH, order), row_block(D_INNER, order),
            state_block(order), row_block(128, order), fixed_block(CONV, CONV_CH), fixed_block(1, D_INNER),
            fixed_block(1, 128), fixed_block(1, 128), fixed_block(256, D_INNER), fixed_block(D_INNER, 128),
        ],
        out_specs=[
            row_block(CONV_CH + 128, order), fixed_block(CONV, 8, CONV_CH), fixed_block(8, CONV_CH),
            fixed_block(8, 128), fixed_block(8, 128),
        ],
        out_shape=[
            jax.ShapeDtypeStruct((SEQ_LEN, CONV_CH + 128), bf16), jax.ShapeDtypeStruct((CONV, 8, CONV_CH), f32),
            jax.ShapeDtypeStruct((8, CONV_CH), f32), jax.ShapeDtypeStruct((8, 128), f32),
            jax.ShapeDtypeStruct((8, 128), f32),
        ],
        scratch_shapes=[pltpu.VMEM((SPAN + TAIL, CONV_CH), f32), pltpu.VMEM((STATE, D_INNER), f32)],
        compiler_params=pltpu.CompilerParams(
            dimension_semantics=("arbitrary",), vmem_limit_bytes=VMEM_LIMIT
        ),
        cost_estimate=pl.CostEstimate(flops=12 * 10**9, bytes_accessed=32 * 10**6, transcendentals=10**7),
        name="mixer_backward",
    )(projected, active, slope, grad_scan, states, inner, taps, skip_wide, dt_bias, rate, spread, reduce_mat)


ROW_BLOCK = 256
UPPER = [(0, 0), (0, 1), (0, 2), (1, 1), (1, 2), (2, 2)]


def gram_kernel(place_ref, push_ref, kept_ref, sent_ref):
    for place, (row, col) in enumerate(UPPER):
        rows = slice(row * ROW_BLOCK, (row + 1) * ROW_BLOCK)
        cols = slice(col * ROW_BLOCK, (col + 1) * ROW_BLOCK)
        tile = dot_tn(push_ref[:, rows], push_ref[:, cols])

        @pl.when(place_ref[0] == place // 3)
        def keep():
            kept_ref[place % 3] = tile

        @pl.when(place_ref[0] != place // 3)
        def send():
            sent_ref[place % 3] = tile


def gram_parts(push, name):
    tiles = jax.ShapeDtypeStruct((3, ROW_BLOCK, ROW_BLOCK), jnp.float32)
    hold = pl.BlockSpec(memory_space=pltpu.VMEM)
    return pl.pallas_call(
        gram_kernel,
        in_specs=[pl.BlockSpec(memory_space=pltpu.SMEM), hold],
        out_shape=[tiles, tiles],
        compiler_params=pltpu.CompilerParams(vmem_limit_bytes=VMEM_LIMIT),
        cost_estimate=pl.CostEstimate(
            flops=2 * D * push.size, bytes_accessed=2 * push.size, transcendentals=0
        ),
        name=name,
    )(core_place(), push)


def core_place():
    return side_of("opt", 0).astype(jnp.int32)[None]


def newton_kernel(transposed, rate, begin, end, place_ref, *refs):
    if begin == 0:
        (own_ref, other_ref), refs = refs[:2], refs[2:]
    else:
        (a_in_ref, r_in_ref, norm_ref), refs = refs[:3], refs[3:]
    if end == 5:
        (push_ref, weight_ref, new_ref), refs = refs[:3], refs[3:]
    else:
        (a_out_ref, r_out_ref, norm_out_ref), refs = refs[:3], refs[3:]
    a_ref, p_ref, t_ref, r_ref, e_ref, k_ref, f_ref = refs
    f32, bf16 = jnp.float32, jnp.bfloat16
    blocks = [slice(i, i + ROW_BLOCK) for i in range(0, D, ROW_BLOCK)]
    size = 1.0 / D
    rows = lax.broadcasted_iota(jnp.int32, (ROW_BLOCK, ROW_BLOCK), 0)
    cols = lax.broadcasted_iota(jnp.int32, (ROW_BLOCK, ROW_BLOCK), 1)
    eye = rows == cols

    def tile_trace(tile):
        kept = jnp.where(eye, tile, 0.0)
        return jnp.sum(jnp.sum(kept, axis=0, keepdims=True), axis=1, keepdims=True)

    def trace_of(ref):
        return sum(tile_trace(ref[block, block]) for block in blocks)

    def shifted(value, row, amount):
        tiles = [value[:, block] for block in blocks]
        tiles[row] = tiles[row] - jnp.where(eye, amount, 0.0)
        return jnp.concatenate(tiles, axis=1)

    def rest_of(target_ref, source_ref, amount):
        for row, block in enumerate(blocks):
            target_ref[block, :] = shifted(source_ref[block, :], row, amount).astype(bf16)

    if begin == 0:
        core = place_ref[0] == 0
        for place, (row, col) in enumerate(UPPER):
            own, other = own_ref[place % 3], other_ref[place % 3]
            tile = jnp.where(core, own, other) if place < 3 else jnp.where(core, other, own)
            a_ref[blocks[row], blocks[col]] = tile
            if row != col:
                a_ref[blocks[col], blocks[row]] = tile.T
        total = trace_of(a_ref)
        norm = 1.0 / (jnp.sqrt(total) + 1e-07)
        scale = norm * norm
        for block in blocks:
            a_ref[block, :] = a_ref[block, :] * scale
        mean = total * scale * size
    else:
        norm = norm_ref[...]
        a_ref[...] = a_in_ref[...]
        r_ref[...] = r_in_ref[...]
        mean = trace_of(a_ref) * size
        r_mean = trace_of(r_ref) * size
    for sweep in range(begin, end):
        rest_of(e_ref, a_ref, mean)
        slope = COEF_B + 2.0 * COEF_C * mean
        for row, block in enumerate(blocks):
            poly = slope * a_ref[block, :] + COEF_C * dot32(e_ref[block, :], e_ref[...])
            p_ref[block, :] = shifted(poly, row, COEF_C * mean * mean)
        shift = trace_of(p_ref) * size
        lead = COEF_A + shift
        rest_of(k_ref, p_ref, shift)
        if sweep == 0:
            for row, block in enumerate(blocks):
                r_ref[block, :] = shifted(p_ref[block, :], row, -COEF_A)
            r_mean = lead
        else:
            rest_of(f_ref, r_ref, r_mean)
            for block in blocks:
                r_ref[block, :] = (
                    lead * r_ref[block, :]
                    + r_mean * k_ref[block, :].astype(f32)
                    + dot32(k_ref[block, :], f_ref[...])
                )
            r_mean = trace_of(r_ref) * size
        if sweep < 4:
            for block in blocks:
                t_ref[block, :] = (
                    lead * a_ref[block, :] + mean * k_ref[block, :].astype(f32) + dot32(k_ref[block, :], e_ref[...])
                )
            t_mean = trace_of(t_ref) * size
            rest_of(f_ref, t_ref, t_mean)
            for block in blocks:
                a_ref[block, :] = (
                    lead * t_ref[block, :] + t_mean * k_ref[block, :].astype(f32) + dot32(f_ref[block, :], k_ref[...])
                )
            mean = trace_of(a_ref) * size
    if end < 5:
        a_out_ref[...] = a_ref[...]
        r_out_ref[...] = r_ref[...]
        norm_out_ref[...] = norm
        return
    rest_of(f_ref, r_ref, r_mean)
    step = norm * (MUON_RATE * rate)
    push = push_ref[...]
    dot = dot_nt if transposed else dot32
    ortho = r_mean * push + dot(push.astype(bf16), f_ref[...])
    new_ref[...] = weight_ref[...] * (1.0 - MUON_RATE * DECAY) - step * ortho


def newton_call(inputs, outs, transposed, begin, end):
    rate = math.sqrt(max(1.0, PROJ / D)) if transposed else math.sqrt(max(1.0, D / D_INNER))
    whole = pltpu.VMEM((D, D), jnp.float32)
    half = pltpu.VMEM((D, D), jnp.bfloat16)
    hold = pl.BlockSpec(memory_space=pltpu.VMEM)
    return pl.pallas_call(
        functools.partial(newton_kernel, transposed, rate, begin, end),
        in_specs=[pl.BlockSpec(memory_space=pltpu.SMEM)] + [hold] * len(inputs),
        out_shape=[jax.ShapeDtypeStruct(shape, jnp.float32) for shape in outs],
        scratch_shapes=[whole, whole, whole, whole, half, half, half],
        compiler_params=pltpu.CompilerParams(vmem_limit_bytes=VMEM_LIMIT),
        cost_estimate=pl.CostEstimate(
            flops=2 * 5 * (end - begin) * 2 * D**3, bytes_accessed=10**7, transcendentals=0
        ),
        name=("newton_in" if transposed else "newton_out") + str(begin),
    )(core_place(), *inputs)


def own_slice(whole, width, along):
    return lax.dynamic_slice_in_dim(whole, lax.axis_index("opt") * width, width, along)


def exchange(value, axis, bit):
    count = lax.axis_size(axis)
    return lax.ppermute(value, axis, [(i, i ^ (1 << bit)) for i in range(count)])


def side_of(axis, bit):
    return (lax.axis_index(axis) >> bit) & 1


def cut(value, axis, bit, dim):
    half = value.shape[dim] // 2
    side = side_of(axis, bit)
    take = lambda index: lax.dynamic_slice_in_dim(value, index * half, half, dim)
    return take(side), take(1 - side)


def join(own, other, axis, bit, dim):
    lower = side_of(axis, bit) == 0
    return jnp.concatenate([jnp.where(lower, own, other), jnp.where(lower, other, own)], axis=dim)


AXES = ("dp", "opt")


def partner_index(bits, offset):
    across = lax.axis_size("opt")
    flip = 0
    for place, (axis, bit) in enumerate(reversed(bits)):
        if (offset >> place) & 1:
            flip ^= (1 << bit) * (across if axis == "dp" else 1)
    return [(i, i ^ flip) for i in range(lax.axis_size("dp") * across)]


def own_index(bits):
    index = 0
    for axis, bit in bits:
        index = 2 * index + side_of(axis, bit)
    return index


def send_parts(parts, bits):
    own = own_index(bits)
    take = lambda offset: lax.dynamic_index_in_dim(parts, own ^ offset, 0, keepdims=False)
    return take(0), [take(offset) for offset in range(1, 1 << len(bits))]


def swap_parts(parts, bits):
    if not isinstance(parts, list):
        parts = [parts] * ((1 << len(bits)) - 1)
    return [lax.ppermute(part, AXES, partner_index(bits, offset)) for offset, part in enumerate(parts, 1)]


def add_parts(kept, received):
    total = kept.astype(jnp.float32)
    for part in received:
        total = total + part.astype(jnp.float32)
    return total.astype(kept.dtype)


def join_parts(piece, received, bits):
    pieces = [piece] + received
    own = own_index(bits)
    places = []
    for place in range(1 << len(bits)):
        value = pieces[0]
        for offset in range(1, 1 << len(bits)):
            value = jnp.where(own ^ offset == place, pieces[offset], value)
        places.append(value)
    return jnp.stack(places)


def dp_groups():
    bits = [("dp", bit) for bit in range(1, (lax.axis_size("dp") - 1).bit_length())]
    return [bits[i : i + 2] for i in range(0, len(bits), 2)]


def split_rows(piece, bits):
    parts = piece.reshape(piece.shape[0], 1 << len(bits), -1, piece.shape[-1]).swapaxes(0, 1)
    return send_parts(parts, bits)


def merge_rows(piece, received, bits):
    parts = join_parts(piece, received, bits).swapaxes(0, 1)
    return parts.reshape(piece.shape[0], -1, piece.shape[-1])


def tie(*values):
    return lax.optimization_barrier(values)


def fetch_shards(shard):
    across = exchange(shard, "opt", 1)
    return [shard, exchange(shard, "opt", 0), across, exchange(across, "opt", 0)]


def in_order(pieces):
    core, far = side_of("opt", 0) == 0, side_of("opt", 1) == 0
    near = [jnp.where(core, pieces[0], pieces[1]), jnp.where(core, pieces[1], pieces[0])]
    other = [jnp.where(core, pieces[2], pieces[3]), jnp.where(core, pieces[3], pieces[2])]
    low = [jnp.where(far, n, o) for n, o in zip(near, other)]
    high = [jnp.where(far, o, n) for n, o in zip(near, other)]
    return jnp.concatenate(low + high, axis=0)


COLUMN_BLOCK = 384
SHARD = PROJ // 4
SHARD_LANES = 896


def project_kernel(
    place_ref, tokens_ref, gain_ref, own_ref, core_ref, across_ref, last_ref,
    proj_ref, hidden_ref, weight_out_ref, scale_ref,
    shards_ref, weight_ref, normed_ref, sems,
):
    step = pl.program_id(0)

    @pl.when(step == 0)
    def start():
        copies = [
            pltpu.make_async_copy(ref, shards_ref.at[place_ref[0] ^ place], sems.at[place])
            for place, ref in enumerate((own_ref, core_ref, across_ref, last_ref))
        ]
        for copy in copies:
            copy.start()
        inflow = tokens_ref[...].astype(jnp.float32)
        scale = lax.rsqrt(jnp.mean(inflow * inflow, axis=1, keepdims=True) + EPSILON)
        normed_ref[...] = (inflow * scale * gain_ref[...]).astype(jnp.bfloat16)
        hidden_ref[...] = normed_ref[...]
        scale_ref[...] = jnp.broadcast_to(scale, scale_ref.shape)
        for copy in copies:
            copy.wait()
        weight_ref[:, PROJ - PROJ % 128 :] = jnp.zeros((D, PADDED - PROJ + PROJ % 128), jnp.bfloat16)
        for place in range(4):
            weight_ref[:, place * SHARD : (place + 1) * SHARD] = shards_ref[place, :, :SHARD]

    block = weight_ref[:, pl.ds(pl.multiple_of(step * COLUMN_BLOCK, 128), COLUMN_BLOCK)]
    weight_out_ref[...] = block
    proj_ref[...] = dot32(normed_ref[...], block).astype(jnp.bfloat16)


def project(tokens, gain_vec, pieces):
    length = tokens.shape[0]
    bf16 = jnp.bfloat16
    hold = pl.BlockSpec(memory_space=pl.ANY)
    return pl.pallas_call(
        project_kernel,
        grid=(PADDED // COLUMN_BLOCK,),
        in_specs=[pl.BlockSpec(memory_space=pltpu.SMEM), fixed_block(length, D), fixed_block(1, D)] + [hold] * 4,
        out_specs=[
            pl.BlockSpec((length, COLUMN_BLOCK), lambda i: (0, i)),
            fixed_block(length, D),
            pl.BlockSpec((D, COLUMN_BLOCK), lambda i: (0, i)),
            fixed_block(length, 128),
        ],
        out_shape=[
            jax.ShapeDtypeStruct((length, PADDED), bf16), jax.ShapeDtypeStruct((length, D), bf16),
            jax.ShapeDtypeStruct((D, PADDED), bf16), jax.ShapeDtypeStruct((length, 128), jnp.float32),
        ],
        scratch_shapes=[
            pltpu.VMEM((4, D, SHARD_LANES), bf16), pltpu.VMEM((D, PADDED), bf16), pltpu.VMEM((length, D), bf16),
            pltpu.SemaphoreType.DMA((4,)),
        ],
        compiler_params=pltpu.CompilerParams(
            dimension_semantics=("arbitrary",), vmem_limit_bytes=VMEM_LIMIT
        ),
        cost_estimate=pl.CostEstimate(
            flops=2 * length * D * PADDED, bytes_accessed=22 * 10**6, transcendentals=0
        ),
        name="project",
    )(lax.axis_index("opt").astype(jnp.int32)[None], tokens, gain_vec[None, :], *pieces)


def weight_grad_kernel(place_ref, hidden_ref, gate_ref, conv_ref, kept_ref, sent_ref, turned_ref, whole_ref):
    step = pl.program_id(0)

    @pl.when(step == 0)
    def start():
        turned_ref[...] = hidden_ref[...].astype(jnp.float32).T.astype(jnp.bfloat16)

    for shard in range(4):
        first = (shard * SHARD) // 128 * 128
        last = min(-(-((shard + 1) * SHARD) // 128) * 128, PADDED)

        @pl.when(step == shard)
        def work():
            done = -(-(shard * SHARD) // 128) * 128
            for ref, begin, end in ((gate_ref, 0, D_INNER), (conv_ref, D_INNER, PADDED)):
                low, high = max(begin, done), min(end, last)
                if low < high:
                    whole_ref[:, low:high] = dot32(turned_ref[...], ref[:, low - begin : high - begin]).astype(jnp.bfloat16)
            block = whole_ref[:, shard * SHARD : (shard + 1) * SHARD]
            block = jnp.concatenate([block, jnp.zeros((D, SHARD_LANES - SHARD), jnp.bfloat16)], axis=1)

            @pl.when(place_ref[0] == shard % 2)
            def keep():
                kept_ref[0] = block

            @pl.when(place_ref[0] != shard % 2)
            def send():
                sent_ref[0] = block


def weight_grad(hidden, gate, conv):
    length = hidden.shape[0]
    bf16 = jnp.bfloat16
    shards = jax.ShapeDtypeStruct((2, D, SHARD_LANES), bf16)
    return pl.pallas_call(
        weight_grad_kernel,
        grid=(4,),
        in_specs=[
            pl.BlockSpec(memory_space=pltpu.SMEM), fixed_block(length, D), fixed_block(length, D_INNER),
            fixed_block(length, PADDED - D_INNER),
        ],
        out_specs=[pl.BlockSpec((1, D, SHARD_LANES), lambda i: (i // 2, 0, 0))] * 2,
        out_shape=[shards, shards],
        scratch_shapes=[pltpu.VMEM((D, length), bf16), pltpu.VMEM((D, PADDED), bf16)],
        compiler_params=pltpu.CompilerParams(
            dimension_semantics=("arbitrary",), vmem_limit_bytes=VMEM_LIMIT
        ),
        cost_estimate=pl.CostEstimate(
            flops=2 * length * D * PADDED, bytes_accessed=14 * 10**6, transcendentals=0
        ),
        name="weight_grad",
    )(side_of("opt", 0).astype(jnp.int32)[None], hidden, gate, conv)


def on_device(tokens, cotangent, w_in, w_out, small, mom_in, mom_out, adam_m, adam_v):
    bf16, f32 = jnp.bfloat16, jnp.float32
    groups = dp_groups()

    own_in = jnp.pad(w_in.astype(bf16), ((0, 0), (0, SHARD_LANES - SHARD)))
    across_in = exchange(own_in, "opt", 1)
    core_in = exchange(own_in, "opt", 0)
    params = in_order(fetch_shards(small.astype(bf16))).astype(f32)
    sections = [D, D + D_INNER, D + D_INNER + CONV * CONV_CH]
    sections += [sections[-1] + CONV_CH + place * HEADS for place in range(3)]
    gain_vec, gate_gain, taps, conv_bias, dt_bias, a_log, skip_gain = jnp.split(params, sections)
    rate = -jnp.exp(a_log)
    spread, reduce_mat = head_matrices()
    fixed = (jnp.repeat(skip_gain, HEAD_CHANNELS)[None, :], pad_heads(dt_bias), pad_heads(rate), spread, reduce_mat)
    own_out = w_out.astype(bf16)
    prepared = (gain_vec, gate_gain[None, :], taps.reshape(CONV, CONV_CH), conv_bias[None, :], fixed)
    across_in, core_in, prepared, own_out = tie(across_in, core_in, prepared, own_out)
    gain_vec, gate_gain, taps, conv_bias, fixed = prepared
    last_in = exchange(across_in, "opt", 0)
    last_in, own_out = tie(last_in, own_out)
    across_out, core_out = exchange(own_out, "opt", 1), exchange(own_out, "opt", 0)
    projected, hidden, w_pad, scale = project(tokens, gain_vec, [own_in, core_in, across_in, last_in])
    across_out, core_out, projected, cotangent = tie(across_out, core_out, projected, cotangent)
    w_out_b = in_order([own_out, core_out, across_out, exchange(across_out, "opt", 0)])
    grad_mixed = dot_nt(cotangent, w_out_b).astype(bf16)

    mixed, active, slope, grad_scan, grad_gate, states, inner, gain_acc, skip_acc = mixer_forward(
        projected, grad_mixed, taps, conv_bias, gate_gain, *fixed
    )

    inflow = tokens.astype(f32)
    square = [("opt", 1), ("dp", 0)]
    out_kept, out_sent = cut(dot_tn(mixed, cotangent).astype(bf16).reshape(2, 2, -1, D), "opt", 0, 1)
    mixed, out_sent = tie(mixed, out_sent)
    out_got = exchange(out_sent, "opt", 0)
    block = (inflow + dot32(mixed, w_out_b)).astype(bf16)
    block, out_got = tie(block, out_got)
    out_kept, out_sent = send_parts((out_kept + out_got).reshape(4, -1, D), square)
    grad_scan, out_sent = tie(grad_scan, out_sent)
    out_got = swap_parts(out_sent, square)
    grad_conv, taps_acc, bias_acc, dt_acc, rate_acc = mixer_backward(
        projected, active, slope, grad_scan, states, inner, taps, *fixed
    )
    grad_conv, out_got = tie(grad_conv, out_got)
    out_kept, out_sent = split_rows(add_parts(out_kept, out_got)[None], groups[0])
    grad_conv, out_sent = tie(grad_conv, out_sent)
    out_got = swap_parts(out_sent, groups[0])
    kept, sent = weight_grad(hidden, grad_gate, grad_conv)
    sent, out_got = tie(sent, out_got)

    in_got = exchange(sent, "opt", 0)
    out_piece = add_parts(out_kept, out_got)
    for bits in groups[1:]:
        out_kept, out_sent = split_rows(out_piece, bits)
        out_piece = add_parts(out_kept, swap_parts(out_sent, bits))
    for bits in reversed(groups[1:]):
        out_piece = merge_rows(out_piece, swap_parts(out_piece, bits), bits)
    out_got = swap_parts(out_piece, groups[0])
    in_got, out_got = tie(in_got, out_got)
    pair_in = kept + in_got
    one_kept, one_sent = cut(pair_in[:, : D // 2], "opt", 1, 0)
    two_kept, two_sent = cut(pair_in[:, D // 2 :], "dp", 0, 1)
    out_rows = merge_rows(out_piece, out_got, groups[0])[0]
    one_sent, two_sent, out_rows, grad_gate = tie(one_sent, two_sent, out_rows, grad_gate)

    one_got, two_got, out_got = exchange(one_sent, "opt", 1), exchange(two_sent, "dp", 0), exchange(out_rows, "dp", 0)
    grad_hidden = dot_nt(grad_gate, w_pad[:, :D_INNER]) + dot_nt(grad_conv, w_pad[:, D_INNER:])
    one_got, two_got, out_got, grad_hidden = tie(one_got, two_got, out_got, grad_hidden)

    one_kept, one_sent = cut((one_kept + one_got)[0], "dp", 0, 0)
    two_kept, two_sent = cut(two_kept + two_got, "opt", 1, 0)
    one_sent, two_sent, out_rows, out_got = tie(one_sent, two_sent, out_rows, out_got)
    one_got, two_got = exchange(one_sent, "dp", 0), exchange(two_sent, "opt", 1)
    owned_out = join(out_rows, out_got, "dp", 0, 0).astype(f32)
    mom_out_new = MOMENTUM * mom_out + owned_out
    push_out = owned_out + MOMENTUM * mom_out_new
    gram_kept, gram_sent = gram_parts(push_out.astype(bf16), "gram_out")
    gram_got = exchange(gram_sent, "opt", 0)
    one_got, two_got, gram_got = tie(one_got, two_got, gram_got)

    gram_out = gram_kept + gram_got
    in_piece = jnp.stack([one_kept + one_got, (two_kept + two_got)[0]])
    in_kept, in_sent = split_rows(in_piece, groups[0])
    in_sent, gram_out, grad_hidden = tie(in_sent, gram_out, grad_hidden)
    in_got = swap_parts(in_sent, groups[0])
    gram_got = exchange(gram_out, "opt", 1)
    normal = inflow * scale[:, :1]
    grad_gain = jnp.sum(normal * grad_hidden, axis=0)
    grad_normal = grad_hidden * gain_vec
    grad_tokens = cotangent.astype(f32) + scale[:, :1] * (
        grad_normal - normal * jnp.mean(grad_normal * normal, axis=1, keepdims=True)
    )
    grad_small = jnp.concatenate([
        grad_gain,
        gain_acc.sum(0),
        taps_acc.sum(1).reshape(-1),
        bias_acc.sum(0),
        dt_acc.sum(0)[:HEADS],
        rate_acc.sum(0)[:HEADS] * rate,
        skip_acc.sum(0).reshape(HEADS, HEAD_CHANNELS).sum(1),
    ])
    in_got, grad_tokens, grad_small = tie(in_got, grad_tokens, grad_small)

    in_piece = add_parts(in_kept, in_got)
    for bits in groups[1:]:
        in_kept, in_sent = split_rows(in_piece, bits)
        in_piece = add_parts(in_kept, swap_parts(in_sent, bits))
    for bits in reversed(groups[1:]):
        in_piece = merge_rows(in_piece, swap_parts(in_piece, bits), bits)
    in_piece, grad_small, gram_got = tie(in_piece, grad_small, gram_got)
    in_got = swap_parts(in_piece, groups[0])
    small_got = exchange(grad_small, "opt", 0)
    gram_out = gram_out + gram_got
    gram_other = exchange(gram_out, "opt", 0)
    in_got, small_got, gram_other = tie(in_got, small_got, gram_other)

    in_rows = merge_rows(in_piece, in_got, groups[0])
    grad_small = grad_small + small_got
    in_rows, grad_small, gram_out = tie(in_rows, grad_small, gram_out)
    in_got = exchange(in_rows, "dp", 0)
    small_got = exchange(grad_small, "opt", 1)
    halfway = newton_call((gram_out, gram_other), ((D, D), (D, D), (1, 1)), False, 0, 2)
    in_got, small_got, halfway = tie(in_got, small_got, halfway)

    owned_in = join(in_rows, in_got, "dp", 0, 1).reshape(D, SHARD_LANES)[:, :SHARD].T.astype(f32)
    mom_in_new = MOMENTUM * mom_in.T + owned_in
    push_in = owned_in + MOMENTUM * mom_in_new
    gram_kept, gram_sent = gram_parts(push_in.astype(bf16), "gram_in")
    grad_small = grad_small + small_got
    gram_sent, grad_small = tie(gram_sent, grad_small)
    gram_got = exchange(gram_sent, "opt", 0)
    small_got = exchange(grad_small, "dp", 0)
    gram_got, small_got = tie(gram_got, small_got)
    gram_in = gram_kept + gram_got
    grad_small = grad_small + small_got
    gram_in, grad_small, halfway = tie(gram_in, grad_small, halfway)
    gram_got = exchange(gram_in, "opt", 1)
    small_got = exchange(grad_small, "dp", 1)
    (w_out_new,) = newton_call((*halfway, push_out, w_out), (w_out.shape,), False, 2, 5)
    gram_got, small_got, w_out_new = tie(gram_got, small_got, w_out_new)
    gram_in = gram_in + gram_got
    grad_small = grad_small + small_got
    gram_in, grad_small = tie(gram_in, grad_small)
    gram_other = exchange(gram_in, "opt", 0)
    for bit in range(2, (lax.axis_size("dp") - 1).bit_length()):
        grad_small = grad_small + exchange(grad_small, "dp", bit)
    gram_other, grad_small = tie(gram_other, grad_small)
    (w_in_new,) = newton_call((gram_in, gram_other, push_in, w_in.T), (push_in.shape,), True, 0, 5)

    owned_small = own_slice(grad_small, small.shape[0], 0)
    adam_m_new = BETA_ONE * adam_m + (1.0 - BETA_ONE) * owned_small
    adam_v_new = BETA_TWO * adam_v + (1.0 - BETA_TWO) * owned_small * owned_small
    small_new = small * (1.0 - ADAM_RATE * DECAY) - ADAM_RATE * (
        adam_m_new / (1.0 - BETA_ONE**STEP)
    ) / (jnp.sqrt(adam_v_new / (1.0 - BETA_TWO**STEP)) + ADAM_EPS)
    return (
        block,
        grad_tokens,
        owned_in.T,
        owned_out,
        owned_small,
        mom_in_new.T,
        mom_out_new,
        w_in_new.T,
        w_out_new,
        small_new,
        adam_m_new,
        adam_v_new,
    )


def solution(mesh):
    in_specs = (
        P(("dp", "opt"), None),
        P(("dp", "opt"), None),
        P(None, "opt"),
        P("opt", None),
        P("opt"),
        P(None, "opt"),
        P("opt", None),
        P("opt"),
        P("opt"),
    )
    out_specs = (
        P(("dp", "opt"), None),
        P(("dp", "opt"), None),
        P(None, "opt"),
        P("opt", None),
        P("opt"),
        P(None, "opt"),
        P("opt", None),
        P(None, "opt"),
        P("opt", None),
        P("opt"),
        P("opt"),
        P("opt"),
    )
    return jax.shard_map(
        on_device, mesh=mesh, in_specs=in_specs, out_specs=out_specs, check_vma=False
    )
```

```python
import functools
import math

import jax
import jax.numpy as jnp
from jax import lax
from jax.experimental import pallas as pl
from jax.experimental.pallas import tpu as pltpu
from jax.sharding import PartitionSpec as P

D = 768
HEADS = 24
HEAD_CHANNELS = 64
STATE = 128
CONV = 4
SEQ_LEN = 1024
STEP = 10
D_INNER = 1536
CONV_CH = 1792
PROJ = 3352


EPSILON = 1e-05
COEF_A = 3.4445
COEF_B = -4.775
COEF_C = 2.0315
MOMENTUM = 0.95
MUON_RATE = 0.5
DECAY = 0.01
ADAM_RATE = 0.2
BETA_ONE = 0.9
BETA_TWO = 0.95
ADAM_EPS = 1e-08


SPAN = 128
CHUNKS = SEQ_LEN // SPAN
PAIRS = HEADS // 2
WIDTH = 2 * HEAD_CHANNELS
CONV_END = D_INNER + CONV_CH
PADDED = CONV_END + 128
TAIL = 8
VMEM_LIMIT = 56 * 1024 * 1024


def dot32(left, right):
    return jnp.dot(left, right, preferred_element_type=jnp.float32)


def dot_nt(left, right):
    return lax.dot_general(left, right, (((1,), (1,)), ((), ())), preferred_element_type=jnp.float32)


def dot_tn(left, right):
    return lax.dot_general(left, right, (((0,), (0,)), ((), ())), preferred_element_type=jnp.float32)


def halves(value):
    high = value.astype(jnp.bfloat16)
    return high, (value - high.astype(jnp.float32)).astype(jnp.bfloat16)


def sigmoid(value):
    return 0.5 * jnp.tanh(0.5 * value) + 0.5


def softplus(value):
    return jnp.maximum(value, 0.0) + jnp.log1p(jnp.exp(-jnp.abs(value)))


def fold_rows(value):
    return jnp.sum(value.reshape(value.shape[0] // 8, 8, value.shape[1]), axis=0)


def sum_first_row(ref):
    ref[0:1, :] = jnp.sum(ref[...], axis=0, keepdims=True)


def triangle(lower):
    rows = lax.broadcasted_iota(jnp.int32, (SPAN, SPAN), 0)
    cols = lax.broadcasted_iota(jnp.int32, (SPAN, SPAN), 1)
    return rows >= cols if lower else rows <= cols


def running_sum(mask, value):
    ones = jnp.where(mask, 1.0, 0.0).astype(jnp.bfloat16)
    high, rest = halves(value)
    low = (value - high.astype(jnp.float32) - rest.astype(jnp.float32)).astype(jnp.bfloat16)
    return dot32(ones, high) + (dot32(ones, rest) + dot32(ones, low))


def head_sums(value, reduce_mat):
    high, low = halves(value)
    return dot32(high, reduce_mat) + dot32(low, reduce_mat)


def step_factors(raw, dt_bias, rate, spread):
    step_size = softplus(raw + dt_bias)
    log_decay = running_sum(triangle(True), step_size * rate)
    last = log_decay[SPAN - 1 : SPAN, :]
    stacked = jnp.concatenate([step_size, jnp.exp(log_decay), jnp.exp(last - log_decay)], axis=0)
    high, low = halves(stacked)
    wide = dot32(jnp.concatenate([high, low], axis=1), spread)
    return step_size, log_decay, wide[:SPAN], wide[SPAN : 2 * SPAN], wide[2 * SPAN :]


def split_pair(value, first):
    return jnp.concatenate(
        [jnp.where(first, value, 0.0), jnp.where(first, 0.0, value)], axis=0
    ).astype(jnp.bfloat16)


def forward_kernel(
    proj_ref, back_ref, taps_ref, conv_bias_ref, gate_gain_ref, skip_ref, dt_bias_ref, rate_ref, spread_ref, reduce_ref,
    mixed_ref, active_ref, slope_ref, grad_scan_ref, grad_gate_ref, states_ref, inner_ref, gain_acc_ref, skip_acc_ref,
    window_ref, state_ref, skip_part_ref,
):
    f32, bf16 = jnp.float32, jnp.bfloat16

    @pl.when(pl.program_id(0) == 0)
    def start():
        window_ref[0:TAIL, :] = jnp.zeros((TAIL, CONV_CH), f32)
        state_ref[...] = jnp.zeros((STATE, D_INNER), f32)
        gain_acc_ref[...] = jnp.zeros((8, D_INNER), f32)
        skip_part_ref[...] = jnp.zeros((8, D_INNER), f32)

    window_ref[TAIL:, :] = proj_ref[:, D_INNER:CONV_END].astype(f32)
    conv_out = conv_bias_ref[...]
    for tap in range(CONV):
        start_row = TAIL - (CONV - 1) + tap
        conv_out = conv_out + taps_ref[tap : tap + 1, :] * window_ref[start_row : start_row + SPAN, :]
    window_ref[0:TAIL, :] = window_ref[SPAN:, :]
    part = sigmoid(conv_out)
    silu = conv_out * part
    active_ref[...] = silu.astype(bf16)
    slope_ref[...] = (part + silu * (1.0 - part)).astype(bf16)

    values = active_ref[:, :D_INNER].astype(f32)
    input_b = active_ref[:, D_INNER : D_INNER + STATE]
    output_c = active_ref[:, D_INNER + STATE :]
    step_size, log_decay, step_wide, decay_wide, end_wide = step_factors(
        proj_ref[:, CONV_END:].astype(f32), dt_bias_ref[...], rate_ref[...], spread_ref[...]
    )
    decay_rows = log_decay.T
    moved = step_wide * values
    state = state_ref[...]
    state_low = state.astype(bf16)
    states_ref[0] = state_low
    state_ref[...] = state * decay_wide[SPAN - 1 : SPAN, :] + dot_tn(input_b, (moved * end_wide).astype(bf16))
    scores = dot_nt(output_c, input_b)
    causal = triangle(True)
    first = lax.broadcasted_iota(jnp.int32, (SPAN, WIDTH), 1) < HEAD_CHANNELS
    pieces = []
    for pair in range(PAIRS):
        lanes = slice(pair * WIDTH, (pair + 1) * WIDTH)
        mixing = []
        for head in (2 * pair, 2 * pair + 1):
            differ = log_decay[:, head : head + 1] - decay_rows[head : head + 1, :]
            mixing.append((scores * jnp.exp(jnp.where(causal, differ, -1e30))).astype(bf16))
        pieces.append(dot32(jnp.concatenate(mixing, axis=1), split_pair(moved[:, lanes], first)))
    inner = jnp.concatenate(pieces, axis=1) + dot32(output_c, state_low) * decay_wide
    scanned = inner + skip_ref[...] * values

    gate_in = proj_ref[:, :D_INNER].astype(f32)
    part = sigmoid(gate_in)
    gate = gate_in * part
    gated = scanned * gate
    scale = lax.rsqrt(jnp.mean(gated * gated, axis=1, keepdims=True) + EPSILON)
    normal = gated * scale
    mixed_ref[...] = (normal * gate_gain_ref[...]).astype(bf16)
    back = back_ref[...].astype(f32)
    gain_acc_ref[...] += fold_rows(back * normal)
    back = back * gate_gain_ref[...]
    grad_gated = scale * (back - normal * jnp.mean(back * normal, axis=1, keepdims=True))
    grad_gate_ref[...] = (grad_gated * scanned * (part + gate * (1.0 - part))).astype(bf16)
    grad_scan_low = (grad_gated * gate).astype(bf16)
    grad_scan_ref[...] = grad_scan_low
    grad_scan = grad_scan_low.astype(f32)
    skip_part_ref[...] += fold_rows(grad_scan * values)
    inner_ref[...] = head_sums(grad_scan * inner, reduce_ref[...])

    @pl.when(pl.program_id(0) == CHUNKS - 1)
    def finish():
        sum_first_row(gain_acc_ref)
        skip_acc_ref[...] = head_sums(skip_part_ref[...], reduce_ref[...])
        sum_first_row(skip_acc_ref)


def backward_kernel(
    proj_ref, active_ref, slope_ref, grad_scan_ref, states_ref, inner_ref, taps_ref, skip_ref, dt_bias_ref, rate_ref,
    spread_ref, reduce_ref,
    grad_ref, taps_acc_ref, bias_acc_ref, dt_acc_ref, rate_acc_ref,
    window_ref, costate_ref,
):
    f32, bf16 = jnp.float32, jnp.bfloat16

    @pl.when(pl.program_id(0) == 0)
    def start():
        window_ref[SPAN:, :] = jnp.zeros((TAIL, CONV_CH), f32)
        costate_ref[...] = jnp.zeros((STATE, D_INNER), f32)
        taps_acc_ref[...] = jnp.zeros((CONV, 8, CONV_CH), f32)
        bias_acc_ref[...] = jnp.zeros((8, CONV_CH), f32)
        dt_acc_ref[...] = jnp.zeros((8, 128), f32)
        rate_acc_ref[...] = jnp.zeros((8, 128), f32)

    values = active_ref[:, :D_INNER].astype(f32)
    input_b = active_ref[:, D_INNER : D_INNER + STATE]
    output_c = active_ref[:, D_INNER + STATE :]
    raw = proj_ref[:, CONV_END:].astype(f32)
    rate = rate_ref[...]
    step_size, log_decay, step_wide, decay_wide, end_wide = step_factors(raw, dt_bias_ref[...], rate, spread_ref[...])
    decay_rows = log_decay.T
    moved = step_wide * values
    grad_scan_low = grad_scan_ref[...]
    grad_scan = grad_scan_low.astype(f32)
    scores = dot_nt(input_b, output_c)
    causal = triangle(False)
    first = lax.broadcasted_iota(jnp.int32, (SPAN, WIDTH), 1) < HEAD_CHANNELS
    grad_scores = jnp.zeros((SPAN, SPAN), f32)
    pieces = []
    for pair in range(PAIRS):
        lanes = slice(pair * WIDTH, (pair + 1) * WIDTH)
        moved_low = moved[:, lanes].astype(bf16)
        grad_pair = split_pair(grad_scan[:, lanes], first)
        grad_mixing = dot_nt(moved_low, grad_pair)
        mixing = []
        for place, head in enumerate((2 * pair, 2 * pair + 1)):
            differ = decay_rows[head : head + 1, :] - log_decay[:, head : head + 1]
            decay = jnp.exp(jnp.where(causal, differ, -1e30))
            mixing.append((scores * decay).astype(bf16))
            grad_scores = grad_scores + decay * grad_mixing[:, place * SPAN : (place + 1) * SPAN]
        pieces.append(dot32(jnp.concatenate(mixing, axis=1), grad_pair))
    grad_inner = jnp.concatenate(pieces, axis=1)

    costate = costate_ref[...]
    costate_low = costate.astype(bf16)
    states_low = states_ref[0]
    last_wide = decay_wide[SPAN - 1 : SPAN, :]
    kept = fold_rows(costate * states_low.astype(f32)) * last_wide
    grad_cross = dot32(input_b, costate_low) * end_wide
    grad_decayed = (grad_scan * decay_wide).astype(bf16)
    grad_scores_low = grad_scores.astype(bf16)
    grad_b = dot32(grad_scores_low, output_c) + dot_nt((moved * end_wide).astype(bf16), costate_low)
    grad_c = dot_tn(grad_scores_low, input_b) + dot_nt(grad_decayed, states_low)
    costate_ref[...] = costate * last_wide + dot_tn(output_c, grad_decayed)

    moved_round = moved.astype(bf16).astype(f32)
    grad_moved = grad_inner + grad_cross
    reduce_mat = reduce_ref[...]
    own = head_sums(moved_round * grad_inner, reduce_mat)
    crossing = dot32((moved * grad_cross).astype(bf16), reduce_mat)
    grad_step = dot32((values * grad_moved).astype(bf16), reduce_mat)
    keeping = jnp.sum(head_sums(kept, reduce_mat), axis=0, keepdims=True)
    grad_log = (
        running_sum(triangle(False), inner_ref[...] - own)
        + running_sum(triangle(True), crossing) - crossing
        + keeping
    )
    grad_raw = (grad_step + rate * grad_log) * sigmoid(raw + dt_bias_ref[...])
    rate_acc_ref[...] += fold_rows(step_size * grad_log)
    dt_acc_ref[...] += fold_rows(grad_raw)
    grad_ref[:, CONV_CH:] = grad_raw.astype(bf16)

    grad_values = step_wide * grad_moved + skip_ref[...] * grad_scan
    grad_active = jnp.concatenate([grad_values, grad_b, grad_c], axis=1)
    grad_conv = grad_active * slope_ref[...].astype(f32)
    bias_acc_ref[...] += fold_rows(grad_conv)
    window_ref[0:SPAN, :] = grad_conv
    conv_in = proj_ref[:, D_INNER:CONV_END].astype(f32)
    grad_in = jnp.zeros((SPAN, CONV_CH), f32)
    for tap in range(CONV):
        start_row = CONV - 1 - tap
        shifted = window_ref[start_row : start_row + SPAN, :]
        grad_in = grad_in + taps_ref[tap : tap + 1, :] * shifted
        taps_acc_ref[tap] += fold_rows(conv_in * shifted)
    grad_ref[:, :CONV_CH] = grad_in.astype(bf16)
    window_ref[SPAN:, :] = window_ref[0:TAIL, :]

    @pl.when(pl.program_id(0) == CHUNKS - 1)
    def finish():
        for tap in range(CONV):
            sum_first_row(taps_acc_ref.at[tap])
        sum_first_row(bias_acc_ref)
        sum_first_row(dt_acc_ref)
        sum_first_row(rate_acc_ref)


def head_matrices():
    spread = jnp.pad(jnp.repeat(jnp.eye(HEADS, dtype=jnp.bfloat16), HEAD_CHANNELS, axis=1), ((0, 128 - HEADS), (0, 0)))
    return jnp.concatenate([spread, spread], axis=0), spread.T


def row_block(width, order):
    return pl.BlockSpec((SPAN, width), lambda i: (order(i), 0))


def fixed_block(*shape):
    return pl.BlockSpec(shape, lambda i: (0,) * len(shape))


def state_block(order):
    return pl.BlockSpec((1, STATE, D_INNER), lambda i: (order(i), 0, 0))


def pad_heads(vector):
    return jnp.pad(vector, (0, 128 - HEADS))[None, :]


def mixer_forward(projected, back, taps, conv_bias, gate_gain, skip_wide, dt_bias, rate, spread, reduce_mat):
    f32, bf16 = jnp.float32, jnp.bfloat16
    order = lambda i: i
    rows = lambda width, kind: jax.ShapeDtypeStruct((SEQ_LEN, width), kind)
    return pl.pallas_call(
        forward_kernel,
        grid=(CHUNKS,),
        in_specs=[
            row_block(PADDED, order), row_block(D_INNER, order), fixed_block(CONV, CONV_CH), fixed_block(1, CONV_CH),
            fixed_block(1, D_INNER), fixed_block(1, D_INNER), fixed_block(1, 128), fixed_block(1, 128),
            fixed_block(256, D_INNER), fixed_block(D_INNER, 128),
        ],
        out_specs=[
            row_block(D_INNER, order), row_block(CONV_CH, order), row_block(CONV_CH, order), row_block(D_INNER, order),
            row_block(D_INNER, order), state_block(order), row_block(128, order), fixed_block(8, D_INNER),
            fixed_block(8, 128),
        ],
        out_shape=[
            rows(D_INNER, bf16), rows(CONV_CH, bf16), rows(CONV_CH, bf16), rows(D_INNER, bf16), rows(D_INNER, bf16),
            jax.ShapeDtypeStruct((CHUNKS, STATE, D_INNER), bf16), rows(128, f32),
            jax.ShapeDtypeStruct((8, D_INNER), f32), jax.ShapeDtypeStruct((8, 128), f32),
        ],
        scratch_shapes=[
            pltpu.VMEM((SPAN + TAIL, CONV_CH), f32), pltpu.VMEM((STATE, D_INNER), f32), pltpu.VMEM((8, D_INNER), f32),
        ],
        compiler_params=pltpu.CompilerParams(
            dimension_semantics=("arbitrary",), vmem_limit_bytes=VMEM_LIMIT
        ),
        cost_estimate=pl.CostEstimate(flops=8 * 10**9, bytes_accessed=32 * 10**6, transcendentals=10**7),
        name="mixer_forward",
    )(projected, back, taps, conv_bias, gate_gain, skip_wide, dt_bias, rate, spread, reduce_mat)


def mixer_backward(projected, active, slope, grad_scan, states, inner, taps, skip_wide, dt_bias, rate, spread, reduce_mat):
    f32, bf16 = jnp.float32, jnp.bfloat16
    order = lambda i: CHUNKS - 1 - i
    return pl.pallas_call(
        backward_kernel,
        grid=(CHUNKS,),
        in_specs=[
            row_block(PADDED, order), row_block(CONV_CH, order), row_block(CONV_CH, order), row_block(D_INNER, order),
            state_block(order), row_block(128, order), fixed_block(CONV, CONV_CH), fixed_block(1, D_INNER),
            fixed_block(1, 128), fixed_block(1, 128), fixed_block(256, D_INNER), fixed_block(D_INNER, 128),
        ],
        out_specs=[
            row_block(CONV_CH + 128, order), fixed_block(CONV, 8, CONV_CH), fixed_block(8, CONV_CH),
            fixed_block(8, 128), fixed_block(8, 128),
        ],
        out_shape=[
            jax.ShapeDtypeStruct((SEQ_LEN, CONV_CH + 128), bf16), jax.ShapeDtypeStruct((CONV, 8, CONV_CH), f32),
            jax.ShapeDtypeStruct((8, CONV_CH), f32), jax.ShapeDtypeStruct((8, 128), f32),
            jax.ShapeDtypeStruct((8, 128), f32),
        ],
        scratch_shapes=[pltpu.VMEM((SPAN + TAIL, CONV_CH), f32), pltpu.VMEM((STATE, D_INNER), f32)],
        compiler_params=pltpu.CompilerParams(
            dimension_semantics=("arbitrary",), vmem_limit_bytes=VMEM_LIMIT
        ),
        cost_estimate=pl.CostEstimate(flops=12 * 10**9, bytes_accessed=32 * 10**6, transcendentals=10**7),
        name="mixer_backward",
    )(projected, active, slope, grad_scan, states, inner, taps, skip_wide, dt_bias, rate, spread, reduce_mat)


ROW_BLOCK = 256
UPPER = [(0, 0), (0, 1), (0, 2), (1, 1), (1, 2), (2, 2)]


def gram_kernel(place_ref, push_ref, kept_ref, sent_ref):
    for place, (row, col) in enumerate(UPPER):
        rows = slice(row * ROW_BLOCK, (row + 1) * ROW_BLOCK)
        cols = slice(col * ROW_BLOCK, (col + 1) * ROW_BLOCK)
        tile = dot_tn(push_ref[:, rows], push_ref[:, cols])

        @pl.when(place_ref[0] == place // 3)
        def keep():
            kept_ref[place % 3] = tile

        @pl.when(place_ref[0] != place // 3)
        def send():
            sent_ref[place % 3] = tile


def gram_parts(push, name):
    tiles = jax.ShapeDtypeStruct((3, ROW_BLOCK, ROW_BLOCK), jnp.float32)
    hold = pl.BlockSpec(memory_space=pltpu.VMEM)
    return pl.pallas_call(
        gram_kernel,
        in_specs=[pl.BlockSpec(memory_space=pltpu.SMEM), hold],
        out_shape=[tiles, tiles],
        compiler_params=pltpu.CompilerParams(vmem_limit_bytes=VMEM_LIMIT),
        cost_estimate=pl.CostEstimate(
            flops=2 * D * push.size, bytes_accessed=2 * push.size, transcendentals=0
        ),
        name=name,
    )(core_place(), push)


def core_place():
    return side_of("opt", 0).astype(jnp.int32)[None]


def newton_kernel(transposed, rate, begin, end, place_ref, *refs):
    if begin == 0:
        (own_ref, other_ref), refs = refs[:2], refs[2:]
    else:
        (a_in_ref, r_in_ref, norm_ref), refs = refs[:3], refs[3:]
    if end == 5:
        (grad_ref, mom_ref, weight_ref, owned_ref, mom_new_ref, new_ref), refs = refs[:6], refs[6:]
    else:
        (a_out_ref, r_out_ref, norm_out_ref), refs = refs[:3], refs[3:]
    a_ref, p_ref, t_ref, r_ref, e_ref, k_ref, f_ref = refs
    f32, bf16 = jnp.float32, jnp.bfloat16
    blocks = [slice(i, i + ROW_BLOCK) for i in range(0, D, ROW_BLOCK)]
    size = 1.0 / D
    rows = lax.broadcasted_iota(jnp.int32, (ROW_BLOCK, ROW_BLOCK), 0)
    cols = lax.broadcasted_iota(jnp.int32, (ROW_BLOCK, ROW_BLOCK), 1)
    eye = rows == cols

    def tile_trace(tile):
        kept = jnp.where(eye, tile, 0.0)
        return jnp.sum(jnp.sum(kept, axis=0, keepdims=True), axis=1, keepdims=True)

    def trace_of(ref):
        return sum(tile_trace(ref[block, block]) for block in blocks)

    def shifted(value, row, amount):
        tiles = [value[:, block] for block in blocks]
        tiles[row] = tiles[row] - jnp.where(eye, amount, 0.0)
        return jnp.concatenate(tiles, axis=1)

    def rest_of(target_ref, source_ref, amount):
        for row, block in enumerate(blocks):
            target_ref[block, :] = shifted(source_ref[block, :], row, amount).astype(bf16)

    if begin == 0:
        core = place_ref[0] == 0
        for place, (row, col) in enumerate(UPPER):
            own, other = own_ref[place % 3], other_ref[place % 3]
            tile = jnp.where(core, own, other) if place < 3 else jnp.where(core, other, own)
            a_ref[blocks[row], blocks[col]] = tile
            if row != col:
                a_ref[blocks[col], blocks[row]] = tile.T
        total = trace_of(a_ref)
        norm = 1.0 / (jnp.sqrt(total) + 1e-07)
        scale = norm * norm
        for block in blocks:
            a_ref[block, :] = a_ref[block, :] * scale
        mean = total * scale * size
    else:
        norm = norm_ref[...]
        a_ref[...] = a_in_ref[...]
        r_ref[...] = r_in_ref[...]
        mean = trace_of(a_ref) * size
        r_mean = trace_of(r_ref) * size
    for sweep in range(begin, end):
        rest_of(e_ref, a_ref, mean)
        slope = COEF_B + 2.0 * COEF_C * mean
        for row, block in enumerate(blocks):
            poly = slope * a_ref[block, :] + COEF_C * dot32(e_ref[block, :], e_ref[...])
            p_ref[block, :] = shifted(poly, row, COEF_C * mean * mean)
        shift = trace_of(p_ref) * size
        lead = COEF_A + shift
        rest_of(k_ref, p_ref, shift)
        if sweep == 0:
            for row, block in enumerate(blocks):
                r_ref[block, :] = shifted(p_ref[block, :], row, -COEF_A)
            r_mean = lead
        else:
            rest_of(f_ref, r_ref, r_mean)
            for block in blocks:
                r_ref[block, :] = (
                    lead * r_ref[block, :]
                    + r_mean * k_ref[block, :].astype(f32)
                    + dot32(k_ref[block, :], f_ref[...])
                )
            r_mean = trace_of(r_ref) * size
        if sweep < 4:
            for block in blocks:
                t_ref[block, :] = (
                    lead * a_ref[block, :] + mean * k_ref[block, :].astype(f32) + dot32(k_ref[block, :], e_ref[...])
                )
            t_mean = trace_of(t_ref) * size
            rest_of(f_ref, t_ref, t_mean)
            for block in blocks:
                a_ref[block, :] = (
                    lead * t_ref[block, :] + t_mean * k_ref[block, :].astype(f32) + dot32(f_ref[block, :], k_ref[...])
                )
            mean = trace_of(a_ref) * size
    if end < 5:
        a_out_ref[...] = a_ref[...]
        r_out_ref[...] = r_ref[...]
        norm_out_ref[...] = norm
        return
    rest_of(f_ref, r_ref, r_mean)
    step = norm * (MUON_RATE * rate)
    owned = grad_ref[0 : weight_ref.shape[0], :].astype(f32)
    owned_ref[...] = owned
    momentum = MOMENTUM * mom_ref[...] + owned
    mom_new_ref[...] = momentum
    push = owned + MOMENTUM * momentum
    dot = dot_nt if transposed else dot32
    ortho = r_mean * push + dot(push.astype(bf16), f_ref[...])
    new_ref[...] = weight_ref[...] * (1.0 - MUON_RATE * DECAY) - step * ortho


STATE_SHAPES = ((D, D), (D, D), (1, 1))


def nesterov(grad, momentum):
    grad = grad.astype(jnp.float32)
    return (grad + MOMENTUM * (MOMENTUM * momentum + grad)).astype(jnp.bfloat16)


def newton_call(inputs, outs, transposed, begin, end):
    rate = math.sqrt(max(1.0, PROJ / D)) if transposed else math.sqrt(max(1.0, D / D_INNER))
    whole = pltpu.VMEM((D, D), jnp.float32)
    half = pltpu.VMEM((D, D), jnp.bfloat16)
    hold = pl.BlockSpec(memory_space=pltpu.VMEM)
    return pl.pallas_call(
        functools.partial(newton_kernel, transposed, rate, begin, end),
        in_specs=[pl.BlockSpec(memory_space=pltpu.SMEM)] + [hold] * len(inputs),
        out_shape=[jax.ShapeDtypeStruct(shape, jnp.float32) for shape in outs],
        scratch_shapes=[whole, whole, whole, whole, half, half, half],
        compiler_params=pltpu.CompilerParams(vmem_limit_bytes=VMEM_LIMIT),
        cost_estimate=pl.CostEstimate(
            flops=2 * 5 * (end - begin) * 2 * D**3, bytes_accessed=10**7, transcendentals=0
        ),
        name=("newton_in" if transposed else "newton_out") + str(begin),
    )(core_place(), *inputs)


def own_slice(whole, width, along):
    return lax.dynamic_slice_in_dim(whole, lax.axis_index("opt") * width, width, along)


def exchange(value, axis, bit):
    count = lax.axis_size(axis)
    return lax.ppermute(value, axis, [(i, i ^ (1 << bit)) for i in range(count)])


def side_of(axis, bit):
    return (lax.axis_index(axis) >> bit) & 1


def cut(value, axis, bit, dim):
    half = value.shape[dim] // 2
    side = side_of(axis, bit)
    take = lambda index: lax.dynamic_slice_in_dim(value, index * half, half, dim)
    return take(side), take(1 - side)


def join(own, other, axis, bit, dim):
    lower = side_of(axis, bit) == 0
    return jnp.concatenate([jnp.where(lower, own, other), jnp.where(lower, other, own)], axis=dim)


AXES = ("dp", "opt")


def partner_index(bits, offset):
    across = lax.axis_size("opt")
    flip = 0
    for place, (axis, bit) in enumerate(reversed(bits)):
        if (offset >> place) & 1:
            flip ^= (1 << bit) * (across if axis == "dp" else 1)
    return [(i, i ^ flip) for i in range(lax.axis_size("dp") * across)]


def own_index(bits):
    index = 0
    for axis, bit in bits:
        index = 2 * index + side_of(axis, bit)
    return index


def send_parts(parts, bits):
    own = own_index(bits)
    take = lambda offset: lax.dynamic_index_in_dim(parts, own ^ offset, 0, keepdims=False)
    return take(0), [take(offset) for offset in range(1, 1 << len(bits))]


def swap_parts(parts, bits):
    if not isinstance(parts, list):
        parts = [parts] * ((1 << len(bits)) - 1)
    return [lax.ppermute(part, AXES, partner_index(bits, offset)) for offset, part in enumerate(parts, 1)]


def add_parts(kept, received):
    total = kept.astype(jnp.float32)
    for part in received:
        total = total + part.astype(jnp.float32)
    return total.astype(kept.dtype)


def join_parts(piece, received, bits):
    pieces = [piece] + received
    own = own_index(bits)
    places = []
    for place in range(1 << len(bits)):
        value = pieces[0]
        for offset in range(1, 1 << len(bits)):
            value = jnp.where(own ^ offset == place, pieces[offset], value)
        places.append(value)
    return jnp.stack(places)


def dp_groups():
    bits = [("dp", bit) for bit in range(1, (lax.axis_size("dp") - 1).bit_length())]
    return [bits[i : i + 2] for i in range(0, len(bits), 2)]


def split_rows(piece, bits):
    parts = piece.reshape(piece.shape[0], 1 << len(bits), -1, piece.shape[-1]).swapaxes(0, 1)
    return send_parts(parts, bits)


def merge_rows(piece, received, bits):
    parts = join_parts(piece, received, bits).swapaxes(0, 1)
    return parts.reshape(piece.shape[0], -1, piece.shape[-1])


def tie(*values):
    return lax.optimization_barrier(values)


def fetch_shards(shard):
    across = exchange(shard, "opt", 1)
    return [shard, exchange(shard, "opt", 0), across, exchange(across, "opt", 0)]


def in_order(pieces):
    core, far = side_of("opt", 0) == 0, side_of("opt", 1) == 0
    near = [jnp.where(core, pieces[0], pieces[1]), jnp.where(core, pieces[1], pieces[0])]
    other = [jnp.where(core, pieces[2], pieces[3]), jnp.where(core, pieces[3], pieces[2])]
    low = [jnp.where(far, n, o) for n, o in zip(near, other)]
    high = [jnp.where(far, o, n) for n, o in zip(near, other)]
    return jnp.concatenate(low + high, axis=0)


COLUMN_BLOCK = 384
SHARD = PROJ // 4
SHARD_LANES = 896
SHARD_ROWS = 896


def project_kernel(
    place_ref, tokens_ref, gain_ref, own_ref, core_ref, across_ref, last_ref,
    proj_ref, hidden_ref, weight_out_ref, scale_ref,
    shards_ref, weight_ref, normed_ref, sems,
):
    step = pl.program_id(0)

    @pl.when(step == 0)
    def start():
        copies = [
            pltpu.make_async_copy(ref, shards_ref.at[place_ref[0] ^ place], sems.at[place])
            for place, ref in enumerate((own_ref, core_ref, across_ref, last_ref))
        ]
        for copy in copies:
            copy.start()
        inflow = tokens_ref[...].astype(jnp.float32)
        scale = lax.rsqrt(jnp.mean(inflow * inflow, axis=1, keepdims=True) + EPSILON)
        normed_ref[...] = (inflow * scale * gain_ref[...]).astype(jnp.bfloat16)
        hidden_ref[...] = normed_ref[...]
        scale_ref[...] = jnp.broadcast_to(scale, scale_ref.shape)
        for copy in copies:
            copy.wait()
        weight_ref[:, PROJ - PROJ % 128 :] = jnp.zeros((D, PADDED - PROJ + PROJ % 128), jnp.bfloat16)
        for place in range(4):
            weight_ref[:, place * SHARD : (place + 1) * SHARD] = shards_ref[place, :, :SHARD]

    block = weight_ref[:, pl.ds(pl.multiple_of(step * COLUMN_BLOCK, 128), COLUMN_BLOCK)]
    weight_out_ref[...] = block
    proj_ref[...] = dot32(normed_ref[...], block).astype(jnp.bfloat16)


def project(tokens, gain_vec, pieces):
    length = tokens.shape[0]
    bf16 = jnp.bfloat16
    hold = pl.BlockSpec(memory_space=pl.ANY)
    return pl.pallas_call(
        project_kernel,
        grid=(PADDED // COLUMN_BLOCK,),
        in_specs=[pl.BlockSpec(memory_space=pltpu.SMEM), fixed_block(length, D), fixed_block(1, D)] + [hold] * 4,
        out_specs=[
            pl.BlockSpec((length, COLUMN_BLOCK), lambda i: (0, i)),
            fixed_block(length, D),
            pl.BlockSpec((D, COLUMN_BLOCK), lambda i: (0, i)),
            fixed_block(length, 128),
        ],
        out_shape=[
            jax.ShapeDtypeStruct((length, PADDED), bf16), jax.ShapeDtypeStruct((length, D), bf16),
            jax.ShapeDtypeStruct((D, PADDED), bf16), jax.ShapeDtypeStruct((length, 128), jnp.float32),
        ],
        scratch_shapes=[
            pltpu.VMEM((4, D, SHARD_LANES), bf16), pltpu.VMEM((D, PADDED), bf16), pltpu.VMEM((length, D), bf16),
            pltpu.SemaphoreType.DMA((4,)),
        ],
        compiler_params=pltpu.CompilerParams(
            dimension_semantics=("arbitrary",), vmem_limit_bytes=VMEM_LIMIT
        ),
        cost_estimate=pl.CostEstimate(
            flops=2 * length * D * PADDED, bytes_accessed=22 * 10**6, transcendentals=0
        ),
        name="project",
    )(lax.axis_index("opt").astype(jnp.int32)[None], tokens, gain_vec[None, :], *pieces)


def weight_grad_kernel(place_ref, hidden_ref, gate_ref, conv_ref, kept_ref, sent_ref, whole_ref):
    step = pl.program_id(0)
    for shard in range(4):
        first = shard * SHARD
        last = min(-(-(first + SHARD) // 128) * 128, PADDED)
        done = -(-first // 128) * 128

        @pl.when(step == shard)
        def work():
            for ref, begin, end in ((gate_ref, 0, D_INNER), (conv_ref, D_INNER, PADDED)):
                low, high = max(begin, done), min(end, last)
                if low < high:
                    whole_ref[low:high, :] = dot_tn(ref[:, low - begin : high - begin], hidden_ref[...])
            block = whole_ref[first : first + SHARD_ROWS, :].astype(jnp.bfloat16)
            rows = lax.broadcasted_iota(jnp.int32, (SHARD_ROWS, D), 0)
            block = jnp.where(rows < SHARD, block, jnp.zeros_like(block))

            @pl.when(place_ref[0] == shard % 2)
            def keep():
                kept_ref[0] = block

            @pl.when(place_ref[0] != shard % 2)
            def send():
                sent_ref[0] = block


def weight_grad(hidden, gate, conv):
    length = hidden.shape[0]
    shards = jax.ShapeDtypeStruct((2, SHARD_ROWS, D), jnp.bfloat16)
    return pl.pallas_call(
        weight_grad_kernel,
        grid=(4,),
        in_specs=[
            pl.BlockSpec(memory_space=pltpu.SMEM), fixed_block(length, D), fixed_block(length, D_INNER),
            fixed_block(length, PADDED - D_INNER),
        ],
        out_specs=[pl.BlockSpec((1, SHARD_ROWS, D), lambda i: (i // 2, 0, 0))] * 2,
        out_shape=[shards, shards],
        scratch_shapes=[pltpu.VMEM((PADDED, D), jnp.float32)],
        compiler_params=pltpu.CompilerParams(
            dimension_semantics=("arbitrary",), vmem_limit_bytes=VMEM_LIMIT
        ),
        cost_estimate=pl.CostEstimate(
            flops=2 * length * D * PADDED, bytes_accessed=14 * 10**6, transcendentals=0
        ),
        name="weight_grad",
    )(core_place(), hidden, gate, conv)


def on_device(tokens, cotangent, w_in, w_out, small, mom_in, mom_out, adam_m, adam_v):
    bf16, f32 = jnp.bfloat16, jnp.float32
    groups = dp_groups()

    own_in = jnp.pad(w_in.astype(bf16), ((0, 0), (0, SHARD_LANES - SHARD)))
    across_in = exchange(own_in, "opt", 1)
    core_in = exchange(own_in, "opt", 0)
    params = in_order(fetch_shards(small.astype(bf16))).astype(f32)
    sections = [D, D + D_INNER, D + D_INNER + CONV * CONV_CH]
    sections += [sections[-1] + CONV_CH + place * HEADS for place in range(3)]
    gain_vec, gate_gain, taps, conv_bias, dt_bias, a_log, skip_gain = jnp.split(params, sections)
    rate = -jnp.exp(a_log)
    spread, reduce_mat = head_matrices()
    fixed = (jnp.repeat(skip_gain, HEAD_CHANNELS)[None, :], pad_heads(dt_bias), pad_heads(rate), spread, reduce_mat)
    own_out = w_out.astype(bf16)
    prepared = (gain_vec, gate_gain[None, :], taps.reshape(CONV, CONV_CH), conv_bias[None, :], fixed)
    across_in, core_in, prepared, own_out = tie(across_in, core_in, prepared, own_out)
    gain_vec, gate_gain, taps, conv_bias, fixed = prepared
    last_in = exchange(across_in, "opt", 0)
    last_in, own_out = tie(last_in, own_out)
    across_out, core_out = exchange(own_out, "opt", 1), exchange(own_out, "opt", 0)
    projected, hidden, w_pad, scale = project(tokens, gain_vec, [own_in, core_in, across_in, last_in])
    across_out, core_out, projected, cotangent = tie(across_out, core_out, projected, cotangent)
    w_out_b = in_order([own_out, core_out, across_out, exchange(across_out, "opt", 0)])
    grad_mixed = dot_nt(cotangent, w_out_b).astype(bf16)

    mixed, active, slope, grad_scan, grad_gate, states, inner, gain_acc, skip_acc = mixer_forward(
        projected, grad_mixed, taps, conv_bias, gate_gain, *fixed
    )

    inflow = tokens.astype(f32)
    square = [("opt", 1), ("dp", 0)]
    out_kept, out_sent = cut(dot_tn(mixed, cotangent).astype(bf16).reshape(2, 2, -1, D), "opt", 0, 1)
    mixed, out_sent = tie(mixed, out_sent)
    out_got = exchange(out_sent, "opt", 0)
    block = (inflow + dot32(mixed, w_out_b)).astype(bf16)
    block, out_got = tie(block, out_got)
    out_kept, out_sent = send_parts((out_kept + out_got).reshape(4, -1, D), square)
    grad_scan, out_sent = tie(grad_scan, out_sent)
    out_got = swap_parts(out_sent, square)
    grad_conv, taps_acc, bias_acc, dt_acc, rate_acc = mixer_backward(
        projected, active, slope, grad_scan, states, inner, taps, *fixed
    )
    grad_conv, out_got = tie(grad_conv, out_got)
    out_kept, out_sent = split_rows(add_parts(out_kept, out_got)[None], groups[0])
    grad_conv, out_sent = tie(grad_conv, out_sent)
    out_got = swap_parts(out_sent, groups[0])
    kept, sent = weight_grad(hidden, grad_gate, grad_conv)
    sent, out_got = tie(sent, out_got)

    in_got = exchange(sent, "opt", 0)
    out_piece = add_parts(out_kept, out_got)
    for bits in groups[1:]:
        out_kept, out_sent = split_rows(out_piece, bits)
        out_piece = add_parts(out_kept, swap_parts(out_sent, bits))
    for bits in reversed(groups[1:]):
        out_piece = merge_rows(out_piece, swap_parts(out_piece, bits), bits)
    out_piece = out_piece[0]
    out_got = exchange(out_piece, "dp", 0)
    in_got, out_got = tie(in_got, out_got)
    pair_in = kept + in_got
    half = D // 2
    one_kept, one_sent = cut(pair_in[:, :, :half], "opt", 1, 0)
    two_kept, two_sent = cut(pair_in[:, :, half:], "dp", 0, 1)
    out_rows = jnp.concatenate([out_piece, out_got], axis=0)
    one_sent, two_sent, out_rows, grad_gate = tie(one_sent, two_sent, out_rows, grad_gate)

    one_got, two_got = exchange(one_sent, "opt", 1), exchange(two_sent, "dp", 0)
    out_got = swap_parts(out_rows, groups[0])
    grad_hidden = dot_nt(grad_gate, w_pad[:, :D_INNER]) + dot_nt(grad_conv, w_pad[:, D_INNER:])
    one_got, two_got, out_got, grad_hidden = tie(one_got, two_got, out_got, grad_hidden)

    one_kept, one_sent = cut((one_kept + one_got)[0], "dp", 0, 0)
    two_kept, two_sent = cut(two_kept + two_got, "opt", 1, 0)
    one_sent, two_sent, out_rows, out_got = tie(one_sent, two_sent, out_rows, out_got)
    one_got, two_got = exchange(one_sent, "dp", 0), exchange(two_sent, "opt", 1)
    grad_out = join_parts(out_rows, out_got, groups[0]).reshape(1 << len(groups[0]), 2, -1, D)
    lower = side_of("dp", 0) == 0
    near, far = grad_out[:, 0].reshape(-1, D), grad_out[:, 1].reshape(-1, D)
    grad_out = jnp.concatenate([jnp.where(lower, near, far), jnp.where(lower, far, near)], axis=0)
    push_out = nesterov(grad_out, mom_out)
    gram_kept, gram_sent = gram_parts(push_out, "gram_out")
    gram_got = exchange(gram_sent, "opt", 0)
    one_got, two_got, gram_got = tie(one_got, two_got, gram_got)

    gram_out = gram_kept + gram_got
    in_piece = jnp.concatenate([one_kept + one_got, (two_kept + two_got)[0]], axis=1)[None]
    in_kept, in_sent = split_rows(in_piece, groups[0])
    mom_turned = mom_in.T
    in_sent, gram_out, grad_hidden, mom_turned = tie(in_sent, gram_out, grad_hidden, mom_turned)
    in_got = swap_parts(in_sent, groups[0])
    gram_got = exchange(gram_out, "opt", 1)
    normal = inflow * scale[:, :1]
    grad_gain = jnp.sum(normal * grad_hidden, axis=0)
    grad_normal = grad_hidden * gain_vec
    grad_tokens = cotangent.astype(f32) + scale[:, :1] * (
        grad_normal - normal * jnp.mean(grad_normal * normal, axis=1, keepdims=True)
    )
    grad_small = jnp.concatenate([
        grad_gain,
        gain_acc[0],
        taps_acc[:, 0].reshape(-1),
        bias_acc[0],
        dt_acc[0, :HEADS],
        rate_acc[0, :HEADS] * rate,
        skip_acc[0, :HEADS],
    ])
    every = [("dp", 0)] + [bit for bits in groups for bit in bits]
    width = SHARD_ROWS >> len(every)
    mom_padded = jnp.pad(mom_turned, ((0, SHARD_ROWS - SHARD), (0, 0)))
    mom_piece = lax.dynamic_slice_in_dim(mom_padded, own_index(every) * width, width, 0)
    in_got, grad_tokens, grad_small, mom_piece = tie(in_got, grad_tokens, grad_small, mom_piece)

    in_piece = add_parts(in_kept, in_got)
    for bits in groups[1:]:
        in_kept, in_sent = split_rows(in_piece, bits)
        in_piece = add_parts(in_kept, swap_parts(in_sent, bits))
    gram_kept, gram_sent = gram_parts(nesterov(in_piece[0], mom_piece), "gram_in")
    for bits in reversed(groups[1:]):
        in_piece = merge_rows(in_piece, swap_parts(in_piece, bits), bits)
    gram_sent, in_piece, grad_small, gram_got = tie(gram_sent, in_piece, grad_small, gram_got)
    in_got = swap_parts(in_piece, groups[0])
    gram_in = exchange(gram_sent, "opt", 0)
    small_got = exchange(grad_small, "opt", 0)
    gram_out = gram_out + gram_got
    gram_other = exchange(gram_out, "opt", 0)
    gram_in, small_got, gram_other = tie(gram_in, small_got, gram_other)

    gram_kept, gram_sent = send_parts((gram_kept + gram_in).reshape(4, -1, ROW_BLOCK), square)
    grad_small = grad_small + small_got
    gram_sent, grad_small, gram_out = tie(gram_sent, grad_small, gram_out)
    gram_got = swap_parts(gram_sent, square)
    small_got = exchange(grad_small, "opt", 1)
    state = newton_call((gram_out, gram_other), STATE_SHAPES, False, 0, 1)
    gram_got, small_got, state = tie(gram_got, small_got, state)

    gram_in = add_parts(gram_kept, gram_got)
    grad_small = grad_small + small_got
    gram_in, grad_small, in_got = tie(gram_in, grad_small, in_got)
    gram_got = exchange(gram_in, "dp", 1)
    small_got = exchange(grad_small, "dp", 0)
    in_rows = merge_rows(in_piece, in_got, groups[0])[0]
    gram_got, small_got, in_rows = tie(gram_got, small_got, in_rows)

    gram_in = gram_in + gram_got
    grad_small = grad_small + small_got
    gram_in, grad_small, in_rows, state = tie(gram_in, grad_small, in_rows, state)
    gram_got = exchange(gram_in, "dp", 2)
    in_got = exchange(in_rows, "dp", 0)
    small_got = exchange(grad_small, "dp", 1)
    state = newton_call(state, STATE_SHAPES, False, 1, 3)
    gram_got, small_got, state, in_got = tie(gram_got, small_got, state, in_got)

    gram_in = gram_in + gram_got
    grad_small = grad_small + small_got
    for bit in range(3, (lax.axis_size("dp") - 1).bit_length()):
        gram_in = gram_in + exchange(gram_in, "dp", bit)
    gram_in, grad_small, state = tie(gram_in, grad_small, state)
    gram_got = swap_parts(gram_in, square)
    small_got = exchange(grad_small, "dp", 2)
    out_shapes, in_shapes = (w_out.shape,) * 3, (mom_turned.shape,) * 3
    owned_out, mom_out_new, w_out_new = newton_call((*state, grad_out, mom_out, w_out), out_shapes, False, 3, 5)
    gram_got, small_got, w_out_new = tie(gram_got, small_got, w_out_new)

    gram_in = join_parts(gram_in, gram_got, square).reshape(3, ROW_BLOCK, ROW_BLOCK)
    grad_small = grad_small + small_got
    for bit in range(3, (lax.axis_size("dp") - 1).bit_length()):
        grad_small = grad_small + exchange(grad_small, "dp", bit)
    gram_in, grad_small, in_rows, in_got = tie(gram_in, grad_small, in_rows, in_got)
    gram_other = exchange(gram_in, "opt", 0)
    grad_in = join(in_rows, in_got, "dp", 0, 0)
    gram_other, grad_in = tie(gram_other, grad_in)
    owned_in, mom_in_new, w_in_new = newton_call(
        (gram_in, gram_other, grad_in, mom_turned, w_in.T), in_shapes, True, 0, 5
    )

    owned_small = own_slice(grad_small, small.shape[0], 0)
    adam_m_new = BETA_ONE * adam_m + (1.0 - BETA_ONE) * owned_small
    adam_v_new = BETA_TWO * adam_v + (1.0 - BETA_TWO) * owned_small * owned_small
    small_new = small * (1.0 - ADAM_RATE * DECAY) - ADAM_RATE * (
        adam_m_new / (1.0 - BETA_ONE**STEP)
    ) / (jnp.sqrt(adam_v_new / (1.0 - BETA_TWO**STEP)) + ADAM_EPS)
    return (
        block,
        grad_tokens,
        owned_in.T,
        owned_out,
        owned_small,
        mom_in_new.T,
        mom_out_new,
        w_in_new.T,
        w_out_new,
        small_new,
        adam_m_new,
        adam_v_new,
    )


def solution(mesh):
    in_specs = (
        P(("dp", "opt"), None),
        P(("dp", "opt"), None),
        P(None, "opt"),
        P("opt", None),
        P("opt"),
        P(None, "opt"),
        P("opt", None),
        P("opt"),
        P("opt"),
    )
    out_specs = (
        P(("dp", "opt"), None),
        P(("dp", "opt"), None),
        P(None, "opt"),
        P("opt", None),
        P("opt"),
        P(None, "opt"),
        P("opt", None),
        P(None, "opt"),
        P("opt", None),
        P("opt"),
        P("opt"),
        P("opt"),
    )
    return jax.shard_map(
        on_device, mesh=mesh, in_specs=in_specs, out_specs=out_specs, check_vma=False
    )
```

```python
import functools
import math

import jax
import jax.numpy as jnp
from jax import lax
from jax.experimental import pallas as pl
from jax.experimental.pallas import tpu as pltpu
from jax.sharding import PartitionSpec as P

D = 768
HEADS = 24
HEAD_CHANNELS = 64
STATE = 128
CONV = 4
SEQ_LEN = 1024
STEP = 10
D_INNER = 1536
CONV_CH = 1792
PROJ = 3352


EPSILON = 1e-05
COEF_A = 3.4445
COEF_B = -4.775
COEF_C = 2.0315
MOMENTUM = 0.95
MUON_RATE = 0.5
DECAY = 0.01
ADAM_RATE = 0.2
BETA_ONE = 0.9
BETA_TWO = 0.95
ADAM_EPS = 1e-08


SPAN = 128
CHUNKS = SEQ_LEN // SPAN
PAIRS = HEADS // 2
WIDTH = 2 * HEAD_CHANNELS
CONV_END = D_INNER + CONV_CH
PADDED = CONV_END + 128
TAIL = 8
VMEM_LIMIT = 56 * 1024 * 1024


def dot32(left, right):
    return jnp.dot(left, right, preferred_element_type=jnp.float32)


def dot_nt(left, right):
    return lax.dot_general(left, right, (((1,), (1,)), ((), ())), preferred_element_type=jnp.float32)


def dot_tn(left, right):
    return lax.dot_general(left, right, (((0,), (0,)), ((), ())), preferred_element_type=jnp.float32)


def halves(value):
    high = value.astype(jnp.bfloat16)
    return high, (value - high.astype(jnp.float32)).astype(jnp.bfloat16)


def sigmoid(value):
    return 0.5 * jnp.tanh(0.5 * value) + 0.5


def softplus(value):
    return jnp.maximum(value, 0.0) + jnp.log1p(jnp.exp(-jnp.abs(value)))


def fold_rows(value):
    return jnp.sum(value.reshape(value.shape[0] // 8, 8, value.shape[1]), axis=0)


def sum_first_row(ref):
    ref[0:1, :] = jnp.sum(ref[...], axis=0, keepdims=True)


def triangle(lower):
    rows = lax.broadcasted_iota(jnp.int32, (SPAN, SPAN), 0)
    cols = lax.broadcasted_iota(jnp.int32, (SPAN, SPAN), 1)
    return rows >= cols if lower else rows <= cols


def running_sum(mask, value):
    ones = jnp.where(mask, 1.0, 0.0).astype(jnp.bfloat16)
    high, rest = halves(value)
    low = (value - high.astype(jnp.float32) - rest.astype(jnp.float32)).astype(jnp.bfloat16)
    return dot32(ones, high) + (dot32(ones, rest) + dot32(ones, low))


def head_sums(value, reduce_mat):
    high, low = halves(value)
    return dot32(high, reduce_mat) + dot32(low, reduce_mat)


def step_factors(raw, dt_bias, rate, spread):
    step_size = softplus(raw + dt_bias)
    log_decay = running_sum(triangle(True), step_size * rate)
    last = log_decay[SPAN - 1 : SPAN, :]
    stacked = jnp.concatenate([step_size, jnp.exp(log_decay), jnp.exp(last - log_decay)], axis=0)
    high, low = halves(stacked)
    wide = dot32(jnp.concatenate([high, low], axis=1), spread)
    return step_size, log_decay, wide[:SPAN], wide[SPAN : 2 * SPAN], wide[2 * SPAN :]


def split_pair(value, first):
    return jnp.concatenate(
        [jnp.where(first, value, 0.0), jnp.where(first, 0.0, value)], axis=0
    ).astype(jnp.bfloat16)


def forward_kernel(
    proj_ref, back_ref, taps_ref, conv_bias_ref, gate_gain_ref, skip_ref, dt_bias_ref, rate_ref, spread_ref, reduce_ref,
    mixed_ref, active_ref, slope_ref, grad_scan_ref, grad_gate_ref, states_ref, inner_ref, gain_acc_ref, skip_acc_ref,
    window_ref, state_ref, skip_part_ref,
):
    f32, bf16 = jnp.float32, jnp.bfloat16

    @pl.when(pl.program_id(0) == 0)
    def start():
        window_ref[0:TAIL, :] = jnp.zeros((TAIL, CONV_CH), f32)
        state_ref[...] = jnp.zeros((STATE, D_INNER), f32)
        gain_acc_ref[...] = jnp.zeros((8, D_INNER), f32)
        skip_part_ref[...] = jnp.zeros((8, D_INNER), f32)

    window_ref[TAIL:, :] = proj_ref[:, D_INNER:CONV_END].astype(f32)
    conv_out = conv_bias_ref[...]
    for tap in range(CONV):
        start_row = TAIL - (CONV - 1) + tap
        conv_out = conv_out + taps_ref[tap : tap + 1, :] * window_ref[start_row : start_row + SPAN, :]
    window_ref[0:TAIL, :] = window_ref[SPAN:, :]
    part = sigmoid(conv_out)
    silu = conv_out * part
    active_ref[...] = silu.astype(bf16)
    slope_ref[...] = (part + silu * (1.0 - part)).astype(bf16)

    values = active_ref[:, :D_INNER].astype(f32)
    input_b = active_ref[:, D_INNER : D_INNER + STATE]
    output_c = active_ref[:, D_INNER + STATE :]
    step_size, log_decay, step_wide, decay_wide, end_wide = step_factors(
        proj_ref[:, CONV_END:].astype(f32), dt_bias_ref[...], rate_ref[...], spread_ref[...]
    )
    decay_rows = log_decay.T
    moved = step_wide * values
    state = state_ref[...]
    state_low = state.astype(bf16)
    states_ref[0] = state_low
    state_ref[...] = state * decay_wide[SPAN - 1 : SPAN, :] + dot_tn(input_b, (moved * end_wide).astype(bf16))
    scores = dot_nt(output_c, input_b)
    causal = triangle(True)
    first = lax.broadcasted_iota(jnp.int32, (SPAN, WIDTH), 1) < HEAD_CHANNELS
    pieces = []
    for pair in range(PAIRS):
        lanes = slice(pair * WIDTH, (pair + 1) * WIDTH)
        mixing = []
        for head in (2 * pair, 2 * pair + 1):
            differ = log_decay[:, head : head + 1] - decay_rows[head : head + 1, :]
            mixing.append((scores * jnp.exp(jnp.where(causal, differ, -1e30))).astype(bf16))
        pieces.append(dot32(jnp.concatenate(mixing, axis=1), split_pair(moved[:, lanes], first)))
    inner = jnp.concatenate(pieces, axis=1) + dot32(output_c, state_low) * decay_wide
    scanned = inner + skip_ref[...] * values

    gate_in = proj_ref[:, :D_INNER].astype(f32)
    part = sigmoid(gate_in)
    gate = gate_in * part
    gated = scanned * gate
    scale = lax.rsqrt(jnp.mean(gated * gated, axis=1, keepdims=True) + EPSILON)
    normal = gated * scale
    mixed_ref[...] = (normal * gate_gain_ref[...]).astype(bf16)
    back = back_ref[...].astype(f32)
    gain_acc_ref[...] += fold_rows(back * normal)
    back = back * gate_gain_ref[...]
    grad_gated = scale * (back - normal * jnp.mean(back * normal, axis=1, keepdims=True))
    grad_gate_ref[...] = (grad_gated * scanned * (part + gate * (1.0 - part))).astype(bf16)
    grad_scan_low = (grad_gated * gate).astype(bf16)
    grad_scan_ref[...] = grad_scan_low
    grad_scan = grad_scan_low.astype(f32)
    skip_part_ref[...] += fold_rows(grad_scan * values)
    inner_ref[...] = head_sums(grad_scan * inner, reduce_ref[...])

    @pl.when(pl.program_id(0) == CHUNKS - 1)
    def finish():
        sum_first_row(gain_acc_ref)
        skip_acc_ref[...] = head_sums(skip_part_ref[...], reduce_ref[...])
        sum_first_row(skip_acc_ref)


def backward_kernel(
    proj_ref, active_ref, slope_ref, grad_scan_ref, states_ref, inner_ref, taps_ref, skip_ref, dt_bias_ref, rate_ref,
    spread_ref, reduce_ref,
    grad_ref, taps_acc_ref, bias_acc_ref, dt_acc_ref, rate_acc_ref,
    window_ref, costate_ref,
):
    f32, bf16 = jnp.float32, jnp.bfloat16

    @pl.when(pl.program_id(0) == 0)
    def start():
        window_ref[SPAN:, :] = jnp.zeros((TAIL, CONV_CH), f32)
        costate_ref[...] = jnp.zeros((STATE, D_INNER), f32)
        taps_acc_ref[...] = jnp.zeros((CONV, 8, CONV_CH), f32)
        bias_acc_ref[...] = jnp.zeros((8, CONV_CH), f32)
        dt_acc_ref[...] = jnp.zeros((8, 128), f32)
        rate_acc_ref[...] = jnp.zeros((8, 128), f32)

    values = active_ref[:, :D_INNER].astype(f32)
    input_b = active_ref[:, D_INNER : D_INNER + STATE]
    output_c = active_ref[:, D_INNER + STATE :]
    raw = proj_ref[:, CONV_END:].astype(f32)
    rate = rate_ref[...]
    step_size, log_decay, step_wide, decay_wide, end_wide = step_factors(raw, dt_bias_ref[...], rate, spread_ref[...])
    decay_rows = log_decay.T
    moved = step_wide * values
    grad_scan_low = grad_scan_ref[...]
    grad_scan = grad_scan_low.astype(f32)
    scores = dot_nt(input_b, output_c)
    causal = triangle(False)
    first = lax.broadcasted_iota(jnp.int32, (SPAN, WIDTH), 1) < HEAD_CHANNELS
    grad_scores = jnp.zeros((SPAN, SPAN), f32)
    pieces = []
    for pair in range(PAIRS):
        lanes = slice(pair * WIDTH, (pair + 1) * WIDTH)
        moved_low = moved[:, lanes].astype(bf16)
        grad_pair = split_pair(grad_scan[:, lanes], first)
        grad_mixing = dot_nt(moved_low, grad_pair)
        mixing = []
        for place, head in enumerate((2 * pair, 2 * pair + 1)):
            differ = decay_rows[head : head + 1, :] - log_decay[:, head : head + 1]
            decay = jnp.exp(jnp.where(causal, differ, -1e30))
            mixing.append((scores * decay).astype(bf16))
            grad_scores = grad_scores + decay * grad_mixing[:, place * SPAN : (place + 1) * SPAN]
        pieces.append(dot32(jnp.concatenate(mixing, axis=1), grad_pair))
    grad_inner = jnp.concatenate(pieces, axis=1)

    costate = costate_ref[...]
    costate_low = costate.astype(bf16)
    states_low = states_ref[0]
    last_wide = decay_wide[SPAN - 1 : SPAN, :]
    kept = fold_rows(costate * states_low.astype(f32)) * last_wide
    grad_cross = dot32(input_b, costate_low) * end_wide
    grad_decayed = (grad_scan * decay_wide).astype(bf16)
    grad_scores_low = grad_scores.astype(bf16)
    grad_b = dot32(grad_scores_low, output_c) + dot_nt((moved * end_wide).astype(bf16), costate_low)
    grad_c = dot_tn(grad_scores_low, input_b) + dot_nt(grad_decayed, states_low)
    costate_ref[...] = costate * last_wide + dot_tn(output_c, grad_decayed)

    moved_round = moved.astype(bf16).astype(f32)
    grad_moved = grad_inner + grad_cross
    reduce_mat = reduce_ref[...]
    own = head_sums(moved_round * grad_inner, reduce_mat)
    crossing = dot32((moved * grad_cross).astype(bf16), reduce_mat)
    grad_step = dot32((values * grad_moved).astype(bf16), reduce_mat)
    keeping = jnp.sum(head_sums(kept, reduce_mat), axis=0, keepdims=True)
    grad_log = (
        running_sum(triangle(False), inner_ref[...] - own)
        + running_sum(triangle(True), crossing) - crossing
        + keeping
    )
    grad_raw = (grad_step + rate * grad_log) * sigmoid(raw + dt_bias_ref[...])
    rate_acc_ref[...] += fold_rows(step_size * grad_log)
    dt_acc_ref[...] += fold_rows(grad_raw)
    grad_ref[:, CONV_CH:] = grad_raw.astype(bf16)

    grad_values = step_wide * grad_moved + skip_ref[...] * grad_scan
    grad_active = jnp.concatenate([grad_values, grad_b, grad_c], axis=1)
    grad_conv = grad_active * slope_ref[...].astype(f32)
    bias_acc_ref[...] += fold_rows(grad_conv)
    window_ref[0:SPAN, :] = grad_conv
    conv_in = proj_ref[:, D_INNER:CONV_END].astype(f32)
    grad_in = jnp.zeros((SPAN, CONV_CH), f32)
    for tap in range(CONV):
        start_row = CONV - 1 - tap
        shifted = window_ref[start_row : start_row + SPAN, :]
        grad_in = grad_in + taps_ref[tap : tap + 1, :] * shifted
        taps_acc_ref[tap] += fold_rows(conv_in * shifted)
    grad_ref[:, :CONV_CH] = grad_in.astype(bf16)
    window_ref[SPAN:, :] = window_ref[0:TAIL, :]

    @pl.when(pl.program_id(0) == CHUNKS - 1)
    def finish():
        for tap in range(CONV):
            sum_first_row(taps_acc_ref.at[tap])
        sum_first_row(bias_acc_ref)
        sum_first_row(dt_acc_ref)
        sum_first_row(rate_acc_ref)


def head_matrices():
    spread = jnp.pad(jnp.repeat(jnp.eye(HEADS, dtype=jnp.bfloat16), HEAD_CHANNELS, axis=1), ((0, 128 - HEADS), (0, 0)))
    return jnp.concatenate([spread, spread], axis=0), spread.T


def row_block(width, order):
    return pl.BlockSpec((SPAN, width), lambda i: (order(i), 0))


def fixed_block(*shape):
    return pl.BlockSpec(shape, lambda i: (0,) * len(shape))


def state_block(order):
    return pl.BlockSpec((1, STATE, D_INNER), lambda i: (order(i), 0, 0))


def pad_heads(vector):
    return jnp.pad(vector, (0, 128 - HEADS))[None, :]


def mixer_forward(projected, back, taps, conv_bias, gate_gain, skip_wide, dt_bias, rate, spread, reduce_mat):
    f32, bf16 = jnp.float32, jnp.bfloat16
    order = lambda i: i
    rows = lambda width, kind: jax.ShapeDtypeStruct((SEQ_LEN, width), kind)
    return pl.pallas_call(
        forward_kernel,
        grid=(CHUNKS,),
        in_specs=[
            row_block(PADDED, order), row_block(D_INNER, order), fixed_block(CONV, CONV_CH), fixed_block(1, CONV_CH),
            fixed_block(1, D_INNER), fixed_block(1, D_INNER), fixed_block(1, 128), fixed_block(1, 128),
            fixed_block(256, D_INNER), fixed_block(D_INNER, 128),
        ],
        out_specs=[
            row_block(D_INNER, order), row_block(CONV_CH, order), row_block(CONV_CH, order), row_block(D_INNER, order),
            row_block(D_INNER, order), state_block(order), row_block(128, order), fixed_block(8, D_INNER),
            fixed_block(8, 128),
        ],
        out_shape=[
            rows(D_INNER, bf16), rows(CONV_CH, bf16), rows(CONV_CH, bf16), rows(D_INNER, bf16), rows(D_INNER, bf16),
            jax.ShapeDtypeStruct((CHUNKS, STATE, D_INNER), bf16), rows(128, f32),
            jax.ShapeDtypeStruct((8, D_INNER), f32), jax.ShapeDtypeStruct((8, 128), f32),
        ],
        scratch_shapes=[
            pltpu.VMEM((SPAN + TAIL, CONV_CH), f32), pltpu.VMEM((STATE, D_INNER), f32), pltpu.VMEM((8, D_INNER), f32),
        ],
        compiler_params=pltpu.CompilerParams(
            dimension_semantics=("arbitrary",), vmem_limit_bytes=VMEM_LIMIT
        ),
        cost_estimate=pl.CostEstimate(flops=8 * 10**9, bytes_accessed=32 * 10**6, transcendentals=10**7),
        name="mixer_forward",
    )(projected, back, taps, conv_bias, gate_gain, skip_wide, dt_bias, rate, spread, reduce_mat)


def mixer_backward(projected, active, slope, grad_scan, states, inner, taps, skip_wide, dt_bias, rate, spread, reduce_mat):
    f32, bf16 = jnp.float32, jnp.bfloat16
    order = lambda i: CHUNKS - 1 - i
    return pl.pallas_call(
        backward_kernel,
        grid=(CHUNKS,),
        in_specs=[
            row_block(PADDED, order), row_block(CONV_CH, order), row_block(CONV_CH, order), row_block(D_INNER, order),
            state_block(order), row_block(128, order), fixed_block(CONV, CONV_CH), fixed_block(1, D_INNER),
            fixed_block(1, 128), fixed_block(1, 128), fixed_block(256, D_INNER), fixed_block(D_INNER, 128),
        ],
        out_specs=[
            row_block(CONV_CH + 128, order), fixed_block(CONV, 8, CONV_CH), fixed_block(8, CONV_CH),
            fixed_block(8, 128), fixed_block(8, 128),
        ],
        out_shape=[
            jax.ShapeDtypeStruct((SEQ_LEN, CONV_CH + 128), bf16), jax.ShapeDtypeStruct((CONV, 8, CONV_CH), f32),
            jax.ShapeDtypeStruct((8, CONV_CH), f32), jax.ShapeDtypeStruct((8, 128), f32),
            jax.ShapeDtypeStruct((8, 128), f32),
        ],
        scratch_shapes=[pltpu.VMEM((SPAN + TAIL, CONV_CH), f32), pltpu.VMEM((STATE, D_INNER), f32)],
        compiler_params=pltpu.CompilerParams(
            dimension_semantics=("arbitrary",), vmem_limit_bytes=VMEM_LIMIT
        ),
        cost_estimate=pl.CostEstimate(flops=12 * 10**9, bytes_accessed=32 * 10**6, transcendentals=10**7),
        name="mixer_backward",
    )(projected, active, slope, grad_scan, states, inner, taps, skip_wide, dt_bias, rate, spread, reduce_mat)


ROW_BLOCK = 256
UPPER = [(0, 0), (0, 1), (0, 2), (1, 1), (1, 2), (2, 2)]


def gram_kernel(place_ref, push_ref, kept_ref, sent_ref):
    for place, (row, col) in enumerate(UPPER):
        rows = slice(row * ROW_BLOCK, (row + 1) * ROW_BLOCK)
        cols = slice(col * ROW_BLOCK, (col + 1) * ROW_BLOCK)
        tile = dot_tn(push_ref[:, rows], push_ref[:, cols])

        @pl.when(place_ref[0] == place // 3)
        def keep():
            kept_ref[place % 3] = tile

        @pl.when(place_ref[0] != place // 3)
        def send():
            sent_ref[place % 3] = tile


def gram_parts(push, name):
    tiles = jax.ShapeDtypeStruct((3, ROW_BLOCK, ROW_BLOCK), jnp.float32)
    hold = pl.BlockSpec(memory_space=pltpu.VMEM)
    return pl.pallas_call(
        gram_kernel,
        in_specs=[pl.BlockSpec(memory_space=pltpu.SMEM), hold],
        out_shape=[tiles, tiles],
        compiler_params=pltpu.CompilerParams(vmem_limit_bytes=VMEM_LIMIT),
        cost_estimate=pl.CostEstimate(
            flops=2 * D * push.size, bytes_accessed=2 * push.size, transcendentals=0
        ),
        name=name,
    )(core_place(), push)


def core_place():
    return side_of("opt", 0).astype(jnp.int32)[None]


def newton_kernel(transposed, rate, begin, end, place_ref, *refs):
    if begin == 0:
        (own_ref, other_ref), refs = refs[:2], refs[2:]
    else:
        (a_in_ref, r_in_ref, norm_ref), refs = refs[:3], refs[3:]
    if end == 5:
        (grad_ref, mom_ref, weight_ref, owned_ref, mom_new_ref, new_ref), refs = refs[:6], refs[6:]
    else:
        (a_out_ref, r_out_ref, norm_out_ref), refs = refs[:3], refs[3:]
    a_ref, t_ref, r_ref, e_ref, k_ref, f_ref, h_refs = refs
    f32, bf16 = jnp.float32, jnp.bfloat16
    blocks = [slice(i, i + ROW_BLOCK) for i in range(0, D, ROW_BLOCK)]
    size = 1.0 / D
    rows = lax.broadcasted_iota(jnp.int32, (ROW_BLOCK, ROW_BLOCK), 0)
    cols = lax.broadcasted_iota(jnp.int32, (ROW_BLOCK, ROW_BLOCK), 1)
    eye = rows == cols

    def whole_sum(value):
        return jnp.sum(jnp.sum(value, axis=0, keepdims=True), axis=1, keepdims=True)

    def trace_of(ref):
        return sum(whole_sum(jnp.where(eye, ref[block, block], 0.0)) for block in blocks)

    def shifted(value, row, amount):
        tiles = [value[:, block] for block in blocks]
        tiles[row] = tiles[row] - jnp.where(eye, amount, 0.0)
        return jnp.concatenate(tiles, axis=1)

    if begin == 0:
        core = place_ref[0] == 0
        for place, (row, col) in enumerate(UPPER):
            own, other = own_ref[place % 3], other_ref[place % 3]
            tile = jnp.where(core, own, other) if place < 3 else jnp.where(core, other, own)
            a_ref[blocks[row], blocks[col]] = tile
            if row != col:
                a_ref[blocks[col], blocks[row]] = tile.T
        total = trace_of(a_ref)
        norm = 1.0 / (jnp.sqrt(total) + 1e-07)
        scale = norm * norm
        for block in blocks:
            a_ref[block, :] = a_ref[block, :] * scale
        a_trace = total * scale
        r_trace = 0.0
    else:
        norm = norm_ref[...]
        a_ref[...] = a_in_ref[...]
        r_ref[...] = r_in_ref[...]
        a_trace, r_trace = trace_of(a_ref), trace_of(r_ref)
        for row, block in enumerate(blocks):
            h_refs[begin % 2, block, :] = shifted(r_ref[block, :], row, r_trace * size).astype(bf16)
    a_square = 0.0
    for row, block in enumerate(blocks):
        value = a_ref[block, :]
        a_square += fold_rows(value * value)
        e_ref[block, :] = shifted(value, row, a_trace * size).astype(bf16)
    a_square = whole_sum(a_square)
    for sweep in range(begin, end):
        mean, r_mean = a_trace * size, r_trace * size
        p_mean = (COEF_B * a_trace + COEF_C * a_square) * size
        lead = COEF_A + p_mean
        slope = COEF_B + 2.0 * COEF_C * mean
        with_a, with_r = 0.0, 0.0
        for row, block in enumerate(blocks):
            old = a_ref[block, :]
            poly = slope * old + COEF_C * dot32(e_ref[block, :], e_ref[...])
            poly = shifted(poly, row, COEF_C * mean * mean)
            with_a += fold_rows(poly * old)
            k_ref[block, :] = shifted(poly, row, p_mean).astype(bf16)
            if sweep == 0:
                r_ref[block, :] = shifted(poly, row, -COEF_A)
                h_refs[1, block, :] = shifted(poly, row, p_mean).astype(bf16)
            else:
                with_r += fold_rows(poly * r_ref[block, :])
        if sweep == 0:
            r_trace = lead * D
        else:
            r_trace = COEF_A * r_trace + whole_sum(with_r)
        t_trace = COEF_A * a_trace + whole_sum(with_a)
        with_k = 0.0
        for row, block in enumerate(blocks):
            part = k_ref[block, :].astype(f32)
            if sweep < 4:
                value = lead * a_ref[block, :] + mean * part + dot32(k_ref[block, :], e_ref[...])
                with_k += fold_rows(value * part)
                t_ref[block, :] = value
                f_ref[block, :] = shifted(value, row, t_trace * size).astype(bf16)
            if sweep > 0:
                value = lead * r_ref[block, :] + r_mean * part + dot32(k_ref[block, :], h_refs[sweep % 2])
                r_ref[block, :] = value
                h_refs[(sweep + 1) % 2, block, :] = shifted(value, row, r_trace * size).astype(bf16)
        if sweep < 4:
            a_trace = lead * t_trace + whole_sum(with_k)
            a_square = 0.0
            for row, block in enumerate(blocks):
                value = (
                    lead * t_ref[block, :]
                    + (t_trace * size) * k_ref[block, :].astype(f32)
                    + dot32(f_ref[block, :], k_ref[...])
                )
                a_square += fold_rows(value * value)
                a_ref[block, :] = value
                e_ref[block, :] = shifted(value, row, a_trace * size).astype(bf16)
            a_square = whole_sum(a_square)
    if end < 5:
        a_out_ref[...] = a_ref[...]
        r_out_ref[...] = r_ref[...]
        norm_out_ref[...] = norm
        return
    r_mean = r_trace * size
    step = norm * (MUON_RATE * rate)
    owned = grad_ref[0 : weight_ref.shape[0], :].astype(f32)
    owned_ref[...] = owned
    momentum = MOMENTUM * mom_ref[...] + owned
    mom_new_ref[...] = momentum
    push = owned + MOMENTUM * momentum
    dot = dot_nt if transposed else dot32
    ortho = r_mean * push + dot(push.astype(bf16), h_refs[1])
    new_ref[...] = weight_ref[...] * (1.0 - MUON_RATE * DECAY) - step * ortho


STATE_SHAPES = ((D, D), (D, D), (1, 1))


def nesterov(grad, momentum):
    grad = grad.astype(jnp.float32)
    return (grad + MOMENTUM * (MOMENTUM * momentum + grad)).astype(jnp.bfloat16)


def newton_call(inputs, outs, transposed, begin, end):
    rate = math.sqrt(max(1.0, PROJ / D)) if transposed else math.sqrt(max(1.0, D / D_INNER))
    whole = pltpu.VMEM((D, D), jnp.float32)
    half = pltpu.VMEM((D, D), jnp.bfloat16)
    hold = pl.BlockSpec(memory_space=pltpu.VMEM)
    return pl.pallas_call(
        functools.partial(newton_kernel, transposed, rate, begin, end),
        in_specs=[pl.BlockSpec(memory_space=pltpu.SMEM)] + [hold] * len(inputs),
        out_shape=[jax.ShapeDtypeStruct(shape, jnp.float32) for shape in outs],
        scratch_shapes=[whole, whole, whole, half, half, half, pltpu.VMEM((2, D, D), jnp.bfloat16)],
        compiler_params=pltpu.CompilerParams(vmem_limit_bytes=VMEM_LIMIT),
        cost_estimate=pl.CostEstimate(
            flops=2 * 5 * (end - begin) * 2 * D**3, bytes_accessed=10**7, transcendentals=0
        ),
        name=("newton_in" if transposed else "newton_out") + str(begin),
    )(core_place(), *inputs)


def own_slice(whole, width, along):
    return lax.dynamic_slice_in_dim(whole, lax.axis_index("opt") * width, width, along)


def exchange(value, axis, bit):
    count = lax.axis_size(axis)
    return lax.ppermute(value, axis, [(i, i ^ (1 << bit)) for i in range(count)])


def side_of(axis, bit):
    return (lax.axis_index(axis) >> bit) & 1


def cut(value, axis, bit, dim):
    half = value.shape[dim] // 2
    side = side_of(axis, bit)
    take = lambda index: lax.dynamic_slice_in_dim(value, index * half, half, dim)
    return take(side), take(1 - side)


def join(own, other, axis, bit, dim):
    lower = side_of(axis, bit) == 0
    return jnp.concatenate([jnp.where(lower, own, other), jnp.where(lower, other, own)], axis=dim)


AXES = ("dp", "opt")


def partner_index(bits, offset):
    across = lax.axis_size("opt")
    flip = 0
    for place, (axis, bit) in enumerate(reversed(bits)):
        if (offset >> place) & 1:
            flip ^= (1 << bit) * (across if axis == "dp" else 1)
    return [(i, i ^ flip) for i in range(lax.axis_size("dp") * across)]


def own_index(bits):
    index = 0
    for axis, bit in bits:
        index = 2 * index + side_of(axis, bit)
    return index


def send_parts(parts, bits):
    own = own_index(bits)
    take = lambda offset: lax.dynamic_index_in_dim(parts, own ^ offset, 0, keepdims=False)
    return take(0), [take(offset) for offset in range(1, 1 << len(bits))]


def swap_parts(parts, bits):
    if not isinstance(parts, list):
        parts = [parts] * ((1 << len(bits)) - 1)
    return [lax.ppermute(part, AXES, partner_index(bits, offset)) for offset, part in enumerate(parts, 1)]


def add_parts(kept, received):
    total = kept.astype(jnp.float32)
    for part in received:
        total = total + part.astype(jnp.float32)
    return total.astype(kept.dtype)


def join_parts(piece, received, bits):
    pieces = [piece] + received
    own = own_index(bits)
    places = []
    for place in range(1 << len(bits)):
        value = pieces[0]
        for offset in range(1, 1 << len(bits)):
            value = jnp.where(own ^ offset == place, pieces[offset], value)
        places.append(value)
    return jnp.stack(places)


def dp_groups():
    bits = [("dp", bit) for bit in range(1, (lax.axis_size("dp") - 1).bit_length())]
    return [bits[i : i + 2] for i in range(0, len(bits), 2)]


def split_rows(piece, bits):
    parts = piece.reshape(piece.shape[0], 1 << len(bits), -1, piece.shape[-1]).swapaxes(0, 1)
    return send_parts(parts, bits)


def merge_rows(piece, received, bits):
    parts = join_parts(piece, received, bits).swapaxes(0, 1)
    return parts.reshape(piece.shape[0], -1, piece.shape[-1])


def tie(*values):
    return lax.optimization_barrier(values)


def fetch_shards(shard):
    across = exchange(shard, "opt", 1)
    return [shard, exchange(shard, "opt", 0), across, exchange(across, "opt", 0)]


def in_order(pieces):
    core, far = side_of("opt", 0) == 0, side_of("opt", 1) == 0
    near = [jnp.where(core, pieces[0], pieces[1]), jnp.where(core, pieces[1], pieces[0])]
    other = [jnp.where(core, pieces[2], pieces[3]), jnp.where(core, pieces[3], pieces[2])]
    low = [jnp.where(far, n, o) for n, o in zip(near, other)]
    high = [jnp.where(far, o, n) for n, o in zip(near, other)]
    return jnp.concatenate(low + high, axis=0)


COLUMN_BLOCK = 384
SHARD = PROJ // 4
SHARD_LANES = 896
SHARD_ROWS = 896


def project_kernel(
    place_ref, tokens_ref, gain_ref, own_ref, core_ref, across_ref, last_ref,
    proj_ref, hidden_ref, weight_out_ref, scale_ref,
    shards_ref, weight_ref, normed_ref, sems,
):
    step = pl.program_id(0)

    @pl.when(step == 0)
    def start():
        copies = [
            pltpu.make_async_copy(ref, shards_ref.at[place_ref[0] ^ place], sems.at[place])
            for place, ref in enumerate((own_ref, core_ref, across_ref, last_ref))
        ]
        for copy in copies:
            copy.start()
        inflow = tokens_ref[...].astype(jnp.float32)
        scale = lax.rsqrt(jnp.mean(inflow * inflow, axis=1, keepdims=True) + EPSILON)
        normed_ref[...] = (inflow * scale * gain_ref[...]).astype(jnp.bfloat16)
        hidden_ref[...] = normed_ref[...]
        scale_ref[...] = jnp.broadcast_to(scale, scale_ref.shape)
        for copy in copies:
            copy.wait()
        weight_ref[:, PROJ - PROJ % 128 :] = jnp.zeros((D, PADDED - PROJ + PROJ % 128), jnp.bfloat16)
        for place in range(4):
            weight_ref[:, place * SHARD : (place + 1) * SHARD] = shards_ref[place, :, :SHARD]

    block = weight_ref[:, pl.ds(pl.multiple_of(step * COLUMN_BLOCK, 128), COLUMN_BLOCK)]
    weight_out_ref[...] = block
    proj_ref[...] = dot32(normed_ref[...], block).astype(jnp.bfloat16)


def project(tokens, gain_vec, pieces):
    length = tokens.shape[0]
    bf16 = jnp.bfloat16
    hold = pl.BlockSpec(memory_space=pl.ANY)
    return pl.pallas_call(
        project_kernel,
        grid=(PADDED // COLUMN_BLOCK,),
        in_specs=[pl.BlockSpec(memory_space=pltpu.SMEM), fixed_block(length, D), fixed_block(1, D)] + [hold] * 4,
        out_specs=[
            pl.BlockSpec((length, COLUMN_BLOCK), lambda i: (0, i)),
            fixed_block(length, D),
            pl.BlockSpec((D, COLUMN_BLOCK), lambda i: (0, i)),
            fixed_block(length, 128),
        ],
        out_shape=[
            jax.ShapeDtypeStruct((length, PADDED), bf16), jax.ShapeDtypeStruct((length, D), bf16),
            jax.ShapeDtypeStruct((D, PADDED), bf16), jax.ShapeDtypeStruct((length, 128), jnp.float32),
        ],
        scratch_shapes=[
            pltpu.VMEM((4, D, SHARD_LANES), bf16), pltpu.VMEM((D, PADDED), bf16), pltpu.VMEM((length, D), bf16),
            pltpu.SemaphoreType.DMA((4,)),
        ],
        compiler_params=pltpu.CompilerParams(
            dimension_semantics=("arbitrary",), vmem_limit_bytes=VMEM_LIMIT
        ),
        cost_estimate=pl.CostEstimate(
            flops=2 * length * D * PADDED, bytes_accessed=22 * 10**6, transcendentals=0
        ),
        name="project",
    )(lax.axis_index("opt").astype(jnp.int32)[None], tokens, gain_vec[None, :], *pieces)


def weight_grad_kernel(kept, place_ref, hidden_ref, gate_ref, conv_ref, out_ref, whole_ref):
    for core in range(2):
        for far in range(2):
            shard = 2 * far + (core if kept else 1 - core)
            first = shard * SHARD // 128 * 128
            last = min(-(-(shard + 1) * SHARD // 128) * 128, PADDED)
            start = shard * SHARD - first

            @pl.when((place_ref[0] == core) & (pl.program_id(0) == far))
            def work():
                for ref, begin, end in ((gate_ref, 0, D_INNER), (conv_ref, D_INNER, PADDED)):
                    low, high = max(begin, first), min(end, last)
                    if low < high:
                        whole_ref[low - first : high - first, :] = dot_tn(
                            ref[:, low - begin : high - begin], hidden_ref[...]
                        )
                block = whole_ref[start : start + SHARD_ROWS, :]
                rows = lax.broadcasted_iota(jnp.int32, (SHARD_ROWS, D), 0)
                out_ref[0] = jnp.where(rows < SHARD, block, 0.0).astype(jnp.bfloat16)


def weight_grad(hidden, gate, conv, kept):
    length = hidden.shape[0]
    return pl.pallas_call(
        functools.partial(weight_grad_kernel, kept),
        grid=(2,),
        in_specs=[
            pl.BlockSpec(memory_space=pltpu.SMEM), fixed_block(length, D), fixed_block(length, D_INNER),
            fixed_block(length, PADDED - D_INNER),
        ],
        out_specs=pl.BlockSpec((1, SHARD_ROWS, D), lambda i: (i, 0, 0)),
        out_shape=jax.ShapeDtypeStruct((2, SHARD_ROWS, D), jnp.bfloat16),
        scratch_shapes=[pltpu.VMEM((SHARD_ROWS + 128, D), jnp.float32)],
        compiler_params=pltpu.CompilerParams(
            dimension_semantics=("arbitrary",), vmem_limit_bytes=VMEM_LIMIT
        ),
        cost_estimate=pl.CostEstimate(
            flops=length * D * PADDED, bytes_accessed=11 * 10**6, transcendentals=0
        ),
        name="weight_grad_own" if kept else "weight_grad_other",
    )(core_place(), hidden, gate, conv)


def on_device(tokens, cotangent, w_in, w_out, small, mom_in, mom_out, adam_m, adam_v):
    bf16, f32 = jnp.bfloat16, jnp.float32
    groups = dp_groups()

    own_in = jnp.pad(w_in.astype(bf16), ((0, 0), (0, SHARD_LANES - SHARD)))
    across_in = exchange(own_in, "opt", 1)
    core_in = exchange(own_in, "opt", 0)
    params = in_order(fetch_shards(small.astype(bf16))).astype(f32)
    sections = [D, D + D_INNER, D + D_INNER + CONV * CONV_CH]
    sections += [sections[-1] + CONV_CH + place * HEADS for place in range(3)]
    gain_vec, gate_gain, taps, conv_bias, dt_bias, a_log, skip_gain = jnp.split(params, sections)
    rate = -jnp.exp(a_log)
    spread, reduce_mat = head_matrices()
    fixed = (jnp.repeat(skip_gain, HEAD_CHANNELS)[None, :], pad_heads(dt_bias), pad_heads(rate), spread, reduce_mat)
    own_out = w_out.astype(bf16)
    prepared = (gain_vec, gate_gain[None, :], taps.reshape(CONV, CONV_CH), conv_bias[None, :], fixed)
    across_in, core_in, prepared, own_out = tie(across_in, core_in, prepared, own_out)
    gain_vec, gate_gain, taps, conv_bias, fixed = prepared
    last_in = exchange(across_in, "opt", 0)
    last_in, own_out = tie(last_in, own_out)
    across_out, core_out = exchange(own_out, "opt", 1), exchange(own_out, "opt", 0)
    projected, hidden, w_pad, scale = project(tokens, gain_vec, [own_in, core_in, across_in, last_in])
    across_out, core_out, projected, cotangent = tie(across_out, core_out, projected, cotangent)
    w_out_b = in_order([own_out, core_out, across_out, exchange(across_out, "opt", 0)])
    grad_mixed = dot_nt(cotangent, w_out_b).astype(bf16)

    mixed, active, slope, grad_scan, grad_gate, states, inner, gain_acc, skip_acc = mixer_forward(
        projected, grad_mixed, taps, conv_bias, gate_gain, *fixed
    )

    inflow = tokens.astype(f32)
    square = [("opt", 1), ("dp", 0)]
    out_kept, out_sent = cut(dot_tn(mixed, cotangent).astype(bf16).reshape(2, 2, -1, D), "opt", 0, 1)
    out_got = exchange(out_sent, "opt", 0)
    out_kept, out_sent = send_parts((out_kept + out_got).reshape(4, -1, D), square)
    grad_scan, out_sent = tie(grad_scan, out_sent)
    out_got = swap_parts(out_sent, square)
    grad_conv, taps_acc, bias_acc, dt_acc, rate_acc = mixer_backward(
        projected, active, slope, grad_scan, states, inner, taps, *fixed
    )
    grad_conv, out_got = tie(grad_conv, out_got)
    out_kept, out_sent = split_rows(add_parts(out_kept, out_got)[None], groups[0])
    grad_conv, out_sent = tie(grad_conv, out_sent)
    out_got = swap_parts(out_sent, groups[0])
    sent = weight_grad(hidden, grad_gate, grad_conv, False)
    grad_conv, sent, out_got = tie(grad_conv, sent, out_got)

    in_got = exchange(sent, "opt", 0)
    kept = weight_grad(hidden, grad_gate, grad_conv, True)
    out_piece = add_parts(out_kept, out_got)
    for bits in groups[1:]:
        out_kept, out_sent = split_rows(out_piece, bits)
        out_piece = add_parts(out_kept, swap_parts(out_sent, bits))
    for bits in reversed(groups[1:]):
        out_piece = merge_rows(out_piece, swap_parts(out_piece, bits), bits)
    out_piece = out_piece[0]
    out_got = exchange(out_piece, "dp", 0)
    in_got, out_got, kept = tie(in_got, out_got, kept)
    pair_in = kept + in_got
    half = D // 2
    one_kept, one_sent = cut(pair_in[:, :, :half], "opt", 1, 0)
    two_kept, two_sent = cut(pair_in[:, :, half:], "dp", 0, 1)
    out_rows = jnp.concatenate([out_piece, out_got], axis=0)
    one_sent, two_sent, out_rows, grad_gate = tie(one_sent, two_sent, out_rows, grad_gate)

    one_got, two_got = exchange(one_sent, "opt", 1), exchange(two_sent, "dp", 0)
    out_got = swap_parts(out_rows, groups[0])
    grad_hidden = dot_nt(grad_gate, w_pad[:, :D_INNER]) + dot_nt(grad_conv, w_pad[:, D_INNER:])
    one_got, two_got, out_got, grad_hidden = tie(one_got, two_got, out_got, grad_hidden)

    one_kept, one_sent = cut((one_kept + one_got)[0], "dp", 0, 0)
    two_kept, two_sent = cut(two_kept + two_got, "opt", 1, 0)
    one_sent, two_sent, out_rows, out_got = tie(one_sent, two_sent, out_rows, out_got)
    one_got, two_got = exchange(one_sent, "dp", 0), exchange(two_sent, "opt", 1)
    grad_out = join_parts(out_rows, out_got, groups[0]).reshape(1 << len(groups[0]), 2, -1, D)
    lower = side_of("dp", 0) == 0
    near, far = grad_out[:, 0].reshape(-1, D), grad_out[:, 1].reshape(-1, D)
    grad_out = jnp.concatenate([jnp.where(lower, near, far), jnp.where(lower, far, near)], axis=0)
    push_out = nesterov(grad_out, mom_out)
    gram_kept, gram_sent = gram_parts(push_out, "gram_out")
    gram_got = exchange(gram_sent, "opt", 0)
    one_got, two_got, gram_got = tie(one_got, two_got, gram_got)

    gram_out = gram_kept + gram_got
    in_piece = jnp.concatenate([one_kept + one_got, (two_kept + two_got)[0]], axis=1)[None]
    in_kept, in_sent = split_rows(in_piece, groups[0])
    mom_turned = mom_in.T
    in_sent, gram_out, grad_hidden, mom_turned = tie(in_sent, gram_out, grad_hidden, mom_turned)
    in_got = swap_parts(in_sent, groups[0])
    gram_got = exchange(gram_out, "opt", 1)
    normal = inflow * scale[:, :1]
    grad_gain = jnp.sum(normal * grad_hidden, axis=0)
    grad_normal = grad_hidden * gain_vec
    grad_tokens = cotangent.astype(f32) + scale[:, :1] * (
        grad_normal - normal * jnp.mean(grad_normal * normal, axis=1, keepdims=True)
    )
    grad_small = jnp.concatenate([
        grad_gain,
        gain_acc[0],
        taps_acc[:, 0].reshape(-1),
        bias_acc[0],
        dt_acc[0, :HEADS],
        rate_acc[0, :HEADS] * rate,
        skip_acc[0, :HEADS],
    ])
    every = [("dp", 0)] + [bit for bits in groups for bit in bits]
    width = SHARD_ROWS >> len(every)
    mom_padded = jnp.pad(mom_turned, ((0, SHARD_ROWS - SHARD), (0, 0)))
    mom_piece = lax.dynamic_slice_in_dim(mom_padded, own_index(every) * width, width, 0)
    in_got, grad_tokens, grad_small, mom_piece = tie(in_got, grad_tokens, grad_small, mom_piece)

    in_piece = add_parts(in_kept, in_got)
    for bits in groups[1:]:
        in_kept, in_sent = split_rows(in_piece, bits)
        in_piece = add_parts(in_kept, swap_parts(in_sent, bits))
    gram_kept, gram_sent = gram_parts(nesterov(in_piece[0], mom_piece), "gram_in")
    for bits in reversed(groups[1:]):
        in_piece = merge_rows(in_piece, swap_parts(in_piece, bits), bits)
    gram_sent, in_piece, grad_small, gram_got = tie(gram_sent, in_piece, grad_small, gram_got)
    in_got = swap_parts(in_piece, groups[0])
    gram_in = exchange(gram_sent, "opt", 0)
    small_got = exchange(grad_small, "opt", 0)
    gram_out = gram_out + gram_got
    gram_other = exchange(gram_out, "opt", 0)
    gram_in, small_got, gram_other = tie(gram_in, small_got, gram_other)

    gram_kept, gram_sent = send_parts((gram_kept + gram_in).reshape(4, -1, ROW_BLOCK), square)
    grad_small = grad_small + small_got
    gram_sent, grad_small, gram_out = tie(gram_sent, grad_small, gram_out)
    gram_got = swap_parts(gram_sent, square)
    small_got = exchange(grad_small, "opt", 1)
    state = newton_call((gram_out, gram_other), STATE_SHAPES, False, 0, 2)
    gram_got, small_got, state = tie(gram_got, small_got, state)

    gram_in = add_parts(gram_kept, gram_got)
    grad_small = grad_small + small_got
    gram_in, grad_small, in_got = tie(gram_in, grad_small, in_got)
    gram_got = exchange(gram_in, "dp", 1)
    small_got = exchange(grad_small, "dp", 0)
    in_rows = merge_rows(in_piece, in_got, groups[0])[0]
    gram_got, small_got, in_rows = tie(gram_got, small_got, in_rows)

    gram_in = gram_in + gram_got
    grad_small = grad_small + small_got
    gram_in, grad_small, in_rows, state = tie(gram_in, grad_small, in_rows, state)
    gram_got = exchange(gram_in, "dp", 2)
    in_got = exchange(in_rows, "dp", 0)
    small_got = exchange(grad_small, "dp", 1)
    out_shapes, in_shapes = (w_out.shape,) * 3, (mom_turned.shape,) * 3
    owned_out, mom_out_new, w_out_new = newton_call((*state, grad_out, mom_out, w_out), out_shapes, False, 2, 5)
    gram_got, small_got, w_out_new, in_got = tie(gram_got, small_got, w_out_new, in_got)

    gram_in = gram_in + gram_got
    grad_small = grad_small + small_got
    for bit in range(3, (lax.axis_size("dp") - 1).bit_length()):
        gram_in = gram_in + exchange(gram_in, "dp", bit)
    gram_in, grad_small, mixed = tie(gram_in, grad_small, mixed)
    gram_got = swap_parts(gram_in, square)
    small_got = exchange(grad_small, "dp", 2)
    block = (inflow + dot32(mixed, w_out_b)).astype(bf16)
    gram_got, small_got, block = tie(gram_got, small_got, block)

    gram_in = join_parts(gram_in, gram_got, square).reshape(3, ROW_BLOCK, ROW_BLOCK)
    grad_small = grad_small + small_got
    for bit in range(3, (lax.axis_size("dp") - 1).bit_length()):
        grad_small = grad_small + exchange(grad_small, "dp", bit)
    gram_in, grad_small, in_rows, in_got = tie(gram_in, grad_small, in_rows, in_got)
    gram_other = exchange(gram_in, "opt", 0)
    grad_in = join(in_rows, in_got, "dp", 0, 0)
    gram_other, grad_in = tie(gram_other, grad_in)
    owned_in, mom_in_new, w_in_new = newton_call(
        (gram_in, gram_other, grad_in, mom_turned, w_in.T), in_shapes, True, 0, 5
    )

    owned_small = own_slice(grad_small, small.shape[0], 0)
    adam_m_new = BETA_ONE * adam_m + (1.0 - BETA_ONE) * owned_small
    adam_v_new = BETA_TWO * adam_v + (1.0 - BETA_TWO) * owned_small * owned_small
    small_new = small * (1.0 - ADAM_RATE * DECAY) - ADAM_RATE * (
        adam_m_new / (1.0 - BETA_ONE**STEP)
    ) / (jnp.sqrt(adam_v_new / (1.0 - BETA_TWO**STEP)) + ADAM_EPS)
    return (
        block,
        grad_tokens,
        owned_in.T,
        owned_out,
        owned_small,
        mom_in_new.T,
        mom_out_new,
        w_in_new.T,
        w_out_new,
        small_new,
        adam_m_new,
        adam_v_new,
    )


def solution(mesh):
    in_specs = (
        P(("dp", "opt"), None),
        P(("dp", "opt"), None),
        P(None, "opt"),
        P("opt", None),
        P("opt"),
        P(None, "opt"),
        P("opt", None),
        P("opt"),
        P("opt"),
    )
    out_specs = (
        P(("dp", "opt"), None),
        P(("dp", "opt"), None),
        P(None, "opt"),
        P("opt", None),
        P("opt"),
        P(None, "opt"),
        P("opt", None),
        P(None, "opt"),
        P("opt", None),
        P("opt"),
        P("opt"),
        P("opt"),
    )
    return jax.shard_map(
        on_device, mesh=mesh, in_specs=in_specs, out_specs=out_specs, check_vma=False
    )
```

```python
import functools
import math

import jax
import jax.numpy as jnp
from jax import lax
from jax.experimental import pallas as pl
from jax.experimental.pallas import tpu as pltpu
from jax.sharding import PartitionSpec as P

D = 768
HEADS = 24
HEAD_CHANNELS = 64
STATE = 128
CONV = 4
SEQ_LEN = 1024
STEP = 10
D_INNER = 1536
CONV_CH = 1792
PROJ = 3352


EPSILON = 1e-05
COEF_A = 3.4445
COEF_B = -4.775
COEF_C = 2.0315
MOMENTUM = 0.95
MUON_RATE = 0.5
DECAY = 0.01
ADAM_RATE = 0.2
BETA_ONE = 0.9
BETA_TWO = 0.95
ADAM_EPS = 1e-08


SPAN = 128
CHUNKS = SEQ_LEN // SPAN
PAIRS = HEADS // 2
WIDTH = 2 * HEAD_CHANNELS
CONV_END = D_INNER + CONV_CH
PADDED = CONV_END + 128
TAIL = 8
VMEM_LIMIT = 56 * 1024 * 1024


def dot32(left, right):
    return jnp.dot(left, right, preferred_element_type=jnp.float32)


def dot_nt(left, right):
    return lax.dot_general(left, right, (((1,), (1,)), ((), ())), preferred_element_type=jnp.float32)


def dot_tn(left, right):
    return lax.dot_general(left, right, (((0,), (0,)), ((), ())), preferred_element_type=jnp.float32)


def halves(value):
    high = value.astype(jnp.bfloat16)
    return high, (value - high.astype(jnp.float32)).astype(jnp.bfloat16)


def sigmoid(value):
    return 0.5 * jnp.tanh(0.5 * value) + 0.5


def softplus(value):
    return jnp.maximum(value, 0.0) + jnp.log1p(jnp.exp(-jnp.abs(value)))


def fold_rows(value):
    return jnp.sum(value.reshape(value.shape[0] // 8, 8, value.shape[1]), axis=0)


def sum_first_row(ref):
    ref[0:1, :] = jnp.sum(ref[...], axis=0, keepdims=True)


def triangle(lower):
    rows = lax.broadcasted_iota(jnp.int32, (SPAN, SPAN), 0)
    cols = lax.broadcasted_iota(jnp.int32, (SPAN, SPAN), 1)
    return rows >= cols if lower else rows <= cols


def running_sum(mask, value):
    ones = jnp.where(mask, 1.0, 0.0).astype(jnp.bfloat16)
    high, rest = halves(value)
    low = (value - high.astype(jnp.float32) - rest.astype(jnp.float32)).astype(jnp.bfloat16)
    wide = dot32(ones, jnp.concatenate([high, rest, low], axis=1))
    return wide[:, :128] + (wide[:, 128:256] + wide[:, 256:])


def head_sums(reduce_mat, exact, rough=()):
    parts = [part for value in exact for part in halves(value)] + [value.astype(jnp.bfloat16) for value in rough]
    sums = dot32(jnp.concatenate(parts, axis=0), reduce_mat)
    results, at = [], 0
    for value in exact:
        rows = value.shape[0]
        results.append(sums[at : at + rows] + sums[at + rows : at + 2 * rows])
        at += 2 * rows
    for value in rough:
        results.append(sums[at : at + value.shape[0]])
        at += value.shape[0]
    return results


def step_factors(raw, dt_bias, rate, spread):
    step_size = softplus(raw + dt_bias)
    log_decay = running_sum(triangle(True), step_size * rate)
    last = log_decay[SPAN - 1 : SPAN, :]
    stacked = jnp.concatenate([step_size, jnp.exp(log_decay), jnp.exp(last - log_decay)], axis=0)
    high, low = halves(stacked)
    wide = dot32(jnp.concatenate([high, low], axis=1), spread)
    return step_size, log_decay, wide[:SPAN], wide[SPAN : 2 * SPAN], wide[2 * SPAN :]


def split_pair(value, first):
    return jnp.concatenate(
        [jnp.where(first, value, 0.0), jnp.where(first, 0.0, value)], axis=0
    ).astype(jnp.bfloat16)


def forward_kernel(
    proj_ref, back_ref, taps_ref, conv_bias_ref, gate_gain_ref, skip_ref, dt_bias_ref, rate_ref, spread_ref, reduce_ref,
    mixed_ref, active_ref, slope_ref, grad_scan_ref, grad_gate_ref, states_ref, inner_ref, gain_acc_ref, skip_acc_ref,
    window_ref, state_ref, skip_part_ref,
):
    f32, bf16 = jnp.float32, jnp.bfloat16

    @pl.when(pl.program_id(0) == 0)
    def start():
        window_ref[0:TAIL, :] = jnp.zeros((TAIL, CONV_CH), f32)
        state_ref[...] = jnp.zeros((STATE, D_INNER), f32)
        gain_acc_ref[...] = jnp.zeros((8, D_INNER), f32)
        skip_part_ref[...] = jnp.zeros((8, D_INNER), f32)

    window_ref[TAIL:, :] = proj_ref[:, D_INNER:CONV_END].astype(f32)
    conv_out = conv_bias_ref[...]
    for tap in range(CONV):
        start_row = TAIL - (CONV - 1) + tap
        conv_out = conv_out + taps_ref[tap : tap + 1, :] * window_ref[start_row : start_row + SPAN, :]
    window_ref[0:TAIL, :] = window_ref[SPAN:, :]
    part = sigmoid(conv_out)
    silu = conv_out * part
    active_ref[...] = silu.astype(bf16)
    slope_ref[...] = (part + silu * (1.0 - part)).astype(bf16)

    values = active_ref[:, :D_INNER].astype(f32)
    input_b = active_ref[:, D_INNER : D_INNER + STATE]
    output_c = active_ref[:, D_INNER + STATE :]
    step_size, log_decay, step_wide, decay_wide, end_wide = step_factors(
        proj_ref[:, CONV_END:].astype(f32), dt_bias_ref[...], rate_ref[...], spread_ref[...]
    )
    decay_rows = log_decay.T
    moved = step_wide * values
    state = state_ref[...]
    state_low = state.astype(bf16)
    states_ref[0] = state_low
    state_ref[...] = state * decay_wide[SPAN - 1 : SPAN, :] + dot_tn(input_b, (moved * end_wide).astype(bf16))
    scores = dot_nt(output_c, input_b)
    causal = triangle(True)
    first = lax.broadcasted_iota(jnp.int32, (SPAN, WIDTH), 1) < HEAD_CHANNELS
    pieces = []
    for pair in range(PAIRS):
        lanes = slice(pair * WIDTH, (pair + 1) * WIDTH)
        mixing = []
        for head in (2 * pair, 2 * pair + 1):
            differ = log_decay[:, head : head + 1] - decay_rows[head : head + 1, :]
            mixing.append((scores * jnp.exp(jnp.where(causal, differ, -1e30))).astype(bf16))
        pieces.append(dot32(jnp.concatenate(mixing, axis=1), split_pair(moved[:, lanes], first)))
    inner = jnp.concatenate(pieces, axis=1) + dot32(output_c, state_low) * decay_wide
    scanned = inner + skip_ref[...] * values

    gate_in = proj_ref[:, :D_INNER].astype(f32)
    part = sigmoid(gate_in)
    gate = gate_in * part
    gated = scanned * gate
    scale = lax.rsqrt(jnp.mean(gated * gated, axis=1, keepdims=True) + EPSILON)
    normal = gated * scale
    mixed_ref[...] = (normal * gate_gain_ref[...]).astype(bf16)
    back = back_ref[...].astype(f32)
    gain_acc_ref[...] += fold_rows(back * normal)
    back = back * gate_gain_ref[...]
    grad_gated = scale * (back - normal * jnp.mean(back * normal, axis=1, keepdims=True))
    grad_gate_ref[...] = (grad_gated * scanned * (part + gate * (1.0 - part))).astype(bf16)
    grad_scan_low = (grad_gated * gate).astype(bf16)
    grad_scan_ref[...] = grad_scan_low
    grad_scan = grad_scan_low.astype(f32)
    skip_part_ref[...] += fold_rows(grad_scan * values)
    (inner_ref[...],) = head_sums(reduce_ref[...], [grad_scan * inner])

    @pl.when(pl.program_id(0) == CHUNKS - 1)
    def finish():
        sum_first_row(gain_acc_ref)
        skip_acc_ref[...] = head_sums(reduce_ref[...], [jnp.concatenate([skip_part_ref[...]] * 2, axis=0)])[0][:8]
        sum_first_row(skip_acc_ref)


def backward_kernel(
    proj_ref, active_ref, slope_ref, grad_scan_ref, states_ref, inner_ref, taps_ref, skip_ref, dt_bias_ref, rate_ref,
    spread_ref, reduce_ref,
    grad_ref, taps_acc_ref, bias_acc_ref, dt_acc_ref, rate_acc_ref,
    window_ref, costate_ref,
):
    f32, bf16 = jnp.float32, jnp.bfloat16

    @pl.when(pl.program_id(0) == 0)
    def start():
        window_ref[SPAN:, :] = jnp.zeros((TAIL, CONV_CH), f32)
        costate_ref[...] = jnp.zeros((STATE, D_INNER), f32)
        taps_acc_ref[...] = jnp.zeros((CONV, 8, CONV_CH), f32)
        bias_acc_ref[...] = jnp.zeros((8, CONV_CH), f32)
        dt_acc_ref[...] = jnp.zeros((8, 128), f32)
        rate_acc_ref[...] = jnp.zeros((8, 128), f32)

    values = active_ref[:, :D_INNER].astype(f32)
    input_b = active_ref[:, D_INNER : D_INNER + STATE]
    output_c = active_ref[:, D_INNER + STATE :]
    raw = proj_ref[:, CONV_END:].astype(f32)
    rate = rate_ref[...]
    step_size, log_decay, step_wide, decay_wide, end_wide = step_factors(raw, dt_bias_ref[...], rate, spread_ref[...])
    decay_rows = log_decay.T
    moved = step_wide * values
    grad_scan_low = grad_scan_ref[...]
    grad_scan = grad_scan_low.astype(f32)
    scores = dot_nt(input_b, output_c)
    causal = triangle(False)
    first = lax.broadcasted_iota(jnp.int32, (SPAN, WIDTH), 1) < HEAD_CHANNELS
    grad_scores = jnp.zeros((SPAN, SPAN), f32)
    pieces = []
    for pair in range(PAIRS):
        lanes = slice(pair * WIDTH, (pair + 1) * WIDTH)
        moved_low = moved[:, lanes].astype(bf16)
        grad_pair = split_pair(grad_scan[:, lanes], first)
        grad_mixing = dot_nt(moved_low, grad_pair)
        mixing = []
        for place, head in enumerate((2 * pair, 2 * pair + 1)):
            differ = decay_rows[head : head + 1, :] - log_decay[:, head : head + 1]
            decay = jnp.exp(jnp.where(causal, differ, -1e30))
            mixing.append((scores * decay).astype(bf16))
            grad_scores = grad_scores + decay * grad_mixing[:, place * SPAN : (place + 1) * SPAN]
        pieces.append(dot32(jnp.concatenate(mixing, axis=1), grad_pair))
    grad_inner = jnp.concatenate(pieces, axis=1)

    costate = costate_ref[...]
    costate_low = costate.astype(bf16)
    states_low = states_ref[0]
    last_wide = decay_wide[SPAN - 1 : SPAN, :]
    kept = fold_rows(costate * states_low.astype(f32)) * last_wide
    grad_cross = dot32(input_b, costate_low) * end_wide
    grad_decayed = (grad_scan * decay_wide).astype(bf16)
    grad_scores_low = grad_scores.astype(bf16)
    grad_b = dot32(grad_scores_low, output_c) + dot_nt((moved * end_wide).astype(bf16), costate_low)
    grad_c = dot_tn(grad_scores_low, input_b) + dot_nt(grad_decayed, states_low)
    costate_ref[...] = costate * last_wide + dot_tn(output_c, grad_decayed)

    moved_round = moved.astype(bf16).astype(f32)
    grad_moved = grad_inner + grad_cross
    kept = jnp.concatenate([kept, jnp.zeros_like(kept)], axis=0)
    own, keeping, crossing, grad_step = head_sums(
        reduce_ref[...], [moved_round * grad_inner, kept], [moved * grad_cross, values * grad_moved]
    )
    keeping = jnp.sum(keeping, axis=0, keepdims=True)
    grad_log = (
        running_sum(triangle(False), inner_ref[...] - own)
        + running_sum(triangle(True), crossing) - crossing
        + keeping
    )
    grad_raw = (grad_step + rate * grad_log) * sigmoid(raw + dt_bias_ref[...])
    rate_acc_ref[...] += fold_rows(step_size * grad_log)
    dt_acc_ref[...] += fold_rows(grad_raw)
    grad_ref[:, CONV_CH:] = grad_raw.astype(bf16)

    grad_values = step_wide * grad_moved + skip_ref[...] * grad_scan
    grad_active = jnp.concatenate([grad_values, grad_b, grad_c], axis=1)
    grad_conv = grad_active * slope_ref[...].astype(f32)
    bias_acc_ref[...] += fold_rows(grad_conv)
    window_ref[0:SPAN, :] = grad_conv
    conv_in = proj_ref[:, D_INNER:CONV_END].astype(f32)
    grad_in = jnp.zeros((SPAN, CONV_CH), f32)
    for tap in range(CONV):
        start_row = CONV - 1 - tap
        shifted = window_ref[start_row : start_row + SPAN, :]
        grad_in = grad_in + taps_ref[tap : tap + 1, :] * shifted
        taps_acc_ref[tap] += fold_rows(conv_in * shifted)
    grad_ref[:, :CONV_CH] = grad_in.astype(bf16)
    window_ref[SPAN:, :] = window_ref[0:TAIL, :]

    @pl.when(pl.program_id(0) == CHUNKS - 1)
    def finish():
        for tap in range(CONV):
            sum_first_row(taps_acc_ref.at[tap])
        sum_first_row(bias_acc_ref)
        sum_first_row(dt_acc_ref)
        sum_first_row(rate_acc_ref)


def head_matrices():
    spread = jnp.pad(jnp.repeat(jnp.eye(HEADS, dtype=jnp.bfloat16), HEAD_CHANNELS, axis=1), ((0, 128 - HEADS), (0, 0)))
    return jnp.concatenate([spread, spread], axis=0), spread.T


def row_block(width, order):
    return pl.BlockSpec((SPAN, width), lambda i: (order(i), 0))


def fixed_block(*shape):
    return pl.BlockSpec(shape, lambda i: (0,) * len(shape))


def state_block(order):
    return pl.BlockSpec((1, STATE, D_INNER), lambda i: (order(i), 0, 0))


def pad_heads(vector):
    return jnp.pad(vector, (0, 128 - HEADS))[None, :]


def mixer_forward(projected, back, taps, conv_bias, gate_gain, skip_wide, dt_bias, rate, spread, reduce_mat):
    f32, bf16 = jnp.float32, jnp.bfloat16
    order = lambda i: i
    rows = lambda width, kind: jax.ShapeDtypeStruct((SEQ_LEN, width), kind)
    return pl.pallas_call(
        forward_kernel,
        grid=(CHUNKS,),
        in_specs=[
            row_block(PADDED, order), row_block(D_INNER, order), fixed_block(CONV, CONV_CH), fixed_block(1, CONV_CH),
            fixed_block(1, D_INNER), fixed_block(1, D_INNER), fixed_block(1, 128), fixed_block(1, 128),
            fixed_block(256, D_INNER), fixed_block(D_INNER, 128),
        ],
        out_specs=[
            row_block(D_INNER, order), row_block(CONV_CH, order), row_block(CONV_CH, order), row_block(D_INNER, order),
            row_block(D_INNER, order), state_block(order), row_block(128, order), fixed_block(8, D_INNER),
            fixed_block(8, 128),
        ],
        out_shape=[
            rows(D_INNER, bf16), rows(CONV_CH, bf16), rows(CONV_CH, bf16), rows(D_INNER, bf16), rows(D_INNER, bf16),
            jax.ShapeDtypeStruct((CHUNKS, STATE, D_INNER), bf16), rows(128, f32),
            jax.ShapeDtypeStruct((8, D_INNER), f32), jax.ShapeDtypeStruct((8, 128), f32),
        ],
        scratch_shapes=[
            pltpu.VMEM((SPAN + TAIL, CONV_CH), f32), pltpu.VMEM((STATE, D_INNER), f32), pltpu.VMEM((8, D_INNER), f32),
        ],
        compiler_params=pltpu.CompilerParams(
            dimension_semantics=("arbitrary",), vmem_limit_bytes=VMEM_LIMIT
        ),
        cost_estimate=pl.CostEstimate(flops=8 * 10**9, bytes_accessed=32 * 10**6, transcendentals=10**7),
        name="mixer_forward",
    )(projected, back, taps, conv_bias, gate_gain, skip_wide, dt_bias, rate, spread, reduce_mat)


def mixer_backward(projected, active, slope, grad_scan, states, inner, taps, skip_wide, dt_bias, rate, spread, reduce_mat):
    f32, bf16 = jnp.float32, jnp.bfloat16
    order = lambda i: CHUNKS - 1 - i
    return pl.pallas_call(
        backward_kernel,
        grid=(CHUNKS,),
        in_specs=[
            row_block(PADDED, order), row_block(CONV_CH, order), row_block(CONV_CH, order), row_block(D_INNER, order),
            state_block(order), row_block(128, order), fixed_block(CONV, CONV_CH), fixed_block(1, D_INNER),
            fixed_block(1, 128), fixed_block(1, 128), fixed_block(256, D_INNER), fixed_block(D_INNER, 128),
        ],
        out_specs=[
            row_block(CONV_CH + 128, order), fixed_block(CONV, 8, CONV_CH), fixed_block(8, CONV_CH),
            fixed_block(8, 128), fixed_block(8, 128),
        ],
        out_shape=[
            jax.ShapeDtypeStruct((SEQ_LEN, CONV_CH + 128), bf16), jax.ShapeDtypeStruct((CONV, 8, CONV_CH), f32),
            jax.ShapeDtypeStruct((8, CONV_CH), f32), jax.ShapeDtypeStruct((8, 128), f32),
            jax.ShapeDtypeStruct((8, 128), f32),
        ],
        scratch_shapes=[pltpu.VMEM((SPAN + TAIL, CONV_CH), f32), pltpu.VMEM((STATE, D_INNER), f32)],
        compiler_params=pltpu.CompilerParams(
            dimension_semantics=("arbitrary",), vmem_limit_bytes=VMEM_LIMIT
        ),
        cost_estimate=pl.CostEstimate(flops=12 * 10**9, bytes_accessed=32 * 10**6, transcendentals=10**7),
        name="mixer_backward",
    )(projected, active, slope, grad_scan, states, inner, taps, skip_wide, dt_bias, rate, spread, reduce_mat)


ROW_BLOCK = 256
UPPER = [(0, 0), (0, 1), (0, 2), (1, 1), (1, 2), (2, 2)]


def gram_kernel(place_ref, push_ref, kept_ref, sent_ref):
    for place, (row, col) in enumerate(UPPER):
        rows = slice(row * ROW_BLOCK, (row + 1) * ROW_BLOCK)
        cols = slice(col * ROW_BLOCK, (col + 1) * ROW_BLOCK)
        tile = dot_tn(push_ref[:, rows], push_ref[:, cols])

        @pl.when(place_ref[0] == place // 3)
        def keep():
            kept_ref[place % 3] = tile

        @pl.when(place_ref[0] != place // 3)
        def send():
            sent_ref[place % 3] = tile


def gram_parts(push, name):
    tiles = jax.ShapeDtypeStruct((3, ROW_BLOCK, ROW_BLOCK), jnp.float32)
    hold = pl.BlockSpec(memory_space=pltpu.VMEM)
    return pl.pallas_call(
        gram_kernel,
        in_specs=[pl.BlockSpec(memory_space=pltpu.SMEM), hold],
        out_shape=[tiles, tiles],
        compiler_params=pltpu.CompilerParams(vmem_limit_bytes=VMEM_LIMIT),
        cost_estimate=pl.CostEstimate(
            flops=2 * D * push.size, bytes_accessed=2 * push.size, transcendentals=0
        ),
        name=name,
    )(core_place(), push)


def core_place():
    return side_of("opt", 0).astype(jnp.int32)[None]


def newton_kernel(transposed, rate, begin, end, place_ref, *refs):
    if begin == 0:
        (own_ref, other_ref), refs = refs[:2], refs[2:]
    else:
        (a_in_ref, r_in_ref, norm_ref), refs = refs[:3], refs[3:]
    if end == 5:
        (grad_ref, mom_ref, weight_ref, owned_ref, mom_new_ref, new_ref), refs = refs[:6], refs[6:]
    else:
        (a_out_ref, r_out_ref, norm_out_ref), refs = refs[:3], refs[3:]
    a_ref, t_ref, r_ref, e_ref, k_ref, f_ref, h_refs = refs
    f32, bf16 = jnp.float32, jnp.bfloat16
    blocks = [slice(i, i + ROW_BLOCK) for i in range(0, D, ROW_BLOCK)]
    size = 1.0 / D
    rows = lax.broadcasted_iota(jnp.int32, (ROW_BLOCK, ROW_BLOCK), 0)
    cols = lax.broadcasted_iota(jnp.int32, (ROW_BLOCK, ROW_BLOCK), 1)
    eye = rows == cols

    def whole_sum(value):
        return jnp.sum(jnp.sum(value, axis=0, keepdims=True), axis=1, keepdims=True)

    def trace_of(ref):
        return sum(whole_sum(jnp.where(eye, ref[block, block], 0.0)) for block in blocks)

    def shifted(value, col, amount):
        tiles = [value[block, :] for block in blocks]
        tiles[col] = tiles[col] - jnp.where(eye, amount, 0.0)
        return jnp.concatenate(tiles, axis=0)

    if begin == 0:
        core = place_ref[0] == 0
        for place, (row, col) in enumerate(UPPER):
            own, other = own_ref[place % 3], other_ref[place % 3]
            tile = jnp.where(core, own, other) if place < 3 else jnp.where(core, other, own)
            a_ref[blocks[row], blocks[col]] = tile
            if row != col:
                a_ref[blocks[col], blocks[row]] = tile.T
        total = trace_of(a_ref)
        norm = 1.0 / (jnp.sqrt(total) + 1e-07)
        scale = norm * norm
        for block in blocks:
            a_ref[block, :] = a_ref[block, :] * scale
        a_trace = total * scale
        r_trace = 0.0
    else:
        norm = norm_ref[...]
        a_ref[...] = a_in_ref[...]
        r_ref[...] = r_in_ref[...]
        a_trace, r_trace = trace_of(a_ref), trace_of(r_ref)
        for col, block in enumerate(blocks):
            h_refs[begin % 2, :, block] = shifted(r_ref[:, block], col, r_trace * size).astype(bf16)
    a_square = 0.0
    for col, block in enumerate(blocks):
        value = a_ref[:, block]
        a_square += fold_rows(value * value)
        e_ref[:, block] = shifted(value, col, a_trace * size).astype(bf16)
    a_square = whole_sum(a_square)
    for sweep in range(begin, end):
        mean, r_mean = a_trace * size, r_trace * size
        p_mean = (COEF_B * a_trace + COEF_C * a_square) * size
        lead = COEF_A + p_mean
        slope = COEF_B + 2.0 * COEF_C * mean
        with_a, with_r = 0.0, 0.0
        for col, block in enumerate(blocks):
            old = a_ref[:, block]
            poly = slope * old + COEF_C * dot32(e_ref[...], e_ref[:, block])
            poly = shifted(poly, col, COEF_C * mean * mean)
            with_a += fold_rows(poly * old)
            rest = shifted(poly, col, p_mean).astype(bf16)
            k_ref[:, block] = rest
            if sweep == 0:
                r_ref[:, block] = shifted(poly, col, -COEF_A)
                h_refs[1, :, block] = rest
            else:
                with_r += fold_rows(poly * r_ref[:, block])
        if sweep == 0:
            r_trace = lead * D
        else:
            r_trace = COEF_A * r_trace + whole_sum(with_r)
        t_trace = COEF_A * a_trace + whole_sum(with_a)
        with_k = 0.0
        for col, block in enumerate(blocks):
            part = k_ref[:, block].astype(f32)
            if sweep < 4:
                value = lead * a_ref[:, block] + mean * part + dot32(k_ref[...], e_ref[:, block])
                with_k += fold_rows(value * part)
                t_ref[:, block] = value
                f_ref[:, block] = shifted(value, col, t_trace * size).astype(bf16)
            if sweep > 0:
                value = lead * r_ref[:, block] + r_mean * part + dot32(k_ref[...], h_refs[sweep % 2, :, block])
                r_ref[:, block] = value
                h_refs[(sweep + 1) % 2, :, block] = shifted(value, col, r_trace * size).astype(bf16)
        if sweep < 4:
            a_trace = lead * t_trace + whole_sum(with_k)
            a_square = 0.0
            for col, block in enumerate(blocks):
                value = (
                    lead * t_ref[:, block]
                    + (t_trace * size) * k_ref[:, block].astype(f32)
                    + dot32(f_ref[...], k_ref[:, block])
                )
                a_square += fold_rows(value * value)
                a_ref[:, block] = value
                e_ref[:, block] = shifted(value, col, a_trace * size).astype(bf16)
            a_square = whole_sum(a_square)
    if end < 5:
        a_out_ref[...] = a_ref[...]
        r_out_ref[...] = r_ref[...]
        norm_out_ref[...] = norm
        return
    r_mean = r_trace * size
    step = norm * (MUON_RATE * rate)
    owned = grad_ref[0 : weight_ref.shape[0], :].astype(f32)
    owned_ref[...] = owned
    momentum = MOMENTUM * mom_ref[...] + owned
    mom_new_ref[...] = momentum
    push = owned + MOMENTUM * momentum
    dot = dot_nt if transposed else dot32
    ortho = r_mean * push + dot(push.astype(bf16), h_refs[1])
    new_ref[...] = weight_ref[...] * (1.0 - MUON_RATE * DECAY) - step * ortho


STATE_SHAPES = ((D, D), (D, D), (1, 1))


def nesterov(grad, momentum):
    grad = grad.astype(jnp.float32)
    return (grad + MOMENTUM * (MOMENTUM * momentum + grad)).astype(jnp.bfloat16)


def newton_call(inputs, outs, transposed, begin, end):
    rate = math.sqrt(max(1.0, PROJ / D)) if transposed else math.sqrt(max(1.0, D / D_INNER))
    whole = pltpu.VMEM((D, D), jnp.float32)
    half = pltpu.VMEM((D, D), jnp.bfloat16)
    hold = pl.BlockSpec(memory_space=pltpu.VMEM)
    return pl.pallas_call(
        functools.partial(newton_kernel, transposed, rate, begin, end),
        in_specs=[pl.BlockSpec(memory_space=pltpu.SMEM)] + [hold] * len(inputs),
        out_shape=[jax.ShapeDtypeStruct(shape, jnp.float32) for shape in outs],
        scratch_shapes=[whole, whole, whole, half, half, half, pltpu.VMEM((2, D, D), jnp.bfloat16)],
        compiler_params=pltpu.CompilerParams(vmem_limit_bytes=VMEM_LIMIT),
        cost_estimate=pl.CostEstimate(
            flops=2 * 5 * (end - begin) * 2 * D**3, bytes_accessed=10**7, transcendentals=0
        ),
        name=("newton_in" if transposed else "newton_out") + str(begin),
    )(core_place(), *inputs)


def own_slice(whole, width, along):
    return lax.dynamic_slice_in_dim(whole, lax.axis_index("opt") * width, width, along)


def exchange(value, axis, bit):
    count = lax.axis_size(axis)
    return lax.ppermute(value, axis, [(i, i ^ (1 << bit)) for i in range(count)])


def side_of(axis, bit):
    return (lax.axis_index(axis) >> bit) & 1


def cut(value, axis, bit, dim):
    half = value.shape[dim] // 2
    side = side_of(axis, bit)
    take = lambda index: lax.dynamic_slice_in_dim(value, index * half, half, dim)
    return take(side), take(1 - side)


def join(own, other, axis, bit, dim):
    lower = side_of(axis, bit) == 0
    return jnp.concatenate([jnp.where(lower, own, other), jnp.where(lower, other, own)], axis=dim)


AXES = ("dp", "opt")


def partner_index(bits, offset):
    across = lax.axis_size("opt")
    flip = 0
    for place, (axis, bit) in enumerate(reversed(bits)):
        if (offset >> place) & 1:
            flip ^= (1 << bit) * (across if axis == "dp" else 1)
    return [(i, i ^ flip) for i in range(lax.axis_size("dp") * across)]


def own_index(bits):
    index = 0
    for axis, bit in bits:
        index = 2 * index + side_of(axis, bit)
    return index


def send_parts(parts, bits):
    own = own_index(bits)
    take = lambda offset: lax.dynamic_index_in_dim(parts, own ^ offset, 0, keepdims=False)
    return take(0), [take(offset) for offset in range(1, 1 << len(bits))]


def swap_parts(parts, bits):
    if not isinstance(parts, list):
        parts = [parts] * ((1 << len(bits)) - 1)
    return [lax.ppermute(part, AXES, partner_index(bits, offset)) for offset, part in enumerate(parts, 1)]


def add_parts(kept, received):
    total = kept.astype(jnp.float32)
    for part in received:
        total = total + part.astype(jnp.float32)
    return total.astype(kept.dtype)


def join_parts(piece, received, bits):
    pieces = [piece] + received
    own = own_index(bits)
    places = []
    for place in range(1 << len(bits)):
        value = pieces[0]
        for offset in range(1, 1 << len(bits)):
            value = jnp.where(own ^ offset == place, pieces[offset], value)
        places.append(value)
    return jnp.stack(places)


def dp_groups():
    bits = [("dp", bit) for bit in range(1, (lax.axis_size("dp") - 1).bit_length())]
    return [bits[i : i + 2] for i in range(0, len(bits), 2)]


def split_rows(piece, bits):
    parts = piece.reshape(piece.shape[0], 1 << len(bits), -1, piece.shape[-1]).swapaxes(0, 1)
    return send_parts(parts, bits)


def merge_rows(piece, received, bits):
    parts = join_parts(piece, received, bits).swapaxes(0, 1)
    return parts.reshape(piece.shape[0], -1, piece.shape[-1])


def tie(*values):
    return lax.optimization_barrier(values)


def fetch_shards(shard):
    across = exchange(shard, "opt", 1)
    return [shard, exchange(shard, "opt", 0), across, exchange(across, "opt", 0)]


def in_order(pieces):
    core, far = side_of("opt", 0) == 0, side_of("opt", 1) == 0
    near = [jnp.where(core, pieces[0], pieces[1]), jnp.where(core, pieces[1], pieces[0])]
    other = [jnp.where(core, pieces[2], pieces[3]), jnp.where(core, pieces[3], pieces[2])]
    low = [jnp.where(far, n, o) for n, o in zip(near, other)]
    high = [jnp.where(far, o, n) for n, o in zip(near, other)]
    return jnp.concatenate(low + high, axis=0)


COLUMN_BLOCK = 384
SHARD = PROJ // 4
SHARD_LANES = 896
SHARD_ROWS = 896


def project_kernel(
    place_ref, hidden_ref, own_ref, core_ref, across_ref, last_ref,
    proj_ref, weight_out_ref,
    shards_ref, weight_ref, sems,
):
    step = pl.program_id(0)

    @pl.when(step == 0)
    def start():
        copies = [
            pltpu.make_async_copy(ref, shards_ref.at[place_ref[0] ^ place], sems.at[place])
            for place, ref in enumerate((own_ref, core_ref, across_ref, last_ref))
        ]
        for copy in copies:
            copy.start()
        for copy in copies:
            copy.wait()
        weight_ref[:, PROJ - PROJ % 128 :] = jnp.zeros((D, PADDED - PROJ + PROJ % 128), jnp.bfloat16)
        for place in range(4):
            weight_ref[:, place * SHARD : (place + 1) * SHARD] = shards_ref[place, :, :SHARD]

    block = weight_ref[:, pl.ds(pl.multiple_of(step * COLUMN_BLOCK, 128), COLUMN_BLOCK)]
    weight_out_ref[...] = block
    proj_ref[...] = dot32(hidden_ref[...], block).astype(jnp.bfloat16)


def project(hidden, pieces):
    length = hidden.shape[0]
    bf16 = jnp.bfloat16
    hold = pl.BlockSpec(memory_space=pl.ANY)
    return pl.pallas_call(
        project_kernel,
        grid=(PADDED // COLUMN_BLOCK,),
        in_specs=[pl.BlockSpec(memory_space=pltpu.SMEM), fixed_block(length, D)] + [hold] * 4,
        out_specs=[
            pl.BlockSpec((length, COLUMN_BLOCK), lambda i: (0, i)),
            pl.BlockSpec((D, COLUMN_BLOCK), lambda i: (0, i)),
        ],
        out_shape=[jax.ShapeDtypeStruct((length, PADDED), bf16), jax.ShapeDtypeStruct((D, PADDED), bf16)],
        scratch_shapes=[
            pltpu.VMEM((4, D, SHARD_LANES), bf16), pltpu.VMEM((D, PADDED), bf16), pltpu.SemaphoreType.DMA((4,)),
        ],
        compiler_params=pltpu.CompilerParams(
            dimension_semantics=("arbitrary",), vmem_limit_bytes=VMEM_LIMIT
        ),
        cost_estimate=pl.CostEstimate(
            flops=2 * length * D * PADDED, bytes_accessed=20 * 10**6, transcendentals=0
        ),
        name="project",
    )(lax.axis_index("opt").astype(jnp.int32)[None], hidden, *pieces)


def weight_grad_kernel(kept, place_ref, hidden_ref, gate_ref, conv_ref, out_ref, whole_ref):
    for core in range(2):
        for far in range(2):
            shard = 2 * far + (core if kept else 1 - core)
            first = shard * SHARD // 128 * 128
            last = min(-(-(shard + 1) * SHARD // 128) * 128, PADDED)
            start = shard * SHARD - first

            @pl.when((place_ref[0] == core) & (pl.program_id(0) == far))
            def work():
                for ref, begin, end in ((gate_ref, 0, D_INNER), (conv_ref, D_INNER, PADDED)):
                    low, high = max(begin, first), min(end, last)
                    if low < high:
                        whole_ref[low - first : high - first, :] = dot_tn(
                            ref[:, low - begin : high - begin], hidden_ref[...]
                        )
                block = whole_ref[start : start + SHARD_ROWS, :]
                rows = lax.broadcasted_iota(jnp.int32, (SHARD_ROWS, D), 0)
                out_ref[0] = jnp.where(rows < SHARD, block, 0.0).astype(jnp.bfloat16)


def weight_grad(hidden, gate, conv, kept):
    length = hidden.shape[0]
    return pl.pallas_call(
        functools.partial(weight_grad_kernel, kept),
        grid=(2,),
        in_specs=[
            pl.BlockSpec(memory_space=pltpu.SMEM), fixed_block(length, D), fixed_block(length, D_INNER),
            fixed_block(length, PADDED - D_INNER),
        ],
        out_specs=pl.BlockSpec((1, SHARD_ROWS, D), lambda i: (i, 0, 0)),
        out_shape=jax.ShapeDtypeStruct((2, SHARD_ROWS, D), jnp.bfloat16),
        scratch_shapes=[pltpu.VMEM((SHARD_ROWS + 128, D), jnp.float32)],
        compiler_params=pltpu.CompilerParams(
            dimension_semantics=("arbitrary",), vmem_limit_bytes=VMEM_LIMIT
        ),
        cost_estimate=pl.CostEstimate(
            flops=length * D * PADDED, bytes_accessed=11 * 10**6, transcendentals=0
        ),
        name="weight_grad_own" if kept else "weight_grad_other",
    )(core_place(), hidden, gate, conv)


def on_device(tokens, cotangent, w_in, w_out, small, mom_in, mom_out, adam_m, adam_v):
    bf16, f32 = jnp.bfloat16, jnp.float32
    groups = dp_groups()

    own_in = jnp.pad(w_in.astype(bf16), ((0, 0), (0, SHARD_LANES - SHARD)))
    across_in = exchange(own_in, "opt", 1)
    core_in = exchange(own_in, "opt", 0)
    params = in_order(fetch_shards(small.astype(bf16))).astype(f32)
    sections = [D, D + D_INNER, D + D_INNER + CONV * CONV_CH]
    sections += [sections[-1] + CONV_CH + place * HEADS for place in range(3)]
    gain_vec, gate_gain, taps, conv_bias, dt_bias, a_log, skip_gain = jnp.split(params, sections)
    rate = -jnp.exp(a_log)
    spread, reduce_mat = head_matrices()
    fixed = (jnp.repeat(skip_gain, HEAD_CHANNELS)[None, :], pad_heads(dt_bias), pad_heads(rate), spread, reduce_mat)
    own_out = w_out.astype(bf16)
    inflow = tokens.astype(f32)
    scale = lax.rsqrt(jnp.mean(inflow * inflow, axis=1, keepdims=True) + EPSILON)
    hidden = (inflow * scale * gain_vec).astype(bf16)
    prepared = (hidden, scale, gain_vec, gate_gain[None, :], taps.reshape(CONV, CONV_CH), conv_bias[None, :], fixed)
    across_in, core_in, prepared, own_out = tie(across_in, core_in, prepared, own_out)
    hidden, scale, gain_vec, gate_gain, taps, conv_bias, fixed = prepared
    last_in = exchange(across_in, "opt", 0)
    last_in, own_out = tie(last_in, own_out)
    across_out, core_out = exchange(own_out, "opt", 1), exchange(own_out, "opt", 0)
    projected, w_pad = project(hidden, [own_in, core_in, across_in, last_in])
    across_out, core_out, projected, cotangent = tie(across_out, core_out, projected, cotangent)
    w_out_b = in_order([own_out, core_out, across_out, exchange(across_out, "opt", 0)])
    grad_mixed = dot_nt(cotangent, w_out_b).astype(bf16)

    mixed, active, slope, grad_scan, grad_gate, states, inner, gain_acc, skip_acc = mixer_forward(
        projected, grad_mixed, taps, conv_bias, gate_gain, *fixed
    )

    square = [("opt", 1), ("dp", 0)]
    out_kept, out_sent = cut(dot_tn(mixed, cotangent).astype(bf16).reshape(2, 2, -1, D), "opt", 0, 1)
    out_got = exchange(out_sent, "opt", 0)
    out_kept, out_sent = send_parts((out_kept + out_got).reshape(4, -1, D), square)
    grad_scan, out_sent = tie(grad_scan, out_sent)
    out_got = swap_parts(out_sent, square)
    grad_conv, taps_acc, bias_acc, dt_acc, rate_acc = mixer_backward(
        projected, active, slope, grad_scan, states, inner, taps, *fixed
    )
    grad_conv, out_got = tie(grad_conv, out_got)
    out_kept, out_sent = split_rows(add_parts(out_kept, out_got)[None], groups[0])
    grad_conv, out_sent = tie(grad_conv, out_sent)
    out_got = swap_parts(out_sent, groups[0])
    sent = weight_grad(hidden, grad_gate, grad_conv, False)
    grad_conv, sent, out_got = tie(grad_conv, sent, out_got)

    in_got = exchange(sent, "opt", 0)
    kept = weight_grad(hidden, grad_gate, grad_conv, True)
    out_piece = add_parts(out_kept, out_got)
    for bits in groups[1:]:
        out_kept, out_sent = split_rows(out_piece, bits)
        out_piece = add_parts(out_kept, swap_parts(out_sent, bits))
    for bits in reversed(groups[1:]):
        out_piece = merge_rows(out_piece, swap_parts(out_piece, bits), bits)
    out_piece = out_piece[0]
    out_got = exchange(out_piece, "dp", 0)
    in_got, out_got, kept = tie(in_got, out_got, kept)
    pair_in = kept + in_got
    half = D // 2
    one_kept, one_sent = cut(pair_in[:, :, :half], "opt", 1, 0)
    two_kept, two_sent = cut(pair_in[:, :, half:], "dp", 0, 1)
    out_rows = jnp.concatenate([out_piece, out_got], axis=0)
    one_sent, two_sent, out_rows, grad_gate = tie(one_sent, two_sent, out_rows, grad_gate)

    one_got, two_got = exchange(one_sent, "opt", 1), exchange(two_sent, "dp", 0)
    out_got = swap_parts(out_rows, groups[0])
    grad_hidden = dot_nt(grad_gate, w_pad[:, :D_INNER]) + dot_nt(grad_conv, w_pad[:, D_INNER:])
    one_got, two_got, out_got, grad_hidden = tie(one_got, two_got, out_got, grad_hidden)

    one_kept, one_sent = cut((one_kept + one_got)[0], "dp", 0, 0)
    two_kept, two_sent = cut(two_kept + two_got, "opt", 1, 0)
    one_sent, two_sent, out_rows, out_got = tie(one_sent, two_sent, out_rows, out_got)
    one_got, two_got = exchange(one_sent, "dp", 0), exchange(two_sent, "opt", 1)
    grad_out = join_parts(out_rows, out_got, groups[0]).reshape(1 << len(groups[0]), 2, -1, D)
    lower = side_of("dp", 0) == 0
    near, far = grad_out[:, 0].reshape(-1, D), grad_out[:, 1].reshape(-1, D)
    grad_out = jnp.concatenate([jnp.where(lower, near, far), jnp.where(lower, far, near)], axis=0)
    push_out = nesterov(grad_out, mom_out)
    gram_kept, gram_sent = gram_parts(push_out, "gram_out")
    gram_got = exchange(gram_sent, "opt", 0)
    one_got, two_got, gram_got = tie(one_got, two_got, gram_got)

    gram_out = gram_kept + gram_got
    in_piece = jnp.concatenate([one_kept + one_got, (two_kept + two_got)[0]], axis=1)[None]
    in_kept, in_sent = split_rows(in_piece, groups[0])
    mom_turned = mom_in.T
    in_sent, gram_out, grad_hidden, mom_turned = tie(in_sent, gram_out, grad_hidden, mom_turned)
    in_got = swap_parts(in_sent, groups[0])
    gram_got = exchange(gram_out, "opt", 1)
    normal = inflow * scale
    grad_gain = jnp.sum(normal * grad_hidden, axis=0)
    grad_normal = grad_hidden * gain_vec
    grad_tokens = cotangent.astype(f32) + scale * (
        grad_normal - normal * jnp.mean(grad_normal * normal, axis=1, keepdims=True)
    )
    grad_small = jnp.concatenate([
        grad_gain,
        gain_acc[0],
        taps_acc[:, 0].reshape(-1),
        bias_acc[0],
        dt_acc[0, :HEADS],
        rate_acc[0, :HEADS] * rate,
        skip_acc[0, :HEADS],
    ])
    every = [("dp", 0)] + [bit for bits in groups for bit in bits]
    width = SHARD_ROWS >> len(every)
    mom_padded = jnp.pad(mom_turned, ((0, SHARD_ROWS - SHARD), (0, 0)))
    mom_piece = lax.dynamic_slice_in_dim(mom_padded, own_index(every) * width, width, 0)
    in_got, grad_tokens, grad_small, mom_piece = tie(in_got, grad_tokens, grad_small, mom_piece)

    in_piece = add_parts(in_kept, in_got)
    for bits in groups[1:]:
        in_kept, in_sent = split_rows(in_piece, bits)
        in_piece = add_parts(in_kept, swap_parts(in_sent, bits))
    gram_kept, gram_sent = gram_parts(nesterov(in_piece[0], mom_piece), "gram_in")
    for bits in reversed(groups[1:]):
        in_piece = merge_rows(in_piece, swap_parts(in_piece, bits), bits)
    gram_sent, in_piece, grad_small, gram_got = tie(gram_sent, in_piece, grad_small, gram_got)
    in_got = swap_parts(in_piece, groups[0])
    gram_in = exchange(gram_sent, "opt", 0)
    small_got = exchange(grad_small, "opt", 0)
    gram_out = gram_out + gram_got
    gram_other = exchange(gram_out, "opt", 0)
    gram_in, small_got, gram_other = tie(gram_in, small_got, gram_other)

    gram_kept, gram_sent = send_parts((gram_kept + gram_in).reshape(4, -1, ROW_BLOCK), square)
    grad_small = grad_small + small_got
    gram_sent, grad_small, gram_out = tie(gram_sent, grad_small, gram_out)
    gram_got = swap_parts(gram_sent, square)
    small_got = exchange(grad_small, "opt", 1)
    state = newton_call((gram_out, gram_other), STATE_SHAPES, False, 0, 2)
    gram_got, small_got, state = tie(gram_got, small_got, state)

    gram_in = add_parts(gram_kept, gram_got)
    grad_small = grad_small + small_got
    gram_in, grad_small, in_got = tie(gram_in, grad_small, in_got)
    gram_got = exchange(gram_in, "dp", 1)
    small_got = exchange(grad_small, "dp", 0)
    in_rows = merge_rows(in_piece, in_got, groups[0])[0]
    gram_got, small_got, in_rows = tie(gram_got, small_got, in_rows)

    gram_in = gram_in + gram_got
    grad_small = grad_small + small_got
    gram_in, grad_small, in_rows, state = tie(gram_in, grad_small, in_rows, state)
    gram_got = exchange(gram_in, "dp", 2)
    in_got = exchange(in_rows, "dp", 0)
    small_got = exchange(grad_small, "dp", 1)
    out_shapes, in_shapes = (w_out.shape,) * 3, (mom_turned.shape,) * 3
    owned_out, mom_out_new, w_out_new = newton_call((*state, grad_out, mom_out, w_out), out_shapes, False, 2, 5)
    gram_got, small_got, w_out_new, in_got = tie(gram_got, small_got, w_out_new, in_got)

    gram_in = gram_in + gram_got
    grad_small = grad_small + small_got
    for bit in range(3, (lax.axis_size("dp") - 1).bit_length()):
        gram_in = gram_in + exchange(gram_in, "dp", bit)
    gram_in, grad_small, mixed = tie(gram_in, grad_small, mixed)
    gram_got = swap_parts(gram_in, square)
    small_got = exchange(grad_small, "dp", 2)
    block = (inflow + dot32(mixed, w_out_b)).astype(bf16)
    gram_got, small_got, block = tie(gram_got, small_got, block)

    gram_in = join_parts(gram_in, gram_got, square).reshape(3, ROW_BLOCK, ROW_BLOCK)
    grad_small = grad_small + small_got
    for bit in range(3, (lax.axis_size("dp") - 1).bit_length()):
        grad_small = grad_small + exchange(grad_small, "dp", bit)
    gram_in, grad_small, in_rows, in_got = tie(gram_in, grad_small, in_rows, in_got)
    gram_other = exchange(gram_in, "opt", 0)
    grad_in = join(in_rows, in_got, "dp", 0, 0)
    gram_other, grad_in = tie(gram_other, grad_in)
    owned_in, mom_in_new, w_in_new = newton_call(
        (gram_in, gram_other, grad_in, mom_turned, w_in.T), in_shapes, True, 0, 5
    )

    owned_small = own_slice(grad_small, small.shape[0], 0)
    adam_m_new = BETA_ONE * adam_m + (1.0 - BETA_ONE) * owned_small
    adam_v_new = BETA_TWO * adam_v + (1.0 - BETA_TWO) * owned_small * owned_small
    small_new = small * (1.0 - ADAM_RATE * DECAY) - ADAM_RATE * (
        adam_m_new / (1.0 - BETA_ONE**STEP)
    ) / (jnp.sqrt(adam_v_new / (1.0 - BETA_TWO**STEP)) + ADAM_EPS)
    return (
        block,
        grad_tokens,
        owned_in.T,
        owned_out,
        owned_small,
        mom_in_new.T,
        mom_out_new,
        w_in_new.T,
        w_out_new,
        small_new,
        adam_m_new,
        adam_v_new,
    )


def solution(mesh):
    in_specs = (
        P(("dp", "opt"), None),
        P(("dp", "opt"), None),
        P(None, "opt"),
        P("opt", None),
        P("opt"),
        P(None, "opt"),
        P("opt", None),
        P("opt"),
        P("opt"),
    )
    out_specs = (
        P(("dp", "opt"), None),
        P(("dp", "opt"), None),
        P(None, "opt"),
        P("opt", None),
        P("opt"),
        P(None, "opt"),
        P("opt", None),
        P(None, "opt"),
        P("opt", None),
        P("opt"),
        P("opt"),
        P("opt"),
    )
    return jax.shard_map(
        on_device, mesh=mesh, in_specs=in_specs, out_specs=out_specs, check_vma=False
    )
```

```python
import functools
import math

import jax
import jax.numpy as jnp
from jax import lax
from jax.experimental import pallas as pl
from jax.experimental.pallas import tpu as pltpu
from jax.sharding import PartitionSpec as P

D = 768
HEADS = 24
HEAD_CHANNELS = 64
STATE = 128
CONV = 4
SEQ_LEN = 1024
STEP = 10
D_INNER = 1536
CONV_CH = 1792
PROJ = 3352


EPSILON = 1e-05
COEF_A = 3.4445
COEF_B = -4.775
COEF_C = 2.0315
MOMENTUM = 0.95
MUON_RATE = 0.5
DECAY = 0.01
ADAM_RATE = 0.2
BETA_ONE = 0.9
BETA_TWO = 0.95
ADAM_EPS = 1e-08


SPAN = 128
CHUNKS = SEQ_LEN // SPAN
PAIRS = HEADS // 2
WIDTH = 2 * HEAD_CHANNELS
CONV_END = D_INNER + CONV_CH
PADDED = CONV_END + 128
TAIL = 8
VMEM_LIMIT = 56 * 1024 * 1024


def dot32(left, right):
    return jnp.dot(left, right, preferred_element_type=jnp.float32)


def dot_nt(left, right):
    return lax.dot_general(left, right, (((1,), (1,)), ((), ())), preferred_element_type=jnp.float32)


def dot_tn(left, right):
    return lax.dot_general(left, right, (((0,), (0,)), ((), ())), preferred_element_type=jnp.float32)


def halves(value):
    high = value.astype(jnp.bfloat16)
    return high, (value - high.astype(jnp.float32)).astype(jnp.bfloat16)


def sigmoid(value):
    return 0.5 * jnp.tanh(0.5 * value) + 0.5


def softplus(value):
    return jnp.maximum(value, 0.0) + jnp.log1p(jnp.exp(-jnp.abs(value)))


def fold_rows(value):
    return jnp.sum(value.reshape(value.shape[0] // 8, 8, value.shape[1]), axis=0)


def sum_first_row(ref):
    ref[0:1, :] = jnp.sum(ref[...], axis=0, keepdims=True)


def triangle(lower):
    rows = lax.broadcasted_iota(jnp.int32, (SPAN, SPAN), 0)
    cols = lax.broadcasted_iota(jnp.int32, (SPAN, SPAN), 1)
    return rows >= cols if lower else rows <= cols


def running_sum(mask, value):
    ones = jnp.where(mask, 1.0, 0.0).astype(jnp.bfloat16)
    high, rest = halves(value)
    low = (value - high.astype(jnp.float32) - rest.astype(jnp.float32)).astype(jnp.bfloat16)
    wide = dot32(ones, jnp.concatenate([high, rest, low], axis=1))
    return wide[:, :128] + (wide[:, 128:256] + wide[:, 256:])


def head_sums(reduce_mat, exact, rough=()):
    parts = [part for value in exact for part in halves(value)] + [value.astype(jnp.bfloat16) for value in rough]
    sums = dot32(jnp.concatenate(parts, axis=0), reduce_mat)
    results, at = [], 0
    for value in exact:
        rows = value.shape[0]
        results.append(sums[at : at + rows] + sums[at + rows : at + 2 * rows])
        at += 2 * rows
    for value in rough:
        results.append(sums[at : at + value.shape[0]])
        at += value.shape[0]
    return results


def step_factors(raw, dt_bias, rate, spread):
    step_size = softplus(raw + dt_bias)
    log_decay = running_sum(triangle(True), step_size * rate)
    last = log_decay[SPAN - 1 : SPAN, :]
    stacked = jnp.concatenate([step_size, jnp.exp(log_decay), jnp.exp(last - log_decay)], axis=0)
    high, low = halves(stacked)
    wide = dot32(jnp.concatenate([high, low], axis=1), spread)
    return step_size, log_decay, wide[:SPAN], wide[SPAN : 2 * SPAN], wide[2 * SPAN :]


def split_pair(value, first):
    return jnp.concatenate(
        [jnp.where(first, value, 0.0), jnp.where(first, 0.0, value)], axis=0
    ).astype(jnp.bfloat16)


def forward_kernel(
    proj_ref, back_ref, taps_ref, conv_bias_ref, gate_gain_ref, skip_ref, dt_bias_ref, rate_ref, spread_ref, reduce_ref,
    mixed_ref, active_ref, slope_ref, grad_scan_ref, grad_gate_ref, states_ref, inner_ref, gain_acc_ref, skip_acc_ref,
    window_ref, state_ref, skip_part_ref,
):
    f32, bf16 = jnp.float32, jnp.bfloat16

    @pl.when(pl.program_id(0) == 0)
    def start():
        window_ref[0:TAIL, :] = jnp.zeros((TAIL, CONV_CH), f32)
        state_ref[...] = jnp.zeros((STATE, D_INNER), f32)
        gain_acc_ref[...] = jnp.zeros((8, D_INNER), f32)
        skip_part_ref[...] = jnp.zeros((8, D_INNER), f32)

    window_ref[TAIL:, :] = proj_ref[:, D_INNER:CONV_END].astype(f32)
    conv_out = conv_bias_ref[...]
    for tap in range(CONV):
        start_row = TAIL - (CONV - 1) + tap
        conv_out = conv_out + taps_ref[tap : tap + 1, :] * window_ref[start_row : start_row + SPAN, :]
    window_ref[0:TAIL, :] = window_ref[SPAN:, :]
    part = sigmoid(conv_out)
    silu = conv_out * part
    active_ref[...] = silu.astype(bf16)
    slope_ref[...] = (part + silu * (1.0 - part)).astype(bf16)

    values = active_ref[:, :D_INNER].astype(f32)
    input_b = active_ref[:, D_INNER : D_INNER + STATE]
    output_c = active_ref[:, D_INNER + STATE :]
    step_size, log_decay, step_wide, decay_wide, end_wide = step_factors(
        proj_ref[:, CONV_END:].astype(f32), dt_bias_ref[...], rate_ref[...], spread_ref[...]
    )
    decay_rows = log_decay.T
    moved = step_wide * values
    state = state_ref[...]
    state_low = state.astype(bf16)
    states_ref[0] = state_low
    state_ref[...] = state * decay_wide[SPAN - 1 : SPAN, :] + dot_tn(input_b, (moved * end_wide).astype(bf16))
    scores = dot_nt(output_c, input_b)
    causal = triangle(True)
    first = lax.broadcasted_iota(jnp.int32, (SPAN, WIDTH), 1) < HEAD_CHANNELS
    pieces = []
    for pair in range(PAIRS):
        lanes = slice(pair * WIDTH, (pair + 1) * WIDTH)
        mixing = []
        for head in (2 * pair, 2 * pair + 1):
            differ = log_decay[:, head : head + 1] - decay_rows[head : head + 1, :]
            mixing.append((scores * jnp.exp(jnp.where(causal, differ, -1e30))).astype(bf16))
        pieces.append(dot32(jnp.concatenate(mixing, axis=1), split_pair(moved[:, lanes], first)))
    inner = jnp.concatenate(pieces, axis=1) + dot32(output_c, state_low) * decay_wide
    scanned = inner + skip_ref[...] * values

    gate_in = proj_ref[:, :D_INNER].astype(f32)
    part = sigmoid(gate_in)
    gate = gate_in * part
    gated = scanned * gate
    scale = lax.rsqrt(jnp.mean(gated * gated, axis=1, keepdims=True) + EPSILON)
    normal = gated * scale
    mixed_ref[...] = (normal * gate_gain_ref[...]).astype(bf16)
    back = back_ref[...].astype(f32)
    gain_acc_ref[...] += fold_rows(back * normal)
    back = back * gate_gain_ref[...]
    grad_gated = scale * (back - normal * jnp.mean(back * normal, axis=1, keepdims=True))
    grad_gate_ref[...] = (grad_gated * scanned * (part + gate * (1.0 - part))).astype(bf16)
    grad_scan_low = (grad_gated * gate).astype(bf16)
    grad_scan_ref[...] = grad_scan_low
    grad_scan = grad_scan_low.astype(f32)
    skip_part_ref[...] += fold_rows(grad_scan * values)
    (inner_ref[...],) = head_sums(reduce_ref[...], [grad_scan * inner])

    @pl.when(pl.program_id(0) == CHUNKS - 1)
    def finish():
        sum_first_row(gain_acc_ref)
        skip_acc_ref[...] = head_sums(reduce_ref[...], [jnp.concatenate([skip_part_ref[...]] * 2, axis=0)])[0][:8]
        sum_first_row(skip_acc_ref)


def backward_kernel(
    proj_ref, active_ref, slope_ref, grad_scan_ref, states_ref, inner_ref, taps_ref, skip_ref, dt_bias_ref, rate_ref,
    spread_ref, reduce_ref,
    grad_ref, taps_acc_ref, bias_acc_ref, dt_acc_ref, rate_acc_ref,
    window_ref, costate_ref,
):
    f32, bf16 = jnp.float32, jnp.bfloat16

    @pl.when(pl.program_id(0) == 0)
    def start():
        window_ref[SPAN:, :] = jnp.zeros((TAIL, CONV_CH), f32)
        costate_ref[...] = jnp.zeros((STATE, D_INNER), f32)
        taps_acc_ref[...] = jnp.zeros((CONV, 8, CONV_CH), f32)
        bias_acc_ref[...] = jnp.zeros((8, CONV_CH), f32)
        dt_acc_ref[...] = jnp.zeros((8, 128), f32)
        rate_acc_ref[...] = jnp.zeros((8, 128), f32)

    values = active_ref[:, :D_INNER].astype(f32)
    input_b = active_ref[:, D_INNER : D_INNER + STATE]
    output_c = active_ref[:, D_INNER + STATE :]
    raw = proj_ref[:, CONV_END:].astype(f32)
    rate = rate_ref[...]
    step_size, log_decay, step_wide, decay_wide, end_wide = step_factors(raw, dt_bias_ref[...], rate, spread_ref[...])
    decay_rows = log_decay.T
    moved = step_wide * values
    grad_scan_low = grad_scan_ref[...]
    grad_scan = grad_scan_low.astype(f32)
    scores = dot_nt(input_b, output_c)
    causal = triangle(False)
    first = lax.broadcasted_iota(jnp.int32, (SPAN, WIDTH), 1) < HEAD_CHANNELS
    grad_scores = jnp.zeros((SPAN, SPAN), f32)
    pieces = []
    for pair in range(PAIRS):
        lanes = slice(pair * WIDTH, (pair + 1) * WIDTH)
        moved_low = moved[:, lanes].astype(bf16)
        grad_pair = split_pair(grad_scan[:, lanes], first)
        grad_mixing = dot_nt(moved_low, grad_pair)
        mixing = []
        for place, head in enumerate((2 * pair, 2 * pair + 1)):
            differ = decay_rows[head : head + 1, :] - log_decay[:, head : head + 1]
            decay = jnp.exp(jnp.where(causal, differ, -1e30))
            mixing.append((scores * decay).astype(bf16))
            grad_scores = grad_scores + decay * grad_mixing[:, place * SPAN : (place + 1) * SPAN]
        pieces.append(dot32(jnp.concatenate(mixing, axis=1), grad_pair))
    grad_inner = jnp.concatenate(pieces, axis=1)

    costate = costate_ref[...]
    costate_low = costate.astype(bf16)
    states_low = states_ref[0]
    last_wide = decay_wide[SPAN - 1 : SPAN, :]
    kept = fold_rows(costate * states_low.astype(f32)) * last_wide
    grad_cross = dot32(input_b, costate_low) * end_wide
    grad_decayed = (grad_scan * decay_wide).astype(bf16)
    grad_scores_low = grad_scores.astype(bf16)
    grad_b = dot32(grad_scores_low, output_c) + dot_nt((moved * end_wide).astype(bf16), costate_low)
    grad_c = dot_tn(grad_scores_low, input_b) + dot_nt(grad_decayed, states_low)
    costate_ref[...] = costate * last_wide + dot_tn(output_c, grad_decayed)

    moved_round = moved.astype(bf16).astype(f32)
    grad_moved = grad_inner + grad_cross
    kept = jnp.concatenate([kept, jnp.zeros_like(kept)], axis=0)
    own, keeping, crossing, grad_step = head_sums(
        reduce_ref[...], [moved_round * grad_inner, kept], [moved * grad_cross, values * grad_moved]
    )
    keeping = jnp.sum(keeping, axis=0, keepdims=True)
    grad_log = (
        running_sum(triangle(False), inner_ref[...] - own)
        + running_sum(triangle(True), crossing) - crossing
        + keeping
    )
    grad_raw = (grad_step + rate * grad_log) * sigmoid(raw + dt_bias_ref[...])
    rate_acc_ref[...] += fold_rows(step_size * grad_log)
    dt_acc_ref[...] += fold_rows(grad_raw)
    grad_ref[:, CONV_CH:] = grad_raw.astype(bf16)

    grad_values = step_wide * grad_moved + skip_ref[...] * grad_scan
    grad_active = jnp.concatenate([grad_values, grad_b, grad_c], axis=1)
    grad_conv = grad_active * slope_ref[...].astype(f32)
    bias_acc_ref[...] += fold_rows(grad_conv)
    window_ref[0:SPAN, :] = grad_conv
    conv_in = proj_ref[:, D_INNER:CONV_END].astype(f32)
    grad_in = jnp.zeros((SPAN, CONV_CH), f32)
    for tap in range(CONV):
        start_row = CONV - 1 - tap
        shifted = window_ref[start_row : start_row + SPAN, :]
        grad_in = grad_in + taps_ref[tap : tap + 1, :] * shifted
        taps_acc_ref[tap] += fold_rows(conv_in * shifted)
    grad_ref[:, :CONV_CH] = grad_in.astype(bf16)
    window_ref[SPAN:, :] = window_ref[0:TAIL, :]

    @pl.when(pl.program_id(0) == CHUNKS - 1)
    def finish():
        for tap in range(CONV):
            sum_first_row(taps_acc_ref.at[tap])
        sum_first_row(bias_acc_ref)
        sum_first_row(dt_acc_ref)
        sum_first_row(rate_acc_ref)


def head_matrices():
    spread = jnp.pad(jnp.repeat(jnp.eye(HEADS, dtype=jnp.bfloat16), HEAD_CHANNELS, axis=1), ((0, 128 - HEADS), (0, 0)))
    return jnp.concatenate([spread, spread], axis=0), spread.T


def row_block(width, order):
    return pl.BlockSpec((SPAN, width), lambda i: (order(i), 0))


def fixed_block(*shape):
    return pl.BlockSpec(shape, lambda i: (0,) * len(shape))


def state_block(order):
    return pl.BlockSpec((1, STATE, D_INNER), lambda i: (order(i), 0, 0))


def pad_heads(vector):
    return jnp.pad(vector, (0, 128 - HEADS))[None, :]


def mixer_forward(projected, back, taps, conv_bias, gate_gain, skip_wide, dt_bias, rate, spread, reduce_mat):
    f32, bf16 = jnp.float32, jnp.bfloat16
    order = lambda i: i
    rows = lambda width, kind: jax.ShapeDtypeStruct((SEQ_LEN, width), kind)
    return pl.pallas_call(
        forward_kernel,
        grid=(CHUNKS,),
        in_specs=[
            row_block(PADDED, order), row_block(D_INNER, order), fixed_block(CONV, CONV_CH), fixed_block(1, CONV_CH),
            fixed_block(1, D_INNER), fixed_block(1, D_INNER), fixed_block(1, 128), fixed_block(1, 128),
            fixed_block(256, D_INNER), fixed_block(D_INNER, 128),
        ],
        out_specs=[
            row_block(D_INNER, order), row_block(CONV_CH, order), row_block(CONV_CH, order), row_block(D_INNER, order),
            row_block(D_INNER, order), state_block(order), row_block(128, order), fixed_block(8, D_INNER),
            fixed_block(8, 128),
        ],
        out_shape=[
            rows(D_INNER, bf16), rows(CONV_CH, bf16), rows(CONV_CH, bf16), rows(D_INNER, bf16), rows(D_INNER, bf16),
            jax.ShapeDtypeStruct((CHUNKS, STATE, D_INNER), bf16), rows(128, f32),
            jax.ShapeDtypeStruct((8, D_INNER), f32), jax.ShapeDtypeStruct((8, 128), f32),
        ],
        scratch_shapes=[
            pltpu.VMEM((SPAN + TAIL, CONV_CH), f32), pltpu.VMEM((STATE, D_INNER), f32), pltpu.VMEM((8, D_INNER), f32),
        ],
        compiler_params=pltpu.CompilerParams(
            dimension_semantics=("arbitrary",), vmem_limit_bytes=VMEM_LIMIT
        ),
        cost_estimate=pl.CostEstimate(flops=8 * 10**9, bytes_accessed=32 * 10**6, transcendentals=10**7),
        name="mixer_forward",
    )(projected, back, taps, conv_bias, gate_gain, skip_wide, dt_bias, rate, spread, reduce_mat)


def mixer_backward(projected, active, slope, grad_scan, states, inner, taps, skip_wide, dt_bias, rate, spread, reduce_mat):
    f32, bf16 = jnp.float32, jnp.bfloat16
    order = lambda i: CHUNKS - 1 - i
    return pl.pallas_call(
        backward_kernel,
        grid=(CHUNKS,),
        in_specs=[
            row_block(PADDED, order), row_block(CONV_CH, order), row_block(CONV_CH, order), row_block(D_INNER, order),
            state_block(order), row_block(128, order), fixed_block(CONV, CONV_CH), fixed_block(1, D_INNER),
            fixed_block(1, 128), fixed_block(1, 128), fixed_block(256, D_INNER), fixed_block(D_INNER, 128),
        ],
        out_specs=[
            row_block(CONV_CH + 128, order), fixed_block(CONV, 8, CONV_CH), fixed_block(8, CONV_CH),
            fixed_block(8, 128), fixed_block(8, 128),
        ],
        out_shape=[
            jax.ShapeDtypeStruct((SEQ_LEN, CONV_CH + 128), bf16), jax.ShapeDtypeStruct((CONV, 8, CONV_CH), f32),
            jax.ShapeDtypeStruct((8, CONV_CH), f32), jax.ShapeDtypeStruct((8, 128), f32),
            jax.ShapeDtypeStruct((8, 128), f32),
        ],
        scratch_shapes=[pltpu.VMEM((SPAN + TAIL, CONV_CH), f32), pltpu.VMEM((STATE, D_INNER), f32)],
        compiler_params=pltpu.CompilerParams(
            dimension_semantics=("arbitrary",), vmem_limit_bytes=VMEM_LIMIT
        ),
        cost_estimate=pl.CostEstimate(flops=12 * 10**9, bytes_accessed=32 * 10**6, transcendentals=10**7),
        name="mixer_backward",
    )(projected, active, slope, grad_scan, states, inner, taps, skip_wide, dt_bias, rate, spread, reduce_mat)


ROW_BLOCK = 256
UPPER = [(0, 0), (0, 1), (0, 2), (1, 1), (1, 2), (2, 2)]


def gram_kernel(place_ref, push_ref, kept_ref, sent_ref):
    for place, (row, col) in enumerate(UPPER):
        rows = slice(row * ROW_BLOCK, (row + 1) * ROW_BLOCK)
        cols = slice(col * ROW_BLOCK, (col + 1) * ROW_BLOCK)
        tile = dot_tn(push_ref[:, rows], push_ref[:, cols])

        @pl.when(place_ref[0] == place // 3)
        def keep():
            kept_ref[place % 3] = tile

        @pl.when(place_ref[0] != place // 3)
        def send():
            sent_ref[place % 3] = tile


def gram_parts(push, name):
    tiles = jax.ShapeDtypeStruct((3, ROW_BLOCK, ROW_BLOCK), jnp.float32)
    hold = pl.BlockSpec(memory_space=pltpu.VMEM)
    return pl.pallas_call(
        gram_kernel,
        in_specs=[pl.BlockSpec(memory_space=pltpu.SMEM), hold],
        out_shape=[tiles, tiles],
        compiler_params=pltpu.CompilerParams(vmem_limit_bytes=VMEM_LIMIT),
        cost_estimate=pl.CostEstimate(
            flops=2 * D * push.size, bytes_accessed=2 * push.size, transcendentals=0
        ),
        name=name,
    )(core_place(), push)


def core_place():
    return side_of("opt", 0).astype(jnp.int32)[None]


def newton_kernel(transposed, rate, begin, end, place_ref, *refs):
    if begin == 0:
        (own_ref, other_ref), refs = refs[:2], refs[2:]
    else:
        (a_in_ref, r_in_ref, norm_ref), refs = refs[:3], refs[3:]
    if end == 5:
        (grad_ref, mom_ref, weight_ref, owned_ref, mom_new_ref, new_ref), refs = refs[:6], refs[6:]
    else:
        (a_out_ref, r_out_ref, norm_out_ref), refs = refs[:3], refs[3:]
    a_ref, t_ref, r_ref, e_ref, k_ref, f_ref, h_refs = refs
    f32, bf16 = jnp.float32, jnp.bfloat16
    blocks = [slice(i, i + ROW_BLOCK) for i in range(0, D, ROW_BLOCK)]
    size = 1.0 / D
    rows = lax.broadcasted_iota(jnp.int32, (ROW_BLOCK, ROW_BLOCK), 0)
    cols = lax.broadcasted_iota(jnp.int32, (ROW_BLOCK, ROW_BLOCK), 1)
    eye = rows == cols

    def whole_sum(value):
        return jnp.sum(jnp.sum(value, axis=0, keepdims=True), axis=1, keepdims=True)

    def trace_of(ref):
        return sum(whole_sum(jnp.where(eye, ref[block, block], 0.0)) for block in blocks)

    def shifted(value, col, amount):
        tiles = [value[block, :] for block in blocks]
        tiles[col] = tiles[col] - jnp.where(eye, amount, 0.0)
        return jnp.concatenate(tiles, axis=0)

    if begin == 0:
        core = place_ref[0] == 0
        for place, (row, col) in enumerate(UPPER):
            own, other = own_ref[place % 3], other_ref[place % 3]
            tile = jnp.where(core, own, other) if place < 3 else jnp.where(core, other, own)
            a_ref[blocks[row], blocks[col]] = tile
            if row != col:
                a_ref[blocks[col], blocks[row]] = tile.T
        total = trace_of(a_ref)
        norm = 1.0 / (jnp.sqrt(total) + 1e-07)
        scale = norm * norm
        for block in blocks:
            a_ref[block, :] = a_ref[block, :] * scale
        a_trace = total * scale
        r_trace = 0.0
    else:
        norm = norm_ref[...]
        a_ref[...] = a_in_ref[...]
        r_ref[...] = r_in_ref[...]
        a_trace, r_trace = trace_of(a_ref), trace_of(r_ref)
        for col, block in enumerate(blocks):
            h_refs[begin % 2, :, block] = shifted(r_ref[:, block], col, r_trace * size).astype(bf16)
    a_square = 0.0
    for col, block in enumerate(blocks):
        value = a_ref[:, block]
        a_square += fold_rows(value * value)
        e_ref[:, block] = shifted(value, col, a_trace * size).astype(bf16)
    a_square = whole_sum(a_square)
    for sweep in range(begin, end):
        mean, r_mean = a_trace * size, r_trace * size
        p_mean = (COEF_B * a_trace + COEF_C * a_square) * size
        lead = COEF_A + p_mean
        slope = COEF_B + 2.0 * COEF_C * mean
        with_a, with_r = 0.0, 0.0
        for col, block in enumerate(blocks):
            old = a_ref[:, block]
            poly = slope * old + COEF_C * dot32(e_ref[...], e_ref[:, block])
            poly = shifted(poly, col, COEF_C * mean * mean)
            with_a += fold_rows(poly * old)
            rest = shifted(poly, col, p_mean).astype(bf16)
            k_ref[:, block] = rest
            if sweep == 0:
                r_ref[:, block] = shifted(poly, col, -COEF_A)
                h_refs[1, :, block] = rest
            else:
                with_r += fold_rows(poly * r_ref[:, block])
        if sweep == 0:
            r_trace = lead * D
        else:
            r_trace = COEF_A * r_trace + whole_sum(with_r)
        t_trace = COEF_A * a_trace + whole_sum(with_a)
        with_k = 0.0
        for col, block in enumerate(blocks):
            part = k_ref[:, block].astype(f32)
            if sweep < 4:
                value = lead * a_ref[:, block] + mean * part + dot32(k_ref[...], e_ref[:, block])
                with_k += fold_rows(value * part)
                t_ref[:, block] = value
                f_ref[:, block] = shifted(value, col, t_trace * size).astype(bf16)
            if sweep > 0:
                value = lead * r_ref[:, block] + r_mean * part + dot32(k_ref[...], h_refs[sweep % 2, :, block])
                r_ref[:, block] = value
                h_refs[(sweep + 1) % 2, :, block] = shifted(value, col, r_trace * size).astype(bf16)
        if sweep < 4:
            a_trace = lead * t_trace + whole_sum(with_k)
            a_square = 0.0
            for col, block in enumerate(blocks):
                value = (
                    lead * t_ref[:, block]
                    + (t_trace * size) * k_ref[:, block].astype(f32)
                    + dot32(f_ref[...], k_ref[:, block])
                )
                a_square += fold_rows(value * value)
                a_ref[:, block] = value
                e_ref[:, block] = shifted(value, col, a_trace * size).astype(bf16)
            a_square = whole_sum(a_square)
    if end < 5:
        a_out_ref[...] = a_ref[...]
        r_out_ref[...] = r_ref[...]
        norm_out_ref[...] = norm
        return
    r_mean = r_trace * size
    step = norm * (MUON_RATE * rate)
    owned = grad_ref[0 : weight_ref.shape[0], :].astype(f32)
    owned_ref[...] = owned
    momentum = MOMENTUM * mom_ref[...] + owned
    mom_new_ref[...] = momentum
    push = owned + MOMENTUM * momentum
    dot = dot_nt if transposed else dot32
    ortho = r_mean * push + dot(push.astype(bf16), h_refs[1])
    new_ref[...] = weight_ref[...] * (1.0 - MUON_RATE * DECAY) - step * ortho


STATE_SHAPES = ((D, D), (D, D), (1, 1))


def nesterov(grad, momentum):
    grad = grad.astype(jnp.float32)
    return (grad + MOMENTUM * (MOMENTUM * momentum + grad)).astype(jnp.bfloat16)


def newton_call(inputs, outs, transposed, begin, end):
    rate = math.sqrt(max(1.0, PROJ / D)) if transposed else math.sqrt(max(1.0, D / D_INNER))
    whole = pltpu.VMEM((D, D), jnp.float32)
    half = pltpu.VMEM((D, D), jnp.bfloat16)
    hold = pl.BlockSpec(memory_space=pltpu.VMEM)
    return pl.pallas_call(
        functools.partial(newton_kernel, transposed, rate, begin, end),
        in_specs=[pl.BlockSpec(memory_space=pltpu.SMEM)] + [hold] * len(inputs),
        out_shape=[jax.ShapeDtypeStruct(shape, jnp.float32) for shape in outs],
        scratch_shapes=[whole, whole, whole, half, half, half, pltpu.VMEM((2, D, D), jnp.bfloat16)],
        compiler_params=pltpu.CompilerParams(vmem_limit_bytes=VMEM_LIMIT),
        cost_estimate=pl.CostEstimate(
            flops=2 * 5 * (end - begin) * 2 * D**3, bytes_accessed=10**7, transcendentals=0
        ),
        name=("newton_in" if transposed else "newton_out") + str(begin),
    )(core_place(), *inputs)


def own_slice(whole, width, along):
    return lax.dynamic_slice_in_dim(whole, lax.axis_index("opt") * width, width, along)


def exchange(value, axis, bit):
    count = lax.axis_size(axis)
    return lax.ppermute(value, axis, [(i, i ^ (1 << bit)) for i in range(count)])


def side_of(axis, bit):
    return (lax.axis_index(axis) >> bit) & 1


def cut(value, axis, bit, dim):
    half = value.shape[dim] // 2
    side = side_of(axis, bit)
    take = lambda index: lax.dynamic_slice_in_dim(value, index * half, half, dim)
    return take(side), take(1 - side)


def join(own, other, axis, bit, dim):
    lower = side_of(axis, bit) == 0
    return jnp.concatenate([jnp.where(lower, own, other), jnp.where(lower, other, own)], axis=dim)


AXES = ("dp", "opt")


def partner_index(bits, offset):
    across = lax.axis_size("opt")
    flip = 0
    for place, (axis, bit) in enumerate(reversed(bits)):
        if (offset >> place) & 1:
            flip ^= (1 << bit) * (across if axis == "dp" else 1)
    return [(i, i ^ flip) for i in range(lax.axis_size("dp") * across)]


def own_index(bits):
    index = 0
    for axis, bit in bits:
        index = 2 * index + side_of(axis, bit)
    return index


def send_parts(parts, bits):
    own = own_index(bits)
    take = lambda offset: lax.dynamic_index_in_dim(parts, own ^ offset, 0, keepdims=False)
    return take(0), [take(offset) for offset in range(1, 1 << len(bits))]


def swap_parts(parts, bits):
    if not isinstance(parts, list):
        parts = [parts] * ((1 << len(bits)) - 1)
    return [lax.ppermute(part, AXES, partner_index(bits, offset)) for offset, part in enumerate(parts, 1)]


def add_parts(kept, received):
    total = kept.astype(jnp.float32)
    for part in received:
        total = total + part.astype(jnp.float32)
    return total.astype(kept.dtype)


def join_parts(piece, received, bits):
    pieces = [piece] + received
    own = own_index(bits)
    places = []
    for place in range(1 << len(bits)):
        value = pieces[0]
        for offset in range(1, 1 << len(bits)):
            value = jnp.where(own ^ offset == place, pieces[offset], value)
        places.append(value)
    return jnp.stack(places)


def dp_groups():
    bits = [("dp", bit) for bit in range(1, (lax.axis_size("dp") - 1).bit_length())]
    return [bits[i : i + 2] for i in range(0, len(bits), 2)]


def split_rows(piece, bits):
    parts = piece.reshape(piece.shape[0], 1 << len(bits), -1, piece.shape[-1]).swapaxes(0, 1)
    return send_parts(parts, bits)


def merge_rows(piece, received, bits):
    parts = join_parts(piece, received, bits).swapaxes(0, 1)
    return parts.reshape(piece.shape[0], -1, piece.shape[-1])


def tie(*values):
    return lax.optimization_barrier(values)


def fetch_shards(shard):
    across = exchange(shard, "opt", 1)
    return [shard, exchange(shard, "opt", 0), across, exchange(across, "opt", 0)]


def in_order(pieces):
    core, far = side_of("opt", 0) == 0, side_of("opt", 1) == 0
    near = [jnp.where(core, pieces[0], pieces[1]), jnp.where(core, pieces[1], pieces[0])]
    other = [jnp.where(core, pieces[2], pieces[3]), jnp.where(core, pieces[3], pieces[2])]
    low = [jnp.where(far, n, o) for n, o in zip(near, other)]
    high = [jnp.where(far, o, n) for n, o in zip(near, other)]
    return jnp.concatenate(low + high, axis=0)


COLUMN_BLOCK = 384
SHARD = PROJ // 4
SHARD_LANES = 896
SHARD_ROWS = 896


def project_kernel(
    place_ref, hidden_ref, own_ref, core_ref, across_ref, last_ref,
    proj_ref, weight_out_ref,
    shards_ref, weight_ref, sems,
):
    step = pl.program_id(0)

    @pl.when(step == 0)
    def start():
        copies = [
            pltpu.make_async_copy(ref, shards_ref.at[place_ref[0] ^ place], sems.at[place])
            for place, ref in enumerate((own_ref, core_ref, across_ref, last_ref))
        ]
        for copy in copies:
            copy.start()
        for copy in copies:
            copy.wait()
        weight_ref[:, PROJ - PROJ % 128 :] = jnp.zeros((D, PADDED - PROJ + PROJ % 128), jnp.bfloat16)
        for place in range(4):
            weight_ref[:, place * SHARD : (place + 1) * SHARD] = shards_ref[place, :, :SHARD]

    block = weight_ref[:, pl.ds(pl.multiple_of(step * COLUMN_BLOCK, 128), COLUMN_BLOCK)]
    weight_out_ref[...] = block
    proj_ref[...] = dot32(hidden_ref[...], block).astype(jnp.bfloat16)


def project(hidden, pieces):
    length = hidden.shape[0]
    bf16 = jnp.bfloat16
    hold = pl.BlockSpec(memory_space=pl.ANY)
    return pl.pallas_call(
        project_kernel,
        grid=(PADDED // COLUMN_BLOCK,),
        in_specs=[pl.BlockSpec(memory_space=pltpu.SMEM), fixed_block(length, D)] + [hold] * 4,
        out_specs=[
            pl.BlockSpec((length, COLUMN_BLOCK), lambda i: (0, i)),
            pl.BlockSpec((D, COLUMN_BLOCK), lambda i: (0, i)),
        ],
        out_shape=[jax.ShapeDtypeStruct((length, PADDED), bf16), jax.ShapeDtypeStruct((D, PADDED), bf16)],
        scratch_shapes=[
            pltpu.VMEM((4, D, SHARD_LANES), bf16), pltpu.VMEM((D, PADDED), bf16), pltpu.SemaphoreType.DMA((4,)),
        ],
        compiler_params=pltpu.CompilerParams(
            dimension_semantics=("arbitrary",), vmem_limit_bytes=VMEM_LIMIT
        ),
        cost_estimate=pl.CostEstimate(
            flops=2 * length * D * PADDED, bytes_accessed=20 * 10**6, transcendentals=0
        ),
        name="project",
    )(lax.axis_index("opt").astype(jnp.int32)[None], hidden, *pieces)


def weight_grad_kernel(kept, place_ref, hidden_ref, gate_ref, conv_ref, out_ref, whole_ref):
    for core in range(2):
        for far in range(2):
            shard = 2 * far + (core if kept else 1 - core)
            first = shard * SHARD // 128 * 128
            last = min(-(-(shard + 1) * SHARD // 128) * 128, PADDED)
            start = shard * SHARD - first

            @pl.when((place_ref[0] == core) & (pl.program_id(0) == far))
            def work():
                for ref, begin, end in ((gate_ref, 0, D_INNER), (conv_ref, D_INNER, PADDED)):
                    low, high = max(begin, first), min(end, last)
                    if low < high:
                        whole_ref[low - first : high - first, :] = dot_tn(
                            ref[:, low - begin : high - begin], hidden_ref[...]
                        )
                block = whole_ref[start : start + SHARD_ROWS, :]
                rows = lax.broadcasted_iota(jnp.int32, (SHARD_ROWS, D), 0)
                out_ref[0] = jnp.where(rows < SHARD, block, 0.0).astype(jnp.bfloat16)


def weight_grad(hidden, gate, conv, kept):
    length = hidden.shape[0]
    return pl.pallas_call(
        functools.partial(weight_grad_kernel, kept),
        grid=(2,),
        in_specs=[
            pl.BlockSpec(memory_space=pltpu.SMEM), fixed_block(length, D), fixed_block(length, D_INNER),
            fixed_block(length, PADDED - D_INNER),
        ],
        out_specs=pl.BlockSpec((1, SHARD_ROWS, D), lambda i: (i, 0, 0)),
        out_shape=jax.ShapeDtypeStruct((2, SHARD_ROWS, D), jnp.bfloat16),
        scratch_shapes=[pltpu.VMEM((SHARD_ROWS + 128, D), jnp.float32)],
        compiler_params=pltpu.CompilerParams(
            dimension_semantics=("arbitrary",), vmem_limit_bytes=VMEM_LIMIT
        ),
        cost_estimate=pl.CostEstimate(
            flops=length * D * PADDED, bytes_accessed=11 * 10**6, transcendentals=0
        ),
        name="weight_grad_own" if kept else "weight_grad_other",
    )(core_place(), hidden, gate, conv)


def on_device(tokens, cotangent, w_in, w_out, small, mom_in, mom_out, adam_m, adam_v):
    bf16, f32 = jnp.bfloat16, jnp.float32
    groups = dp_groups()

    own_in = jnp.pad(w_in.astype(bf16), ((0, 0), (0, SHARD_LANES - SHARD)))
    own_in, small_low = tie(own_in, small.astype(bf16))
    across_in = exchange(own_in, "opt", 1)
    core_in = exchange(own_in, "opt", 0)
    params = in_order(fetch_shards(small_low)).astype(f32)
    sections = [D, D + D_INNER, D + D_INNER + CONV * CONV_CH]
    sections += [sections[-1] + CONV_CH + place * HEADS for place in range(3)]
    gain_vec, gate_gain, taps, conv_bias, dt_bias, a_log, skip_gain = jnp.split(params, sections)
    rate = -jnp.exp(a_log)
    spread, reduce_mat = head_matrices()
    fixed = (jnp.repeat(skip_gain, HEAD_CHANNELS)[None, :], pad_heads(dt_bias), pad_heads(rate), spread, reduce_mat)
    own_out = w_out.astype(bf16)
    inflow = tokens.astype(f32)
    scale = lax.rsqrt(jnp.mean(inflow * inflow, axis=1, keepdims=True) + EPSILON)
    hidden = (inflow * scale * gain_vec).astype(bf16)
    prepared = (hidden, scale, gain_vec, gate_gain[None, :], taps.reshape(CONV, CONV_CH), conv_bias[None, :], fixed)
    across_in, core_in, prepared, own_out = tie(across_in, core_in, prepared, own_out)
    hidden, scale, gain_vec, gate_gain, taps, conv_bias, fixed = prepared
    last_in = exchange(across_in, "opt", 0)
    last_in, own_out = tie(last_in, own_out)
    across_out, core_out = exchange(own_out, "opt", 1), exchange(own_out, "opt", 0)
    projected, w_pad = project(hidden, [own_in, core_in, across_in, last_in])
    across_out, core_out, projected, cotangent = tie(across_out, core_out, projected, cotangent)
    w_out_b = in_order([own_out, core_out, across_out, exchange(across_out, "opt", 0)])
    grad_mixed = dot_nt(cotangent, w_out_b).astype(bf16)

    mixed, active, slope, grad_scan, grad_gate, states, inner, gain_acc, skip_acc = mixer_forward(
        projected, grad_mixed, taps, conv_bias, gate_gain, *fixed
    )

    square = [("opt", 1), ("dp", 0)]
    out_kept, out_sent = cut(dot_tn(mixed, cotangent).astype(bf16).reshape(2, 2, -1, D), "opt", 0, 1)
    out_got = exchange(out_sent, "opt", 0)
    out_kept, out_sent = send_parts((out_kept + out_got).reshape(4, -1, D), square)
    grad_scan, out_sent = tie(grad_scan, out_sent)
    out_got = swap_parts(out_sent, square)
    grad_conv, taps_acc, bias_acc, dt_acc, rate_acc = mixer_backward(
        projected, active, slope, grad_scan, states, inner, taps, *fixed
    )
    grad_conv, out_got = tie(grad_conv, out_got)
    out_kept, out_sent = split_rows(add_parts(out_kept, out_got)[None], groups[0])
    grad_conv, out_sent = tie(grad_conv, out_sent)
    out_got = swap_parts(out_sent, groups[0])
    sent = weight_grad(hidden, grad_gate, grad_conv, False)
    grad_conv, sent, out_got = tie(grad_conv, sent, out_got)

    in_got = exchange(sent, "opt", 0)
    kept = weight_grad(hidden, grad_gate, grad_conv, True)
    out_piece = add_parts(out_kept, out_got)
    for bits in groups[1:]:
        out_kept, out_sent = split_rows(out_piece, bits)
        out_piece = add_parts(out_kept, swap_parts(out_sent, bits))
    for bits in reversed(groups[1:]):
        out_piece = merge_rows(out_piece, swap_parts(out_piece, bits), bits)
    out_piece = out_piece[0]
    out_got = exchange(out_piece, "dp", 0)
    in_got, out_got, kept = tie(in_got, out_got, kept)
    pair_in = kept + in_got
    half = D // 2
    one_kept, one_sent = cut(pair_in[:, :, :half], "opt", 1, 0)
    two_kept, two_sent = cut(pair_in[:, :, half:], "dp", 0, 1)
    out_rows = jnp.concatenate([out_piece, out_got], axis=0)
    one_sent, two_sent, out_rows, grad_gate, mixed = tie(one_sent, two_sent, out_rows, grad_gate, mixed)

    one_got, two_got = exchange(one_sent, "opt", 1), exchange(two_sent, "dp", 0)
    out_got = swap_parts(out_rows, groups[0])
    grad_hidden = dot_nt(grad_gate, w_pad[:, :D_INNER]) + dot_nt(grad_conv, w_pad[:, D_INNER:])
    block = (inflow + dot32(mixed, w_out_b)).astype(bf16)
    one_got, two_got, out_got, grad_hidden, block = tie(one_got, two_got, out_got, grad_hidden, block)

    one_kept, one_sent = cut((one_kept + one_got)[0], "dp", 0, 0)
    two_kept, two_sent = cut(two_kept + two_got, "opt", 1, 0)
    one_sent, two_sent, out_rows, out_got = tie(one_sent, two_sent, out_rows, out_got)
    one_got, two_got = exchange(one_sent, "dp", 0), exchange(two_sent, "opt", 1)
    grad_out = join_parts(out_rows, out_got, groups[0]).reshape(1 << len(groups[0]), 2, -1, D)
    lower = side_of("dp", 0) == 0
    near, far = grad_out[:, 0].reshape(-1, D), grad_out[:, 1].reshape(-1, D)
    grad_out = jnp.concatenate([jnp.where(lower, near, far), jnp.where(lower, far, near)], axis=0)
    push_out = nesterov(grad_out, mom_out)
    gram_kept, gram_sent = gram_parts(push_out, "gram_out")
    gram_got = exchange(gram_sent, "opt", 0)
    one_got, two_got, gram_got = tie(one_got, two_got, gram_got)

    gram_out = gram_kept + gram_got
    in_piece = jnp.concatenate([one_kept + one_got, (two_kept + two_got)[0]], axis=1)[None]
    in_kept, in_sent = split_rows(in_piece, groups[0])
    mom_turned = mom_in.T
    in_sent, gram_out, grad_hidden, mom_turned = tie(in_sent, gram_out, grad_hidden, mom_turned)
    in_got = swap_parts(in_sent, groups[0])
    gram_got = exchange(gram_out, "opt", 1)
    normal = inflow * scale
    grad_gain = jnp.sum(normal * grad_hidden, axis=0)
    grad_normal = grad_hidden * gain_vec
    grad_tokens = cotangent.astype(f32) + scale * (
        grad_normal - normal * jnp.mean(grad_normal * normal, axis=1, keepdims=True)
    )
    grad_small = jnp.concatenate([
        grad_gain,
        gain_acc[0],
        taps_acc[:, 0].reshape(-1),
        bias_acc[0],
        dt_acc[0, :HEADS],
        rate_acc[0, :HEADS] * rate,
        skip_acc[0, :HEADS],
    ])
    every = [("dp", 0)] + [bit for bits in groups for bit in bits]
    width = SHARD_ROWS >> len(every)
    mom_padded = jnp.pad(mom_turned, ((0, SHARD_ROWS - SHARD), (0, 0)))
    mom_piece = lax.dynamic_slice_in_dim(mom_padded, own_index(every) * width, width, 0)
    in_got, grad_tokens, grad_small, mom_piece = tie(in_got, grad_tokens, grad_small, mom_piece)

    in_piece = add_parts(in_kept, in_got)
    for bits in groups[1:]:
        in_kept, in_sent = split_rows(in_piece, bits)
        in_piece = add_parts(in_kept, swap_parts(in_sent, bits))
    gram_kept, gram_sent = gram_parts(nesterov(in_piece[0], mom_piece), "gram_in")
    for bits in reversed(groups[1:]):
        in_piece = merge_rows(in_piece, swap_parts(in_piece, bits), bits)
    gram_sent, in_piece, grad_small, gram_got = tie(gram_sent, in_piece, grad_small, gram_got)
    in_rows = in_piece[0]
    in_got = exchange(in_rows, "dp", 2)
    gram_in = exchange(gram_sent, "opt", 0)
    small_got = exchange(grad_small, "opt", 0)
    gram_out = gram_out + gram_got
    gram_other = exchange(gram_out, "opt", 0)
    gram_in, small_got, gram_other, in_got = tie(gram_in, small_got, gram_other, in_got)

    gram_kept, gram_sent = send_parts((gram_kept + gram_in).reshape(4, -1, ROW_BLOCK), square)
    grad_small = grad_small + small_got
    in_rows = join(in_rows, in_got, "dp", 2, 0)
    gram_sent, grad_small, gram_out, in_rows = tie(gram_sent, grad_small, gram_out, in_rows)
    in_got = exchange(in_rows, "dp", 1)
    gram_got = swap_parts(gram_sent, square)
    small_got = exchange(grad_small, "opt", 1)
    state = newton_call((gram_out, gram_other), STATE_SHAPES, False, 0, 2)
    gram_got, small_got, state, in_got = tie(gram_got, small_got, state, in_got)

    gram_in = add_parts(gram_kept, gram_got)
    grad_small = grad_small + small_got
    gram_in, grad_small, in_got = tie(gram_in, grad_small, in_got)
    gram_got = exchange(gram_in, "dp", 1)
    small_got = exchange(grad_small, "dp", 0)
    in_rows = join(in_rows, in_got, "dp", 1, 0)
    gram_got, small_got, in_rows = tie(gram_got, small_got, in_rows)

    gram_in = gram_in + gram_got
    grad_small = grad_small + small_got
    gram_in, grad_small, in_rows, state = tie(gram_in, grad_small, in_rows, state)
    gram_got = exchange(gram_in, "dp", 2)
    in_got = exchange(in_rows, "dp", 0)
    small_got = exchange(grad_small, "dp", 1)
    out_shapes, in_shapes = (w_out.shape,) * 3, (mom_turned.shape,) * 3
    state = newton_call(state, STATE_SHAPES, False, 2, 4)
    gram_got, small_got, state, in_got = tie(gram_got, small_got, state, in_got)

    gram_in = gram_in + gram_got
    grad_small = grad_small + small_got
    for bit in range(3, (lax.axis_size("dp") - 1).bit_length()):
        gram_in = gram_in + exchange(gram_in, "dp", bit)
    gram_in, grad_small, state = tie(gram_in, grad_small, state)
    gram_got = swap_parts(gram_in, square)
    small_got = exchange(grad_small, "dp", 2)
    owned_out, mom_out_new, w_out_new = newton_call((*state, grad_out, mom_out, w_out), out_shapes, False, 4, 5)
    gram_got, small_got, w_out_new = tie(gram_got, small_got, w_out_new)

    gram_in = join_parts(gram_in, gram_got, square).reshape(3, ROW_BLOCK, ROW_BLOCK)
    grad_small = grad_small + small_got
    for bit in range(3, (lax.axis_size("dp") - 1).bit_length()):
        grad_small = grad_small + exchange(grad_small, "dp", bit)
    gram_in, grad_small, in_rows, in_got = tie(gram_in, grad_small, in_rows, in_got)
    gram_other = exchange(gram_in, "opt", 0)
    grad_in = join(in_rows, in_got, "dp", 0, 0)
    gram_other, grad_in = tie(gram_other, grad_in)
    owned_in, mom_in_new, w_in_new = newton_call(
        (gram_in, gram_other, grad_in, mom_turned, w_in.T), in_shapes, True, 0, 5
    )

    owned_small = own_slice(grad_small, small.shape[0], 0)
    adam_m_new = BETA_ONE * adam_m + (1.0 - BETA_ONE) * owned_small
    adam_v_new = BETA_TWO * adam_v + (1.0 - BETA_TWO) * owned_small * owned_small
    small_new = small * (1.0 - ADAM_RATE * DECAY) - ADAM_RATE * (
        adam_m_new / (1.0 - BETA_ONE**STEP)
    ) / (jnp.sqrt(adam_v_new / (1.0 - BETA_TWO**STEP)) + ADAM_EPS)
    return (
        block,
        grad_tokens,
        owned_in.T,
        owned_out,
        owned_small,
        mom_in_new.T,
        mom_out_new,
        w_in_new.T,
        w_out_new,
        small_new,
        adam_m_new,
        adam_v_new,
    )


def solution(mesh):
    in_specs = (
        P(("dp", "opt"), None),
        P(("dp", "opt"), None),
        P(None, "opt"),
        P("opt", None),
        P("opt"),
        P(None, "opt"),
        P("opt", None),
        P("opt"),
        P("opt"),
    )
    out_specs = (
        P(("dp", "opt"), None),
        P(("dp", "opt"), None),
        P(None, "opt"),
        P("opt", None),
        P("opt"),
        P(None, "opt"),
        P("opt", None),
        P(None, "opt"),
        P("opt", None),
        P("opt"),
        P("opt"),
        P("opt"),
    )
    return jax.shard_map(
        on_device, mesh=mesh, in_specs=in_specs, out_specs=out_specs, check_vma=False
    )
```

```python
import functools
import math

import jax
import jax.numpy as jnp
from jax import lax
from jax.experimental import pallas as pl
from jax.experimental.pallas import tpu as pltpu
from jax.sharding import PartitionSpec as P

D = 768
HEADS = 24
HEAD_CHANNELS = 64
STATE = 128
CONV = 4
SEQ_LEN = 1024
STEP = 10
D_INNER = 1536
CONV_CH = 1792
PROJ = 3352


EPSILON = 1e-05
COEF_A = 3.4445
COEF_B = -4.775
COEF_C = 2.0315
MOMENTUM = 0.95
MUON_RATE = 0.5
DECAY = 0.01
ADAM_RATE = 0.2
BETA_ONE = 0.9
BETA_TWO = 0.95
ADAM_EPS = 1e-08


SPAN = 128
CHUNKS = SEQ_LEN // SPAN
PAIRS = HEADS // 2
WIDTH = 2 * HEAD_CHANNELS
CONV_END = D_INNER + CONV_CH
PADDED = CONV_END + 128
TAIL = 8
VMEM_LIMIT = 56 * 1024 * 1024


def dot32(left, right):
    return jnp.dot(left, right, preferred_element_type=jnp.float32)


def dot_nt(left, right):
    return lax.dot_general(left, right, (((1,), (1,)), ((), ())), preferred_element_type=jnp.float32)


def dot_tn(left, right):
    return lax.dot_general(left, right, (((0,), (0,)), ((), ())), preferred_element_type=jnp.float32)


def halves(value):
    high = value.astype(jnp.bfloat16)
    return high, (value - high.astype(jnp.float32)).astype(jnp.bfloat16)


def sigmoid(value):
    return 0.5 * jnp.tanh(0.5 * value) + 0.5


def softplus(value):
    return jnp.maximum(value, 0.0) + jnp.log1p(jnp.exp(-jnp.abs(value)))


def fold_rows(value):
    return jnp.sum(value.reshape(value.shape[0] // 8, 8, value.shape[1]), axis=0)


def sum_first_row(ref):
    ref[0:1, :] = jnp.sum(ref[...], axis=0, keepdims=True)


def triangle(lower):
    rows = lax.broadcasted_iota(jnp.int32, (SPAN, SPAN), 0)
    cols = lax.broadcasted_iota(jnp.int32, (SPAN, SPAN), 1)
    return rows >= cols if lower else rows <= cols


def running_sum(mask, value):
    ones = jnp.where(mask, 1.0, 0.0).astype(jnp.bfloat16)
    high, rest = halves(value)
    low = (value - high.astype(jnp.float32) - rest.astype(jnp.float32)).astype(jnp.bfloat16)
    wide = dot32(ones, jnp.concatenate([high, rest, low], axis=1))
    return wide[:, :128] + (wide[:, 128:256] + wide[:, 256:])


def head_sums(reduce_mat, exact, rough=()):
    parts = [part for value in exact for part in halves(value)] + [value.astype(jnp.bfloat16) for value in rough]
    sums = dot32(jnp.concatenate(parts, axis=0), reduce_mat)
    results, at = [], 0
    for value in exact:
        rows = value.shape[0]
        results.append(sums[at : at + rows] + sums[at + rows : at + 2 * rows])
        at += 2 * rows
    for value in rough:
        results.append(sums[at : at + value.shape[0]])
        at += value.shape[0]
    return results


def step_factors(raw, dt_bias, rate, spread):
    step_size = softplus(raw + dt_bias)
    log_decay = running_sum(triangle(True), step_size * rate)
    last = log_decay[SPAN - 1 : SPAN, :]
    stacked = jnp.concatenate([step_size, jnp.exp(log_decay), jnp.exp(last - log_decay)], axis=0)
    high, low = halves(stacked)
    wide = dot32(jnp.concatenate([high, low], axis=1), spread)
    return step_size, log_decay, wide[:SPAN], wide[SPAN : 2 * SPAN], wide[2 * SPAN :]


def split_pair(value, first):
    return jnp.concatenate(
        [jnp.where(first, value, 0.0), jnp.where(first, 0.0, value)], axis=0
    ).astype(jnp.bfloat16)


def forward_kernel(
    proj_ref, back_ref, taps_ref, conv_bias_ref, gate_gain_ref, skip_ref, dt_bias_ref, rate_ref, spread_ref, reduce_ref,
    mixed_ref, active_ref, slope_ref, grad_scan_ref, grad_gate_ref, states_ref, inner_ref, gain_acc_ref, skip_acc_ref,
    window_ref, state_ref, skip_part_ref,
):
    f32, bf16 = jnp.float32, jnp.bfloat16

    @pl.when(pl.program_id(0) == 0)
    def start():
        window_ref[0:TAIL, :] = jnp.zeros((TAIL, CONV_CH), f32)
        state_ref[...] = jnp.zeros((STATE, D_INNER), f32)
        gain_acc_ref[...] = jnp.zeros((8, D_INNER), f32)
        skip_part_ref[...] = jnp.zeros((8, D_INNER), f32)

    window_ref[TAIL:, :] = proj_ref[:, D_INNER:CONV_END].astype(f32)
    conv_out = conv_bias_ref[...]
    for tap in range(CONV):
        start_row = TAIL - (CONV - 1) + tap
        conv_out = conv_out + taps_ref[tap : tap + 1, :] * window_ref[start_row : start_row + SPAN, :]
    window_ref[0:TAIL, :] = window_ref[SPAN:, :]
    part = sigmoid(conv_out)
    silu = conv_out * part
    active_ref[...] = silu.astype(bf16)
    slope_ref[...] = (part + silu * (1.0 - part)).astype(bf16)

    values = active_ref[:, :D_INNER].astype(f32)
    input_b = active_ref[:, D_INNER : D_INNER + STATE]
    output_c = active_ref[:, D_INNER + STATE :]
    step_size, log_decay, step_wide, decay_wide, end_wide = step_factors(
        proj_ref[:, CONV_END:].astype(f32), dt_bias_ref[...], rate_ref[...], spread_ref[...]
    )
    decay_rows = log_decay.T
    moved = step_wide * values
    state = state_ref[...]
    state_low = state.astype(bf16)
    states_ref[0] = state_low
    state_ref[...] = state * decay_wide[SPAN - 1 : SPAN, :] + dot_tn(input_b, (moved * end_wide).astype(bf16))
    scores = dot_nt(output_c, input_b)
    causal = triangle(True)
    first = lax.broadcasted_iota(jnp.int32, (SPAN, WIDTH), 1) < HEAD_CHANNELS
    pieces = []
    for pair in range(PAIRS):
        lanes = slice(pair * WIDTH, (pair + 1) * WIDTH)
        mixing = []
        for head in (2 * pair, 2 * pair + 1):
            differ = log_decay[:, head : head + 1] - decay_rows[head : head + 1, :]
            mixing.append((scores * jnp.exp(jnp.where(causal, differ, -1e30))).astype(bf16))
        pieces.append(dot32(jnp.concatenate(mixing, axis=1), split_pair(moved[:, lanes], first)))
    inner = jnp.concatenate(pieces, axis=1) + dot32(output_c, state_low) * decay_wide
    scanned = inner + skip_ref[...] * values

    gate_in = proj_ref[:, :D_INNER].astype(f32)
    part = sigmoid(gate_in)
    gate = gate_in * part
    gated = scanned * gate
    scale = lax.rsqrt(jnp.mean(gated * gated, axis=1, keepdims=True) + EPSILON)
    normal = gated * scale
    mixed_ref[...] = (normal * gate_gain_ref[...]).astype(bf16)
    back = back_ref[...].astype(f32)
    gain_acc_ref[...] += fold_rows(back * normal)
    back = back * gate_gain_ref[...]
    grad_gated = scale * (back - normal * jnp.mean(back * normal, axis=1, keepdims=True))
    grad_gate_ref[...] = (grad_gated * scanned * (part + gate * (1.0 - part))).astype(bf16)
    grad_scan_low = (grad_gated * gate).astype(bf16)
    grad_scan_ref[...] = grad_scan_low
    grad_scan = grad_scan_low.astype(f32)
    skip_part_ref[...] += fold_rows(grad_scan * values)
    (inner_ref[...],) = head_sums(reduce_ref[...], [grad_scan * inner])

    @pl.when(pl.program_id(0) == CHUNKS - 1)
    def finish():
        sum_first_row(gain_acc_ref)
        skip_acc_ref[...] = head_sums(reduce_ref[...], [jnp.concatenate([skip_part_ref[...]] * 2, axis=0)])[0][:8]
        sum_first_row(skip_acc_ref)


def backward_kernel(
    proj_ref, active_ref, slope_ref, grad_scan_ref, states_ref, inner_ref, taps_ref, skip_ref, dt_bias_ref, rate_ref,
    spread_ref, reduce_ref,
    grad_ref, taps_acc_ref, bias_acc_ref, dt_acc_ref, rate_acc_ref,
    window_ref, costate_ref,
):
    f32, bf16 = jnp.float32, jnp.bfloat16

    @pl.when(pl.program_id(0) == 0)
    def start():
        window_ref[SPAN:, :] = jnp.zeros((TAIL, CONV_CH), f32)
        costate_ref[...] = jnp.zeros((STATE, D_INNER), f32)
        taps_acc_ref[...] = jnp.zeros((CONV, 8, CONV_CH), f32)
        bias_acc_ref[...] = jnp.zeros((8, CONV_CH), f32)
        dt_acc_ref[...] = jnp.zeros((8, 128), f32)
        rate_acc_ref[...] = jnp.zeros((8, 128), f32)

    values = active_ref[:, :D_INNER].astype(f32)
    input_b = active_ref[:, D_INNER : D_INNER + STATE]
    output_c = active_ref[:, D_INNER + STATE :]
    raw = proj_ref[:, CONV_END:].astype(f32)
    rate = rate_ref[...]
    step_size, log_decay, step_wide, decay_wide, end_wide = step_factors(raw, dt_bias_ref[...], rate, spread_ref[...])
    decay_rows = log_decay.T
    moved = step_wide * values
    grad_scan_low = grad_scan_ref[...]
    grad_scan = grad_scan_low.astype(f32)
    scores = dot_nt(input_b, output_c)
    causal = triangle(False)
    first = lax.broadcasted_iota(jnp.int32, (SPAN, WIDTH), 1) < HEAD_CHANNELS
    grad_scores = jnp.zeros((SPAN, SPAN), f32)
    pieces = []
    for pair in range(PAIRS):
        lanes = slice(pair * WIDTH, (pair + 1) * WIDTH)
        moved_low = moved[:, lanes].astype(bf16)
        grad_pair = split_pair(grad_scan[:, lanes], first)
        grad_mixing = dot_nt(moved_low, grad_pair)
        mixing = []
        for place, head in enumerate((2 * pair, 2 * pair + 1)):
            differ = decay_rows[head : head + 1, :] - log_decay[:, head : head + 1]
            decay = jnp.exp(jnp.where(causal, differ, -1e30))
            mixing.append((scores * decay).astype(bf16))
            grad_scores = grad_scores + decay * grad_mixing[:, place * SPAN : (place + 1) * SPAN]
        pieces.append(dot32(jnp.concatenate(mixing, axis=1), grad_pair))
    grad_inner = jnp.concatenate(pieces, axis=1)

    costate = costate_ref[...]
    costate_low = costate.astype(bf16)
    states_low = states_ref[0]
    last_wide = decay_wide[SPAN - 1 : SPAN, :]
    kept = fold_rows(costate * states_low.astype(f32)) * last_wide
    grad_cross = dot32(input_b, costate_low) * end_wide
    grad_decayed = (grad_scan * decay_wide).astype(bf16)
    grad_scores_low = grad_scores.astype(bf16)
    grad_b = dot32(grad_scores_low, output_c) + dot_nt((moved * end_wide).astype(bf16), costate_low)
    grad_c = dot_tn(grad_scores_low, input_b) + dot_nt(grad_decayed, states_low)
    costate_ref[...] = costate * last_wide + dot_tn(output_c, grad_decayed)

    moved_round = moved.astype(bf16).astype(f32)
    grad_moved = grad_inner + grad_cross
    kept = jnp.concatenate([kept, jnp.zeros_like(kept)], axis=0)
    own, keeping, crossing, grad_step = head_sums(
        reduce_ref[...], [moved_round * grad_inner, kept], [moved * grad_cross, values * grad_moved]
    )
    keeping = jnp.sum(keeping, axis=0, keepdims=True)
    grad_log = (
        running_sum(triangle(False), inner_ref[...] - own)
        + running_sum(triangle(True), crossing) - crossing
        + keeping
    )
    grad_raw = (grad_step + rate * grad_log) * sigmoid(raw + dt_bias_ref[...])
    rate_acc_ref[...] += fold_rows(step_size * grad_log)
    dt_acc_ref[...] += fold_rows(grad_raw)
    grad_ref[:, CONV_CH:] = grad_raw.astype(bf16)

    grad_values = step_wide * grad_moved + skip_ref[...] * grad_scan
    grad_active = jnp.concatenate([grad_values, grad_b, grad_c], axis=1)
    grad_conv = grad_active * slope_ref[...].astype(f32)
    bias_acc_ref[...] += fold_rows(grad_conv)
    window_ref[0:SPAN, :] = grad_conv
    conv_in = proj_ref[:, D_INNER:CONV_END].astype(f32)
    grad_in = jnp.zeros((SPAN, CONV_CH), f32)
    for tap in range(CONV):
        start_row = CONV - 1 - tap
        shifted = window_ref[start_row : start_row + SPAN, :]
        grad_in = grad_in + taps_ref[tap : tap + 1, :] * shifted
        taps_acc_ref[tap] += fold_rows(conv_in * shifted)
    grad_ref[:, :CONV_CH] = grad_in.astype(bf16)
    window_ref[SPAN:, :] = window_ref[0:TAIL, :]

    @pl.when(pl.program_id(0) == CHUNKS - 1)
    def finish():
        for tap in range(CONV):
            sum_first_row(taps_acc_ref.at[tap])
        sum_first_row(bias_acc_ref)
        sum_first_row(dt_acc_ref)
        sum_first_row(rate_acc_ref)


def head_matrices():
    spread = jnp.pad(jnp.repeat(jnp.eye(HEADS, dtype=jnp.bfloat16), HEAD_CHANNELS, axis=1), ((0, 128 - HEADS), (0, 0)))
    return jnp.concatenate([spread, spread], axis=0), spread.T


def row_block(width, order):
    return pl.BlockSpec((SPAN, width), lambda i: (order(i), 0))


def fixed_block(*shape):
    return pl.BlockSpec(shape, lambda i: (0,) * len(shape))


def state_block(order):
    return pl.BlockSpec((1, STATE, D_INNER), lambda i: (order(i), 0, 0))


def pad_heads(vector):
    return jnp.pad(vector, (0, 128 - HEADS))[None, :]


def mixer_forward(projected, back, taps, conv_bias, gate_gain, skip_wide, dt_bias, rate, spread, reduce_mat):
    f32, bf16 = jnp.float32, jnp.bfloat16
    order = lambda i: i
    rows = lambda width, kind: jax.ShapeDtypeStruct((SEQ_LEN, width), kind)
    return pl.pallas_call(
        forward_kernel,
        grid=(CHUNKS,),
        in_specs=[
            row_block(PADDED, order), row_block(D_INNER, order), fixed_block(CONV, CONV_CH), fixed_block(1, CONV_CH),
            fixed_block(1, D_INNER), fixed_block(1, D_INNER), fixed_block(1, 128), fixed_block(1, 128),
            fixed_block(256, D_INNER), fixed_block(D_INNER, 128),
        ],
        out_specs=[
            row_block(D_INNER, order), row_block(CONV_CH, order), row_block(CONV_CH, order), row_block(D_INNER, order),
            row_block(D_INNER, order), state_block(order), row_block(128, order), fixed_block(8, D_INNER),
            fixed_block(8, 128),
        ],
        out_shape=[
            rows(D_INNER, bf16), rows(CONV_CH, bf16), rows(CONV_CH, bf16), rows(D_INNER, bf16), rows(D_INNER, bf16),
            jax.ShapeDtypeStruct((CHUNKS, STATE, D_INNER), bf16), rows(128, f32),
            jax.ShapeDtypeStruct((8, D_INNER), f32), jax.ShapeDtypeStruct((8, 128), f32),
        ],
        scratch_shapes=[
            pltpu.VMEM((SPAN + TAIL, CONV_CH), f32), pltpu.VMEM((STATE, D_INNER), f32), pltpu.VMEM((8, D_INNER), f32),
        ],
        compiler_params=pltpu.CompilerParams(
            dimension_semantics=("arbitrary",), vmem_limit_bytes=VMEM_LIMIT
        ),
        cost_estimate=pl.CostEstimate(flops=8 * 10**9, bytes_accessed=32 * 10**6, transcendentals=10**7),
        name="mixer_forward",
    )(projected, back, taps, conv_bias, gate_gain, skip_wide, dt_bias, rate, spread, reduce_mat)


def mixer_backward(projected, active, slope, grad_scan, states, inner, taps, skip_wide, dt_bias, rate, spread, reduce_mat):
    f32, bf16 = jnp.float32, jnp.bfloat16
    order = lambda i: CHUNKS - 1 - i
    return pl.pallas_call(
        backward_kernel,
        grid=(CHUNKS,),
        in_specs=[
            row_block(PADDED, order), row_block(CONV_CH, order), row_block(CONV_CH, order), row_block(D_INNER, order),
            state_block(order), row_block(128, order), fixed_block(CONV, CONV_CH), fixed_block(1, D_INNER),
            fixed_block(1, 128), fixed_block(1, 128), fixed_block(256, D_INNER), fixed_block(D_INNER, 128),
        ],
        out_specs=[
            row_block(CONV_CH + 128, order), fixed_block(CONV, 8, CONV_CH), fixed_block(8, CONV_CH),
            fixed_block(8, 128), fixed_block(8, 128),
        ],
        out_shape=[
            jax.ShapeDtypeStruct((SEQ_LEN, CONV_CH + 128), bf16), jax.ShapeDtypeStruct((CONV, 8, CONV_CH), f32),
            jax.ShapeDtypeStruct((8, CONV_CH), f32), jax.ShapeDtypeStruct((8, 128), f32),
            jax.ShapeDtypeStruct((8, 128), f32),
        ],
        scratch_shapes=[pltpu.VMEM((SPAN + TAIL, CONV_CH), f32), pltpu.VMEM((STATE, D_INNER), f32)],
        compiler_params=pltpu.CompilerParams(
            dimension_semantics=("arbitrary",), vmem_limit_bytes=VMEM_LIMIT
        ),
        cost_estimate=pl.CostEstimate(flops=12 * 10**9, bytes_accessed=32 * 10**6, transcendentals=10**7),
        name="mixer_backward",
    )(projected, active, slope, grad_scan, states, inner, taps, skip_wide, dt_bias, rate, spread, reduce_mat)


ROW_BLOCK = 256
UPPER = [(0, 0), (0, 1), (0, 2), (1, 1), (1, 2), (2, 2)]


def gram_kernel(place_ref, push_ref, kept_ref, sent_ref):
    for place, (row, col) in enumerate(UPPER):
        rows = slice(row * ROW_BLOCK, (row + 1) * ROW_BLOCK)
        cols = slice(col * ROW_BLOCK, (col + 1) * ROW_BLOCK)
        tile = dot_tn(push_ref[:, rows], push_ref[:, cols])

        @pl.when(place_ref[0] == place // 3)
        def keep():
            kept_ref[place % 3] = tile

        @pl.when(place_ref[0] != place // 3)
        def send():
            sent_ref[place % 3] = tile


def gram_parts(push, name):
    tiles = jax.ShapeDtypeStruct((3, ROW_BLOCK, ROW_BLOCK), jnp.float32)
    hold = pl.BlockSpec(memory_space=pltpu.VMEM)
    return pl.pallas_call(
        gram_kernel,
        in_specs=[pl.BlockSpec(memory_space=pltpu.SMEM), hold],
        out_shape=[tiles, tiles],
        compiler_params=pltpu.CompilerParams(vmem_limit_bytes=VMEM_LIMIT),
        cost_estimate=pl.CostEstimate(
            flops=2 * D * push.size, bytes_accessed=2 * push.size, transcendentals=0
        ),
        name=name,
    )(core_place(), push)


def core_place():
    return side_of("opt", 0).astype(jnp.int32)[None]


def newton_kernel(transposed, rate, begin, end, place_ref, *refs):
    if begin == 0:
        (own_ref, other_ref), refs = refs[:2], refs[2:]
    else:
        (a_in_ref, r_in_ref, norm_ref), refs = refs[:3], refs[3:]
    if end == 5:
        (grad_ref, mom_ref, weight_ref, owned_ref, mom_new_ref, new_ref), refs = refs[:6], refs[6:]
    else:
        (a_out_ref, r_out_ref, norm_out_ref), refs = refs[:3], refs[3:]
    a_ref, t_ref, r_ref, e_ref, k_ref, f_ref, h_refs = refs
    f32, bf16 = jnp.float32, jnp.bfloat16
    blocks = [slice(i, i + ROW_BLOCK) for i in range(0, D, ROW_BLOCK)]
    size = 1.0 / D
    rows = lax.broadcasted_iota(jnp.int32, (ROW_BLOCK, ROW_BLOCK), 0)
    cols = lax.broadcasted_iota(jnp.int32, (ROW_BLOCK, ROW_BLOCK), 1)
    eye = rows == cols

    def whole_sum(value):
        return jnp.sum(jnp.sum(value, axis=0, keepdims=True), axis=1, keepdims=True)

    def trace_of(ref):
        return sum(whole_sum(jnp.where(eye, ref[block, block], 0.0)) for block in blocks)

    def shifted(value, col, amount):
        tiles = [value[block, :] for block in blocks]
        tiles[col] = tiles[col] - jnp.where(eye, amount, 0.0)
        return jnp.concatenate(tiles, axis=0)

    if begin == 0:
        core = place_ref[0] == 0
        for place, (row, col) in enumerate(UPPER):
            own, other = own_ref[place % 3], other_ref[place % 3]
            tile = jnp.where(core, own, other) if place < 3 else jnp.where(core, other, own)
            a_ref[blocks[row], blocks[col]] = tile
            if row != col:
                a_ref[blocks[col], blocks[row]] = tile.T
        total = trace_of(a_ref)
        norm = 1.0 / (jnp.sqrt(total) + 1e-07)
        scale = norm * norm
        for block in blocks:
            a_ref[block, :] = a_ref[block, :] * scale
        a_trace = total * scale
        r_trace = 0.0
    else:
        norm = norm_ref[...]
        a_ref[...] = a_in_ref[...]
        r_ref[...] = r_in_ref[...]
        a_trace, r_trace = trace_of(a_ref), trace_of(r_ref)
        for col, block in enumerate(blocks):
            h_refs[begin % 2, :, block] = shifted(r_ref[:, block], col, r_trace * size).astype(bf16)
    a_square = 0.0
    for col, block in enumerate(blocks):
        value = a_ref[:, block]
        a_square += fold_rows(value * value)
        e_ref[:, block] = shifted(value, col, a_trace * size).astype(bf16)
    a_square = whole_sum(a_square)
    for sweep in range(begin, end):
        mean, r_mean = a_trace * size, r_trace * size
        p_mean = (COEF_B * a_trace + COEF_C * a_square) * size
        lead = COEF_A + p_mean
        slope = COEF_B + 2.0 * COEF_C * mean
        with_a, with_r = 0.0, 0.0
        for col, block in enumerate(blocks):
            old = a_ref[:, block]
            poly = slope * old + COEF_C * dot32(e_ref[...], e_ref[:, block])
            poly = shifted(poly, col, COEF_C * mean * mean)
            with_a += fold_rows(poly * old)
            rest = shifted(poly, col, p_mean).astype(bf16)
            k_ref[:, block] = rest
            if sweep == 0:
                r_ref[:, block] = shifted(poly, col, -COEF_A)
                h_refs[1, :, block] = rest
            else:
                with_r += fold_rows(poly * r_ref[:, block])
        if sweep == 0:
            r_trace = lead * D
        else:
            r_trace = COEF_A * r_trace + whole_sum(with_r)
        t_trace = COEF_A * a_trace + whole_sum(with_a)
        with_k = 0.0
        for col, block in enumerate(blocks):
            part = k_ref[:, block].astype(f32)
            if sweep < 4:
                value = lead * a_ref[:, block] + mean * part + dot32(k_ref[...], e_ref[:, block])
                with_k += fold_rows(value * part)
                t_ref[:, block] = value
                f_ref[:, block] = shifted(value, col, t_trace * size).astype(bf16)
            if sweep > 0:
                value = lead * r_ref[:, block] + r_mean * part + dot32(k_ref[...], h_refs[sweep % 2, :, block])
                r_ref[:, block] = value
                h_refs[(sweep + 1) % 2, :, block] = shifted(value, col, r_trace * size).astype(bf16)
        if sweep < 4:
            a_trace = lead * t_trace + whole_sum(with_k)
            a_square = 0.0
            for col, block in enumerate(blocks):
                value = (
                    lead * t_ref[:, block]
                    + (t_trace * size) * k_ref[:, block].astype(f32)
                    + dot32(f_ref[...], k_ref[:, block])
                )
                a_square += fold_rows(value * value)
                a_ref[:, block] = value
                e_ref[:, block] = shifted(value, col, a_trace * size).astype(bf16)
            a_square = whole_sum(a_square)
    if end < 5:
        a_out_ref[...] = a_ref[...]
        r_out_ref[...] = r_ref[...]
        norm_out_ref[...] = norm
        return
    r_mean = r_trace * size
    step = norm * (MUON_RATE * rate)
    owned = grad_ref[0 : weight_ref.shape[0], :].astype(f32)
    owned_ref[...] = owned
    momentum = MOMENTUM * mom_ref[...] + owned
    mom_new_ref[...] = momentum
    push = owned + MOMENTUM * momentum
    dot = dot_nt if transposed else dot32
    ortho = r_mean * push + dot(push.astype(bf16), h_refs[1])
    new_ref[...] = weight_ref[...] * (1.0 - MUON_RATE * DECAY) - step * ortho


STATE_SHAPES = ((D, D), (D, D), (1, 1))


def nesterov(grad, momentum):
    grad = grad.astype(jnp.float32)
    return (grad + MOMENTUM * (MOMENTUM * momentum + grad)).astype(jnp.bfloat16)


def newton_call(inputs, outs, transposed, begin, end):
    rate = math.sqrt(max(1.0, PROJ / D)) if transposed else math.sqrt(max(1.0, D / D_INNER))
    whole = pltpu.VMEM((D, D), jnp.float32)
    half = pltpu.VMEM((D, D), jnp.bfloat16)
    hold = pl.BlockSpec(memory_space=pltpu.VMEM)
    return pl.pallas_call(
        functools.partial(newton_kernel, transposed, rate, begin, end),
        in_specs=[pl.BlockSpec(memory_space=pltpu.SMEM)] + [hold] * len(inputs),
        out_shape=[jax.ShapeDtypeStruct(shape, jnp.float32) for shape in outs],
        scratch_shapes=[whole, whole, whole, half, half, half, pltpu.VMEM((2, D, D), jnp.bfloat16)],
        compiler_params=pltpu.CompilerParams(vmem_limit_bytes=VMEM_LIMIT),
        cost_estimate=pl.CostEstimate(
            flops=2 * 5 * (end - begin) * 2 * D**3, bytes_accessed=10**7, transcendentals=0
        ),
        name=("newton_in" if transposed else "newton_out") + str(begin),
    )(core_place(), *inputs)


def own_slice(whole, width, along):
    return lax.dynamic_slice_in_dim(whole, lax.axis_index("opt") * width, width, along)


def exchange(value, axis, bit):
    count = lax.axis_size(axis)
    return lax.ppermute(value, axis, [(i, i ^ (1 << bit)) for i in range(count)])


def side_of(axis, bit):
    return (lax.axis_index(axis) >> bit) & 1


def cut(value, axis, bit, dim):
    half = value.shape[dim] // 2
    side = side_of(axis, bit)
    take = lambda index: lax.dynamic_slice_in_dim(value, index * half, half, dim)
    return take(side), take(1 - side)


def join(own, other, axis, bit, dim):
    lower = side_of(axis, bit) == 0
    return jnp.concatenate([jnp.where(lower, own, other), jnp.where(lower, other, own)], axis=dim)


AXES = ("dp", "opt")


def partner_index(bits, offset):
    across = lax.axis_size("opt")
    flip = 0
    for place, (axis, bit) in enumerate(reversed(bits)):
        if (offset >> place) & 1:
            flip ^= (1 << bit) * (across if axis == "dp" else 1)
    return [(i, i ^ flip) for i in range(lax.axis_size("dp") * across)]


def own_index(bits):
    index = 0
    for axis, bit in bits:
        index = 2 * index + side_of(axis, bit)
    return index


def send_parts(parts, bits):
    own = own_index(bits)
    take = lambda offset: lax.dynamic_index_in_dim(parts, own ^ offset, 0, keepdims=False)
    return take(0), [take(offset) for offset in range(1, 1 << len(bits))]


def swap_parts(parts, bits):
    if not isinstance(parts, list):
        parts = [parts] * ((1 << len(bits)) - 1)
    return [lax.ppermute(part, AXES, partner_index(bits, offset)) for offset, part in enumerate(parts, 1)]


def add_parts(kept, received):
    total = kept.astype(jnp.float32)
    for part in received:
        total = total + part.astype(jnp.float32)
    return total.astype(kept.dtype)


def join_parts(piece, received, bits):
    pieces = [piece] + received
    own = own_index(bits)
    places = []
    for place in range(1 << len(bits)):
        value = pieces[0]
        for offset in range(1, 1 << len(bits)):
            value = jnp.where(own ^ offset == place, pieces[offset], value)
        places.append(value)
    return jnp.stack(places)


def dp_groups():
    bits = [("dp", bit) for bit in range(1, (lax.axis_size("dp") - 1).bit_length())]
    return [bits[i : i + 2] for i in range(0, len(bits), 2)]


def split_rows(piece, bits):
    parts = piece.reshape(piece.shape[0], 1 << len(bits), -1, piece.shape[-1]).swapaxes(0, 1)
    return send_parts(parts, bits)


def merge_rows(piece, received, bits):
    parts = join_parts(piece, received, bits).swapaxes(0, 1)
    return parts.reshape(piece.shape[0], -1, piece.shape[-1])


def tie(*values):
    return lax.optimization_barrier(values)


def fetch_shards(shard):
    across = exchange(shard, "opt", 1)
    return [shard, exchange(shard, "opt", 0), across, exchange(across, "opt", 0)]


def in_order(pieces):
    core, far = side_of("opt", 0) == 0, side_of("opt", 1) == 0
    near = [jnp.where(core, pieces[0], pieces[1]), jnp.where(core, pieces[1], pieces[0])]
    other = [jnp.where(core, pieces[2], pieces[3]), jnp.where(core, pieces[3], pieces[2])]
    low = [jnp.where(far, n, o) for n, o in zip(near, other)]
    high = [jnp.where(far, o, n) for n, o in zip(near, other)]
    return jnp.concatenate(low + high, axis=0)


COLUMN_BLOCK = 384
SHARD = PROJ // 4
SHARD_LANES = 896
SHARD_ROWS = 896


def project_kernel(
    place_ref, hidden_ref, own_ref, core_ref, across_ref, last_ref,
    proj_ref, weight_out_ref,
    shards_ref, weight_ref, sems,
):
    step = pl.program_id(0)

    @pl.when(step == 0)
    def start():
        copies = [
            pltpu.make_async_copy(ref, shards_ref.at[place_ref[0] ^ place], sems.at[place])
            for place, ref in enumerate((own_ref, core_ref, across_ref, last_ref))
        ]
        for copy in copies:
            copy.start()
        for copy in copies:
            copy.wait()
        weight_ref[:, PROJ - PROJ % 128 :] = jnp.zeros((D, PADDED - PROJ + PROJ % 128), jnp.bfloat16)
        for place in range(4):
            weight_ref[:, place * SHARD : (place + 1) * SHARD] = shards_ref[place, :, :SHARD]

    block = weight_ref[:, pl.ds(pl.multiple_of(step * COLUMN_BLOCK, 128), COLUMN_BLOCK)]
    weight_out_ref[...] = block
    proj_ref[...] = dot32(hidden_ref[...], block).astype(jnp.bfloat16)


def project(hidden, pieces):
    length = hidden.shape[0]
    bf16 = jnp.bfloat16
    hold = pl.BlockSpec(memory_space=pl.ANY)
    return pl.pallas_call(
        project_kernel,
        grid=(PADDED // COLUMN_BLOCK,),
        in_specs=[pl.BlockSpec(memory_space=pltpu.SMEM), fixed_block(length, D)] + [hold] * 4,
        out_specs=[
            pl.BlockSpec((length, COLUMN_BLOCK), lambda i: (0, i)),
            pl.BlockSpec((D, COLUMN_BLOCK), lambda i: (0, i)),
        ],
        out_shape=[jax.ShapeDtypeStruct((length, PADDED), bf16), jax.ShapeDtypeStruct((D, PADDED), bf16)],
        scratch_shapes=[
            pltpu.VMEM((4, D, SHARD_LANES), bf16), pltpu.VMEM((D, PADDED), bf16), pltpu.SemaphoreType.DMA((4,)),
        ],
        compiler_params=pltpu.CompilerParams(
            dimension_semantics=("arbitrary",), vmem_limit_bytes=VMEM_LIMIT
        ),
        cost_estimate=pl.CostEstimate(
            flops=2 * length * D * PADDED, bytes_accessed=20 * 10**6, transcendentals=0
        ),
        name="project",
    )(lax.axis_index("opt").astype(jnp.int32)[None], hidden, *pieces)


def weight_grad_kernel(kept, place_ref, hidden_ref, gate_ref, conv_ref, out_ref, whole_ref):
    for core in range(2):
        for far in range(2):
            shard = 2 * far + (core if kept else 1 - core)
            first = shard * SHARD // 128 * 128
            last = min(-(-(shard + 1) * SHARD // 128) * 128, PADDED)
            start = shard * SHARD - first

            @pl.when((place_ref[0] == core) & (pl.program_id(0) == far))
            def work():
                for ref, begin, end in ((gate_ref, 0, D_INNER), (conv_ref, D_INNER, PADDED)):
                    low, high = max(begin, first), min(end, last)
                    if low < high:
                        whole_ref[low - first : high - first, :] = dot_tn(
                            ref[:, low - begin : high - begin], hidden_ref[...]
                        )
                block = whole_ref[start : start + SHARD_ROWS, :]
                rows = lax.broadcasted_iota(jnp.int32, (SHARD_ROWS, D), 0)
                out_ref[0] = jnp.where(rows < SHARD, block, 0.0).astype(jnp.bfloat16)


def weight_grad(hidden, gate, conv, kept):
    length = hidden.shape[0]
    return pl.pallas_call(
        functools.partial(weight_grad_kernel, kept),
        grid=(2,),
        in_specs=[
            pl.BlockSpec(memory_space=pltpu.SMEM), fixed_block(length, D), fixed_block(length, D_INNER),
            fixed_block(length, PADDED - D_INNER),
        ],
        out_specs=pl.BlockSpec((1, SHARD_ROWS, D), lambda i: (i, 0, 0)),
        out_shape=jax.ShapeDtypeStruct((2, SHARD_ROWS, D), jnp.bfloat16),
        scratch_shapes=[pltpu.VMEM((SHARD_ROWS + 128, D), jnp.float32)],
        compiler_params=pltpu.CompilerParams(
            dimension_semantics=("arbitrary",), vmem_limit_bytes=VMEM_LIMIT
        ),
        cost_estimate=pl.CostEstimate(
            flops=length * D * PADDED, bytes_accessed=11 * 10**6, transcendentals=0
        ),
        name="weight_grad_own" if kept else "weight_grad_other",
    )(core_place(), hidden, gate, conv)


def on_device(tokens, cotangent, w_in, w_out, small, mom_in, mom_out, adam_m, adam_v):
    bf16, f32 = jnp.bfloat16, jnp.float32
    groups = dp_groups()

    own_in = jnp.pad(w_in.astype(bf16), ((0, 0), (0, SHARD_LANES - SHARD)))
    own_in, small_low = tie(own_in, small.astype(bf16))
    across_in = exchange(own_in, "opt", 1)
    core_in = exchange(own_in, "opt", 0)
    params = in_order(fetch_shards(small_low)).astype(f32)
    sections = [D, D + D_INNER, D + D_INNER + CONV * CONV_CH]
    sections += [sections[-1] + CONV_CH + place * HEADS for place in range(3)]
    gain_vec, gate_gain, taps, conv_bias, dt_bias, a_log, skip_gain = jnp.split(params, sections)
    rate = -jnp.exp(a_log)
    spread, reduce_mat = head_matrices()
    fixed = (jnp.repeat(skip_gain, HEAD_CHANNELS)[None, :], pad_heads(dt_bias), pad_heads(rate), spread, reduce_mat)
    own_out = w_out.astype(bf16)
    inflow = tokens.astype(f32)
    scale = lax.rsqrt(jnp.mean(inflow * inflow, axis=1, keepdims=True) + EPSILON)
    hidden = (inflow * scale * gain_vec).astype(bf16)
    prepared = (hidden, scale, gain_vec, gate_gain[None, :], taps.reshape(CONV, CONV_CH), conv_bias[None, :], fixed)
    across_in, core_in, prepared, own_out = tie(across_in, core_in, prepared, own_out)
    hidden, scale, gain_vec, gate_gain, taps, conv_bias, fixed = prepared
    last_in = exchange(across_in, "opt", 0)
    last_in, own_out = tie(last_in, own_out)
    across_out, core_out = exchange(own_out, "opt", 1), exchange(own_out, "opt", 0)
    projected, w_pad = project(hidden, [own_in, core_in, across_in, last_in])
    across_out, core_out, projected, cotangent = tie(across_out, core_out, projected, cotangent)
    w_out_b = in_order([own_out, core_out, across_out, exchange(across_out, "opt", 0)])
    grad_mixed = dot_nt(cotangent, w_out_b).astype(bf16)

    mixed, active, slope, grad_scan, grad_gate, states, inner, gain_acc, skip_acc = mixer_forward(
        projected, grad_mixed, taps, conv_bias, gate_gain, *fixed
    )

    square = [("opt", 1), ("dp", 0)]
    out_kept, out_sent = cut(dot_tn(mixed, cotangent).astype(bf16).reshape(2, 2, -1, D), "opt", 0, 1)
    out_got = exchange(out_sent, "opt", 0)
    out_kept, out_sent = send_parts((out_kept + out_got).reshape(4, -1, D), square)
    grad_scan, out_sent = tie(grad_scan, out_sent)
    out_got = swap_parts(out_sent, square)
    grad_conv, taps_acc, bias_acc, dt_acc, rate_acc = mixer_backward(
        projected, active, slope, grad_scan, states, inner, taps, *fixed
    )
    grad_conv, out_got = tie(grad_conv, out_got)
    out_kept, out_sent = split_rows(add_parts(out_kept, out_got)[None], groups[0])
    grad_conv, out_sent = tie(grad_conv, out_sent)
    out_got = swap_parts(out_sent, groups[0])
    sent = weight_grad(hidden, grad_gate, grad_conv, False)
    grad_conv, sent, out_got = tie(grad_conv, sent, out_got)

    in_got = exchange(sent, "opt", 0)
    kept = weight_grad(hidden, grad_gate, grad_conv, True)
    out_piece = add_parts(out_kept, out_got)
    for bits in groups[1:]:
        out_kept, out_sent = split_rows(out_piece, bits)
        out_piece = add_parts(out_kept, swap_parts(out_sent, bits))
    for bits in reversed(groups[1:]):
        out_piece = merge_rows(out_piece, swap_parts(out_piece, bits), bits)
    out_piece = out_piece[0]
    out_got = exchange(out_piece, "dp", 0)
    in_got, out_got, kept = tie(in_got, out_got, kept)
    pair_in = kept + in_got
    half = D // 2
    one_kept, one_sent = cut(pair_in[:, :, :half], "opt", 1, 0)
    two_kept, two_sent = cut(pair_in[:, :, half:], "dp", 0, 1)
    out_rows = jnp.stack([out_piece, out_got])
    one_sent, two_sent, out_rows, grad_gate, mixed = tie(one_sent, two_sent, out_rows, grad_gate, mixed)

    one_got, two_got = exchange(one_sent, "opt", 1), exchange(two_sent, "dp", 0)
    out_got = exchange(out_rows, "dp", 2)
    grad_hidden = dot_nt(grad_gate, w_pad[:, :D_INNER]) + dot_nt(grad_conv, w_pad[:, D_INNER:])
    out_got, grad_hidden = tie(out_got, grad_hidden)
    out_rows = join(out_rows, out_got, "dp", 2, 1)
    out_rows, mixed = tie(out_rows, mixed)
    out_got = exchange(out_rows, "dp", 1)
    block = (inflow + dot32(mixed, w_out_b)).astype(bf16)
    one_got, two_got, out_got, grad_hidden, block = tie(one_got, two_got, out_got, grad_hidden, block)

    one_kept, one_sent = cut((one_kept + one_got)[0], "dp", 0, 0)
    two_kept, two_sent = cut(two_kept + two_got, "opt", 1, 0)
    one_sent, two_sent, out_rows, out_got = tie(one_sent, two_sent, out_rows, out_got)
    one_got, two_got = exchange(one_sent, "dp", 0), exchange(two_sent, "opt", 1)
    near, far = join(out_rows, out_got, "dp", 1, 1)
    grad_out = join(near, far, "dp", 0, 0)
    push_out = nesterov(grad_out, mom_out)
    gram_kept, gram_sent = gram_parts(push_out, "gram_out")
    gram_got = exchange(gram_sent, "opt", 0)
    one_got, two_got, gram_got = tie(one_got, two_got, gram_got)

    gram_out = gram_kept + gram_got
    in_piece = jnp.concatenate([one_kept + one_got, (two_kept + two_got)[0]], axis=1)[None]
    in_kept, in_sent = split_rows(in_piece, groups[0])
    mom_turned = mom_in.T
    in_sent, gram_out, grad_hidden, mom_turned = tie(in_sent, gram_out, grad_hidden, mom_turned)
    in_got = swap_parts(in_sent, groups[0])
    gram_got = exchange(gram_out, "opt", 1)
    normal = inflow * scale
    grad_gain = jnp.sum(normal * grad_hidden, axis=0)
    grad_normal = grad_hidden * gain_vec
    grad_tokens = cotangent.astype(f32) + scale * (
        grad_normal - normal * jnp.mean(grad_normal * normal, axis=1, keepdims=True)
    )
    grad_small = jnp.concatenate([
        grad_gain,
        gain_acc[0],
        taps_acc[:, 0].reshape(-1),
        bias_acc[0],
        dt_acc[0, :HEADS],
        rate_acc[0, :HEADS] * rate,
        skip_acc[0, :HEADS],
    ])
    every = [("dp", 0)] + [bit for bits in groups for bit in bits]
    width = SHARD_ROWS >> len(every)
    mom_padded = jnp.pad(mom_turned, ((0, SHARD_ROWS - SHARD), (0, 0)))
    mom_piece = lax.dynamic_slice_in_dim(mom_padded, own_index(every) * width, width, 0)
    in_got, grad_tokens, grad_small, mom_piece = tie(in_got, grad_tokens, grad_small, mom_piece)

    in_piece = add_parts(in_kept, in_got)
    for bits in groups[1:]:
        in_kept, in_sent = split_rows(in_piece, bits)
        in_piece = add_parts(in_kept, swap_parts(in_sent, bits))
    push_piece = nesterov(in_piece[0], mom_piece)
    for bits in reversed(groups[1:]):
        in_piece = merge_rows(in_piece, swap_parts(in_piece, bits), bits)
    in_rows, push_piece = tie(in_piece[0], push_piece)
    in_got = exchange(in_rows, "dp", 2)
    gram_kept, gram_sent = gram_parts(push_piece, "gram_in")
    gram_sent, in_got, grad_small, gram_got = tie(gram_sent, in_got, grad_small, gram_got)
    gram_in = exchange(gram_sent, "opt", 0)
    small_got = exchange(grad_small, "opt", 0)
    gram_out = gram_out + gram_got
    gram_other = exchange(gram_out, "opt", 0)
    in_rows = join(in_rows, in_got, "dp", 2, 0)
    gram_in, small_got, gram_other, in_rows = tie(gram_in, small_got, gram_other, in_rows)

    gram_kept, gram_sent = send_parts((gram_kept + gram_in).reshape(4, -1, ROW_BLOCK), square)
    grad_small = grad_small + small_got
    gram_sent, grad_small, gram_out, in_rows = tie(gram_sent, grad_small, gram_out, in_rows)
    in_got = exchange(in_rows, "dp", 1)
    gram_got = swap_parts(gram_sent, square)
    small_got = exchange(grad_small, "opt", 1)
    state = newton_call((gram_out, gram_other), STATE_SHAPES, False, 0, 2)
    gram_got, small_got, state, in_got = tie(gram_got, small_got, state, in_got)

    gram_in = add_parts(gram_kept, gram_got)
    grad_small = grad_small + small_got
    gram_in, grad_small, in_got = tie(gram_in, grad_small, in_got)
    gram_got = exchange(gram_in, "dp", 1)
    small_got = exchange(grad_small, "dp", 0)
    in_rows = join(in_rows, in_got, "dp", 1, 0)
    gram_got, small_got, in_rows = tie(gram_got, small_got, in_rows)

    gram_in = gram_in + gram_got
    grad_small = grad_small + small_got
    gram_in, grad_small, in_rows, state = tie(gram_in, grad_small, in_rows, state)
    gram_got = exchange(gram_in, "dp", 2)
    in_got = exchange(in_rows, "dp", 0)
    small_got = exchange(grad_small, "dp", 1)
    out_shapes, in_shapes = (w_out.shape,) * 3, (mom_turned.shape,) * 3
    state = newton_call(state, STATE_SHAPES, False, 2, 4)
    gram_got, small_got, state, in_got = tie(gram_got, small_got, state, in_got)

    gram_in = gram_in + gram_got
    grad_small = grad_small + small_got
    for bit in range(3, (lax.axis_size("dp") - 1).bit_length()):
        gram_in = gram_in + exchange(gram_in, "dp", bit)
    gram_in, grad_small, state = tie(gram_in, grad_small, state)
    gram_got = swap_parts(gram_in, square)
    small_got = exchange(grad_small, "dp", 2)
    owned_out, mom_out_new, w_out_new = newton_call((*state, grad_out, mom_out, w_out), out_shapes, False, 4, 5)
    gram_got, small_got, w_out_new = tie(gram_got, small_got, w_out_new)

    gram_in = join_parts(gram_in, gram_got, square).reshape(3, ROW_BLOCK, ROW_BLOCK)
    grad_small = grad_small + small_got
    for bit in range(3, (lax.axis_size("dp") - 1).bit_length()):
        grad_small = grad_small + exchange(grad_small, "dp", bit)
    gram_in, grad_small, in_rows, in_got = tie(gram_in, grad_small, in_rows, in_got)
    gram_other = exchange(gram_in, "opt", 0)
    grad_in = join(in_rows, in_got, "dp", 0, 0)
    gram_other, grad_in = tie(gram_other, grad_in)
    owned_in, mom_in_new, w_in_new = newton_call(
        (gram_in, gram_other, grad_in, mom_turned, w_in.T), in_shapes, True, 0, 5
    )

    owned_small = own_slice(grad_small, small.shape[0], 0)
    adam_m_new = BETA_ONE * adam_m + (1.0 - BETA_ONE) * owned_small
    adam_v_new = BETA_TWO * adam_v + (1.0 - BETA_TWO) * owned_small * owned_small
    small_new = small * (1.0 - ADAM_RATE * DECAY) - ADAM_RATE * (
        adam_m_new / (1.0 - BETA_ONE**STEP)
    ) / (jnp.sqrt(adam_v_new / (1.0 - BETA_TWO**STEP)) + ADAM_EPS)
    return (
        block,
        grad_tokens,
        owned_in.T,
        owned_out,
        owned_small,
        mom_in_new.T,
        mom_out_new,
        w_in_new.T,
        w_out_new,
        small_new,
        adam_m_new,
        adam_v_new,
    )


def solution(mesh):
    in_specs = (
        P(("dp", "opt"), None),
        P(("dp", "opt"), None),
        P(None, "opt"),
        P("opt", None),
        P("opt"),
        P(None, "opt"),
        P("opt", None),
        P("opt"),
        P("opt"),
    )
    out_specs = (
        P(("dp", "opt"), None),
        P(("dp", "opt"), None),
        P(None, "opt"),
        P("opt", None),
        P("opt"),
        P(None, "opt"),
        P("opt", None),
        P(None, "opt"),
        P("opt", None),
        P("opt"),
        P("opt"),
        P("opt"),
    )
    return jax.shard_map(
        on_device, mesh=mesh, in_specs=in_specs, out_specs=out_specs, check_vma=False
    )
```
